32 devices in a mesh: groups: 2 (over y), tensor: 4 (over z), replica: 4 (over x, core).
Axes of the slice: x: 2, y: 2, z: 4, core: 2. Of those that a mesh axis runs over, the one named last changes fastest.
Arguments:
- hidden: bfloat16 [2, 1024, 8192], P(None, ('groups', 'replica'), 'tensor'), parts along dimension 1, may hold values from -6 to 6
- base_weight: bfloat16 [8192, 2048], P('tensor'), may hold values from -0.0625 to 0.0625
- delta_values: bfloat16 [16, 8192, 2048], P(('groups', 'replica'), 'tensor'), parts along dimension 0, may hold values from -4 to 4
- delta_scales: bfloat16 [16, 64, 2048], P(('groups', 'replica'), 'tensor'), parts along dimension 0, may hold values from 0.0019989014 to 0.019897461
- tenant_slot: int32 [8], replicated, may hold values from 0 to 7, each once
- seg_tenant: int32 [8, 4], P(('groups', 'replica')), parts along dimension 0, may hold values from 0 to 7, as said below
- seg_length: int32 [8, 4], P(('groups', 'replica')), parts along dimension 0, may hold values from 1 to 40, 128 in all within a row
- queries: bfloat16 [2, 1024, 8192], P(None, ('groups', 'replica', 'tensor')), parts along dimension 1, may hold values from -48 to 48
- kv_cache: bfloat16 [1024, 128, 2048], P(('groups', 'replica', 'tensor')), parts along dimension 0, may hold values from -48 to 48
- cache_length: int32 [1024], P(('groups', 'replica', 'tensor')), parts along dimension 0, may hold values from 2 to 128
Outputs:
- new_kv: bfloat16 [2, 1024, 2048], P(None, ('groups', 'replica', 'tensor')), parts along dimension 1
- attention: bfloat16 [2, 1024, 8192], P(None, ('groups', 'replica', 'tensor')), parts along dimension 1
The draws below stay inside these ranges and needn't reach their ends.
There are 2 independent parts, one for each index of `groups`. The reference program is written for one: setup_inputs(seed, part) draws one part's arguments, and reference() takes and returns one part's arrays. A program takes and returns all parts, laid end to end along the dimension named above; an argument that names none is the same for every part. Nothing has to cross between parts.
Inputs may be any that keep to these rules, and one draw needn't show every extreme that they name: `seg_tenant`: the 4 tenants of one replica are distinct. `tenant_slot`: each tenant has exactly one slot. `seg_length`: a replica's lengths sum to 128; its largest is exactly 40.
All inputs are finite; a program needn't handle non-finite values.
Results may differ from the reference program's by a relative error of at most 0.0056.
Values may be sent and summed in bfloat16 or wider, within the bound.
No kernel may reach another device: no remote copies, remote signals or barrier semaphores. Data moves between devices by JAX's collectives and lax.ppermute only.
A program may use at most 256 MiB of HBM per device.

```python
import math
import jax
import jax.numpy as jnp
import numpy as np
from jax import lax

D = 8192
HEADS = 64
KVH = 8
HD = 128
KV2 = 2048
QW = 8192
BLOCK = 128
ROWS = 128
SEGS = 4
SEG_MOST = 40
CACHE = 128
TENANTS = 8
N_TENSOR = 4
N_REPLICA = 4


def cache_base(key):
    normals = jnp.clip(jax.random.normal(jax.random.fold_in(key, 101), (N_REPLICA * ROWS, CACHE, KV2), jnp.float32), -4.0, 4.0)
    return normals


def draw_kv_cache(key, part):
    normals = cache_base(key)
    return normals.astype(jnp.bfloat16)


def draw_queries(key, part):
    key = jax.random.fold_in(key, 5)
    drawn = jnp.clip(jax.random.normal(key, (2, N_REPLICA * ROWS, QW), jnp.float32), -4.0, 4.0)
    return drawn.astype(jnp.bfloat16)


def draw_seg_tenant(key, part):
    key = jax.random.fold_in(key, 3)
    replica_keys = jax.random.split(key, N_REPLICA)

    def pick_tenants(one_key):
        return jax.random.permutation(one_key, TENANTS)[:SEGS]
    return jax.vmap(pick_tenants)(replica_keys).astype(jnp.int32)


def set_ends(entries, stream_key, least, largest):
    longest = entries.shape.index(max(entries.shape))
    spots = []
    for shift in (0, 1):
        where = [jax.random.randint(jax.random.fold_in(stream_key, axis), (), 0, length) for axis, length in enumerate(entries.shape)]
        where[longest] = (where[longest] + shift) % entries.shape[longest]
        spots.append(tuple(where))
    return entries.at[spots[0]].set(least).at[spots[1]].set(largest)


def shard_levels(stream_key, dims, cuts, low, top_value):
    gain, own = 1.0, jax.random.fold_in(stream_key, 6)
    for axis_at, blocks in cuts:
        draws = jnp.exp(jax.random.uniform(jax.random.fold_in(own, axis_at), (blocks,), jnp.float32, low / len(cuts), top_value / len(cuts)))
        gain = gain * jnp.repeat(draws, dims[axis_at] // blocks).reshape([-1 if axis == axis_at else 1 for axis in range(len(dims))])
    return gain


def length_profile(count, total, reach, skew):
    portions = [(1 << 20) // math.isqrt(standing ** skew) + 1 for standing in range(2, count + 1)]
    surplus, given = total - reach - (count - 1), [1] * (count - 1)
    while surplus > 0:
        movable = [i for i in range(count - 1) if given[i] < reach]
        mass, remaining = sum([portions[i] for i in movable]), surplus
        for i in movable:
            extra = min(reach - given[i], max(1, remaining * portions[i] // mass), surplus)
            given[i] = given[i] + extra
            surplus = surplus - extra
    return np.array([reach] + given)


def ragged(stream_key, amount, total, limit, slope):
    if amount == 2:
        one = jax.random.randint(stream_key, (), max(1, total - limit), min(limit, total - 1) + 1)
        return jnp.stack([one, total - one])
    tallies = jnp.asarray(length_profile(amount, total, limit, slope), jnp.int32)
    couples = (amount - 1) // 2
    giver, sink = tallies[1:1 + 2 * couples:2], tallies[2:2 + 2 * couples:2]
    room = jnp.minimum(giver - 1, limit - sink)
    moved = jax.random.randint(jax.random.fold_in(stream_key, 1), (couples,), 0, 1 << 20) % (room + 1)
    tallies = tallies.at[1:1 + 2 * couples:2].set(giver - moved).at[2:2 + 2 * couples:2].set(sink + moved)
    return tallies[jax.random.permutation(jax.random.fold_in(stream_key, 2), amount)]


def gaussian(rng, extent, scale, most, pieces=(), held_as=jnp.bfloat16):
    level = shard_levels(rng, extent, pieces, -0.22, 0.18) if pieces else 1.0
    entries = jax.random.normal(rng, extent, jnp.float32) * scale * level
    return jnp.minimum(jnp.maximum(entries, -most), most).astype(held_as)


def setup_inputs(seed: int = 0, part: int = 0) -> dict:
    streams_of = jax.random.split(jax.random.key(seed), 11)
    part_splits = jax.random.split(jax.random.fold_in(streams_of[10], part), 11)
    hidden = gaussian(part_splits[0], (2, N_REPLICA * ROWS, D), 1.0, 6.0, ((1, 4), (2, 4)))
    base_weight = gaussian(streams_of[1], (D, KV2), D ** -0.5, 0.0625, ((0, 4),))
    delta_values = gaussian(part_splits[2], (TENANTS, D, KV2), 1.0, 4.0, ((0, 4), (1, 4)))
    delta_scales = jnp.clip(jnp.exp(math.log(0.019897461) - 2.2979944 * jax.random.uniform(part_splits[3], (TENANTS, D // BLOCK, KV2), jnp.float32) ** shard_levels(part_splits[3], (TENANTS, D // BLOCK, KV2), ((0, 4), (1, 4)), -0.2, 0.2)), 0.0019989014, 0.019897461).astype(jnp.bfloat16)
    tenant_slot = jax.random.permutation(streams_of[4], TENANTS).astype(jnp.int32)
    seg_tenant = draw_seg_tenant(jax.random.fold_in(jax.random.fold_in(streams_of[10], part), 71), part)
    seg_length = jax.vmap(lambda own: ragged(own, SEGS, ROWS, SEG_MOST, 0))(jax.random.split(part_splits[6], N_REPLICA)).reshape((N_REPLICA, SEGS)).astype(jnp.int32)
    queries = draw_queries(jax.random.fold_in(jax.random.fold_in(streams_of[10], part), 71), part)
    kv_cache = draw_kv_cache(jax.random.fold_in(jax.random.fold_in(streams_of[10], part), 71), part)
    cache_length = set_ends(jax.random.randint(part_splits[9], (N_REPLICA * ROWS,), 2, CACHE + 1), jax.random.fold_in(part_splits[9], 1), 2, CACHE).astype(jnp.int32)
    return {"hidden": hidden, "base_weight": base_weight, "delta_values": delta_values, "delta_scales": delta_scales, "tenant_slot": tenant_slot, "seg_tenant": seg_tenant, "seg_length": seg_length, "queries": queries, "kv_cache": kv_cache, "cache_length": cache_length}


def dequantize(values, scales):
    widened = values.astype(jnp.float32).reshape(D // BLOCK, BLOCK, KV2) * scales.astype(jnp.float32)[:, None, :]
    return widened.reshape(D, KV2).astype(jnp.bfloat16)

def attend(queries, new_kv, kv_cache, cache_length):
    row_total = queries.shape[1]
    group_size = HEADS // KVH
    key_width = KVH * HD
    query_heads = queries.astype(jnp.float32).reshape(2, row_total, KVH, group_size, HD)
    cache_keys = kv_cache[:, :, :key_width].astype(jnp.float32).reshape(row_total, CACHE, KVH, HD)
    cache_vals = kv_cache[:, :, key_width:].astype(jnp.float32).reshape(row_total, CACHE, KVH, HD)
    new_keys = new_kv[:, :, :key_width].astype(jnp.float32).reshape(2, row_total, KVH, HD)
    new_vals = new_kv[:, :, key_width:].astype(jnp.float32).reshape(2, row_total, KVH, HD)
    inv_scale = 1.0 / math.sqrt(HD)
    score_cache = jnp.einsum('srkgd,rpkd->srkgp', query_heads, cache_keys) * inv_scale
    score_new = jnp.einsum('srkgd,trkd->srkgt', query_heads, new_keys) * inv_scale
    positions = jnp.arange(CACHE, dtype=jnp.int32)
    live_cache = positions[None, :] < cache_length[:, None]
    steps_idx = jnp.arange(2, dtype=jnp.int32)
    live_new = steps_idx[None, :] <= steps_idx[:, None]
    score_cache = jnp.where(live_cache[None, :, None, None, :], score_cache, -1e+30)
    score_new = jnp.where(live_new[:, None, None, None, :], score_new, -1e+30)
    scores = jnp.concatenate([score_cache, score_new], axis=-1)
    row_max = lax.optimization_barrier(jnp.max(scores, axis=-1, keepdims=True))
    expo = jnp.exp(scores - row_max)
    probs = (expo / lax.optimization_barrier(jnp.sum(expo, axis=-1, keepdims=True))).astype(jnp.bfloat16).astype(jnp.float32)
    out_cache = jnp.einsum('srkgp,rpkd->srkgd', probs[..., :CACHE], cache_vals)
    out_new = jnp.einsum('srkgt,trkd->srkgd', probs[..., CACHE:], new_vals)
    return (out_cache + out_new).astype(jnp.bfloat16).reshape(2, row_total, QW)

def reference(hidden, base_weight, delta_values, delta_scales, tenant_slot, seg_tenant, seg_length, queries, kv_cache, cache_length):
    per_replica = jnp.moveaxis(hidden.reshape(2, N_REPLICA, ROWS, D), 1, 0)

    def one_replica(operands):
        rep_x, tenants, lengths = operands
        lengths = lengths.astype(jnp.int32)
        seg_ends = jnp.cumsum(lengths).astype(jnp.int32)
        starts = (seg_ends - lengths).astype(jnp.int32)
        padded = jnp.pad(rep_x, ((0, 0), (0, SEG_MOST), (0, 0)))

        def one_segment(seg_operands):
            tenant, begin_row, row_count = seg_operands
            slot_index = tenant_slot[tenant]
            weight = dequantize(delta_values[slot_index], delta_scales[slot_index])
            row_block = lax.dynamic_slice_in_dim(padded, begin_row.astype(jnp.int32), SEG_MOST, 1)
            keep_mask = jnp.arange(SEG_MOST, dtype=jnp.int32) < row_count
            row_block = jnp.where(keep_mask[None, :, None], row_block, jnp.zeros_like(row_block))
            split_x = row_block.reshape(2, SEG_MOST, N_TENSOR, D // N_TENSOR).astype(jnp.float32)
            split_w = weight.reshape(N_TENSOR, D // N_TENSOR, KV2).astype(jnp.float32)
            block_parts = jnp.einsum('srnd,ndk->srnk', split_x, split_w).astype(jnp.bfloat16)
            block_parts = lax.optimization_barrier(block_parts)
            return lax.optimization_barrier(jnp.sum(block_parts.astype(jnp.float32), axis=2))
        seg_terms = lax.map(one_segment, (tenants, starts, lengths))
        row_ids = jnp.arange(ROWS, dtype=jnp.int32)
        seg_of_row = lax.optimization_barrier(jnp.sum((row_ids[:, None] >= seg_ends[None, :]).astype(jnp.int32), axis=1))
        offset = row_ids - starts[seg_of_row]
        delta_rows = jnp.moveaxis(seg_terms[seg_of_row, :, offset], 1, 0)
        base_rows = jnp.dot(rep_x.reshape(2 * ROWS, D), base_weight, preferred_element_type=jnp.float32).reshape(2, ROWS, KV2)
        return (base_rows + delta_rows).astype(jnp.bfloat16)
    new_rep = lax.map(one_replica, (per_replica, seg_tenant, seg_length))
    new_kv = jnp.moveaxis(new_rep, 0, 1).reshape(2, N_REPLICA * ROWS, KV2)
    attention = attend(queries, new_kv, kv_cache, cache_length)
    return (new_kv, attention)
```

```python
import functools
import math

import jax
import jax.numpy as jnp
from jax import lax
from jax.experimental import pallas as pl
from jax.experimental.pallas import tpu as pltpu
from jax.sharding import PartitionSpec as P

HEADS = 64
KVH = 8
HD = 128
GROUP = HEADS // KVH
KEYS = KVH * HD
BLOCK = 128
SEG_MOST = 40
SLOTS = 2
NEG = -1e30
VMEM_LIMIT = 40 * 1024 * 1024


def row_positions(meta_ref, slot_ref, first, steps, rows, shape, axis):
    index = lax.broadcasted_iota(jnp.int32, shape, axis)
    source = index // (steps * rows)
    step = (index // rows) % steps
    row = index % rows
    per_slot = 2 * steps * SEG_MOST
    place = jnp.full(shape, -1, jnp.int32)
    for src in range(2):
        begin = jnp.int32(0)
        for seg in range(meta_ref.shape[1] // 2):
            slot = slot_ref[meta_ref[src, seg]] - first
            length = meta_ref[src, meta_ref.shape[1] // 2 + seg]
            end = begin + length
            held = jnp.logical_and(slot >= 0, slot < SLOTS)
            offset = jnp.where(held, slot * per_slot + src * steps * SEG_MOST - begin, -(1 << 20))
            inside = (source == src) & (row >= begin) & (row < end)
            place = jnp.where(inside, offset + step * SEG_MOST + row, place)
            begin = end
    return place


def delta_body(with_base, steps, rows, *refs):
    if with_base:
        (first_ref, meta_ref, slot_ref, xa_ref, xb_ref, val_ref, sc_ref, base_ref, da_ref, db_ref,
         xc_ref, scatter_ref) = refs
    else:
        (first_ref, meta_ref, slot_ref, xa_ref, xb_ref, val_ref, sc_ref, da_ref, db_ref,
         xc_ref, scatter_ref) = refs
    width = val_ref.shape[1]
    tile = val_ref.shape[2]
    half = steps * rows
    taken = SLOTS * 2 * steps * SEG_MOST
    per_slot = taken // SLOTS

    @pl.when(pl.program_id(0) == 0)
    def _():
        first = first_ref[0]
        along = row_positions(meta_ref, slot_ref, first, steps, rows, (1, 2 * half), 1)
        picks = (lax.broadcasted_iota(jnp.int32, (taken, 2 * half), 0) == along).astype(jnp.bfloat16)
        down = row_positions(meta_ref, slot_ref, first, steps, rows, (2 * half, 1), 0)
        scatter_ref[...] = (
            lax.broadcasted_iota(jnp.int32, (2 * half, taken), 1) == down
        ).astype(jnp.bfloat16)
        xa = xa_ref[...].reshape(half, width)
        xb = xb_ref[...].reshape(half, width)
        got = jnp.dot(picks[:, :half], xa, preferred_element_type=jnp.float32)
        got += jnp.dot(picks[:, half:], xb, preferred_element_type=jnp.float32)
        xc_ref[...] = got.astype(jnp.bfloat16)

    parts = []
    for slot in range(SLOTS):
        scaled = [
            val_ref[slot, b * BLOCK:(b + 1) * BLOCK, :] * sc_ref[slot, b:b + 1, :]
            for b in range(width // BLOCK)
        ]
        weight = jnp.concatenate(scaled, axis=0)
        parts.append(
            jnp.dot(
                xc_ref[slot * per_slot:(slot + 1) * per_slot, :], weight,
                preferred_element_type=jnp.float32,
            ).astype(jnp.bfloat16)
        )
    spread = jnp.dot(
        scatter_ref[...], jnp.concatenate(parts, axis=0), preferred_element_type=jnp.float32
    )
    own = spread[:half]
    if with_base:
        own = own + jnp.dot(
            xa_ref[...].reshape(half, width), base_ref[...], preferred_element_type=jnp.float32
        )
    da_ref[...] = own.reshape(steps, rows, tile).astype(da_ref.dtype)
    db_ref[...] = spread[half:].reshape(steps, rows, tile).astype(db_ref.dtype)


def delta_rows(first, meta, slots, xa, xb, values, scales, base=None):
    steps, rows, width = xa.shape
    columns = values.shape[2]
    tile = min(256, columns)
    smem = pl.BlockSpec(memory_space=pltpu.SMEM)
    whole = pl.BlockSpec((steps, rows, width), lambda i: (0, 0, 0))
    in_specs = [
        smem, smem, smem, whole, whole,
        pl.BlockSpec((SLOTS, width, tile), lambda i: (0, 0, i)),
        pl.BlockSpec((SLOTS, width // BLOCK, tile), lambda i: (0, 0, i)),
    ]
    args = [first, meta, slots, xa, xb, values, scales]
    flops = 2 * SLOTS * 2 * steps * SEG_MOST * width * columns
    size = values.size * 2
    if base is not None:
        in_specs.append(pl.BlockSpec((width, tile), lambda i: (0, i)))
        args.append(base)
        flops += 2 * steps * rows * width * columns
        size += base.size * 2
    out = pl.BlockSpec((steps, rows, tile), lambda i: (0, 0, i))
    taken = SLOTS * 2 * steps * SEG_MOST
    return pl.pallas_call(
        functools.partial(delta_body, base is not None, steps, rows),
        grid=(columns // tile,),
        in_specs=in_specs,
        out_specs=(out, out),
        out_shape=(
            jax.ShapeDtypeStruct(
                (steps, rows, columns), jnp.float32 if base is not None else jnp.bfloat16
            ),
            jax.ShapeDtypeStruct((steps, rows, columns), jnp.bfloat16),
        ),
        scratch_shapes=[
            pltpu.VMEM((taken, width), jnp.bfloat16),
            pltpu.VMEM((2 * steps * rows, taken), jnp.bfloat16),
        ],
        cost_estimate=pl.CostEstimate(flops=flops, bytes_accessed=size, transcendentals=0),
        compiler_params=pltpu.CompilerParams(vmem_limit_bytes=VMEM_LIMIT),
        name="delta_rows",
    )(*args)


def cache_body(len_ref, q_ref, kv_ref, o_ref, lse_ref):
    block = q_ref.shape[0]
    cached = kv_ref.shape[1]
    rows_of = 2 * GROUP
    scale = 1.0 / math.sqrt(HD)
    position = lax.broadcasted_iota(jnp.int32, (HEADS * 2, cached), 1)
    for r in range(block):
        length = len_ref[pl.program_id(0) * block + r]
        scores = jnp.concatenate(
            [
                lax.dot_general(
                    q_ref[r, k * rows_of:(k + 1) * rows_of, :],
                    kv_ref[r, :, k * HD:(k + 1) * HD],
                    (((1,), (1,)), ((), ())),
                    preferred_element_type=jnp.float32,
                )
                for k in range(KVH)
            ],
            axis=0,
        ) * scale
        scores = jnp.where(position < length, scores, NEG)
        top = jnp.max(scores, axis=1, keepdims=True)
        expo = jnp.exp(scores - top)
        total = jnp.sum(expo, axis=1, keepdims=True)
        expo = expo.astype(jnp.bfloat16)
        out = jnp.concatenate(
            [
                jnp.dot(
                    expo[k * rows_of:(k + 1) * rows_of, :],
                    kv_ref[r, :, KEYS + k * HD:KEYS + (k + 1) * HD],
                    preferred_element_type=jnp.float32,
                )
                for k in range(KVH)
            ],
            axis=0,
        )
        o_ref[r] = out / total
        lse_ref[r] = top + jnp.log(total)


def attend_cache(lengths, q, kv_cache):
    rows, heads2, _ = q.shape
    cached, width = kv_cache.shape[1:]
    block = min(4, rows)
    return pl.pallas_call(
        cache_body,
        grid=(rows // block,),
        in_specs=[
            pl.BlockSpec(memory_space=pltpu.SMEM),
            pl.BlockSpec((block, heads2, HD), lambda i: (i, 0, 0)),
            pl.BlockSpec((block, cached, width), lambda i: (i, 0, 0)),
        ],
        out_specs=(
            pl.BlockSpec((block, heads2, HD), lambda i: (i, 0, 0)),
            pl.BlockSpec((block, heads2, 1), lambda i: (i, 0, 0)),
        ),
        out_shape=(
            jax.ShapeDtypeStruct((rows, heads2, HD), jnp.float32),
            jax.ShapeDtypeStruct((rows, heads2, 1), jnp.float32),
        ),
        cost_estimate=pl.CostEstimate(
            flops=4 * rows * heads2 * cached * HD,
            bytes_accessed=kv_cache.size * 2,
            transcendentals=rows * heads2 * cached,
        ),
        compiler_params=pltpu.CompilerParams(vmem_limit_bytes=VMEM_LIMIT),
        name="attend_cache",
    )(lengths, q, kv_cache)


def join_body(q_ref, o_ref, lse_ref, k_ref, v_ref, out_ref):
    block = q_ref.shape[0]
    pairs = 2 * KVH
    shape = (2 * HEADS, pairs)
    row = lax.broadcasted_iota(jnp.int32, shape, 0)
    col = lax.broadcasted_iota(jnp.int32, shape, 1)
    live = (row // (2 * GROUP) == col % KVH) & (col // KVH <= (row // GROUP) % 2)
    scale = 1.0 / math.sqrt(HD)
    for r in range(block):
        scores = lax.dot_general(
            q_ref[r], k_ref[r], (((1,), (1,)), ((), ())), preferred_element_type=jnp.float32
        ) * scale
        scores = jnp.where(live, scores, NEG)
        lse = lse_ref[r]
        top = jnp.maximum(jnp.max(scores, axis=1, keepdims=True), lse)
        expo = jnp.exp(scores - top)
        before = jnp.exp(lse - top)
        total = before + jnp.sum(expo, axis=1, keepdims=True)
        out = o_ref[r] * before + jnp.dot(
            expo.astype(jnp.bfloat16), v_ref[r], preferred_element_type=jnp.float32
        )
        out_ref[r] = (out / total).astype(jnp.bfloat16)


def attend_join(q, o, lse, new_keys, new_vals):
    rows, heads2, _ = q.shape
    pairs = new_keys.shape[1]
    block = min(8, rows)

    def spec(second, last):
        return pl.BlockSpec((block, second, last), lambda i: (i, 0, 0))

    return pl.pallas_call(
        join_body,
        grid=(rows // block,),
        in_specs=[
            spec(heads2, HD), spec(heads2, HD), spec(heads2, 1), spec(pairs, HD), spec(pairs, HD),
        ],
        out_specs=spec(heads2, HD),
        out_shape=jax.ShapeDtypeStruct((rows, heads2, HD), jnp.bfloat16),
        compiler_params=pltpu.CompilerParams(vmem_limit_bytes=VMEM_LIMIT),
        name="attend_join",
    )(q, o, lse, new_keys, new_vals)


def scatter_sum(partial, tensor):
    steps, rows, columns = partial.shape
    shard = rows // tensor
    me = lax.axis_index("tensor")

    def block(at):
        return lax.dynamic_slice_in_dim(partial, at * shard, shard, 1)

    total = block(me).astype(jnp.float32)
    for shift in range(1, tensor):
        pairs = [(i, (i + shift) % tensor) for i in range(tensor)]
        sent = lax.ppermute(block((me + shift) % tensor), "tensor", pairs)
        total = total + sent.astype(jnp.float32)
    return total


def local(
    replicas,
    tensor,
    hidden,
    base_weight,
    delta_values,
    delta_scales,
    tenant_slot,
    seg_tenant,
    seg_length,
    queries,
    kv_cache,
    cache_length,
):
    def swap(value, mask):
        return lax.ppermute(value, "replica", [(i, i ^ mask) for i in range(replicas)])

    first = (lax.axis_index("replica") * SLOTS).reshape(1)
    meta = jnp.concatenate([seg_tenant, seg_length], axis=1)
    meta = jnp.concatenate([meta, swap(meta, 1)], axis=0)
    sibling = swap(hidden, 1)
    far = []
    for mask in range(2, replicas, 2):
        far.append((mask, swap(meta, mask), [swap(hidden[s:s + 1], mask) for s in range(2)]))

    own, other = delta_rows(
        first, meta, tenant_slot, hidden, sibling, delta_values, delta_scales, base_weight
    )
    own = own + swap(other, 1).astype(jnp.float32)

    steps = [own[0:1], own[1:2]]
    for mask, far_meta, chunks in far:
        for s, chunk in enumerate(chunks):
            chunk_sibling = swap(chunk, 1)
            mine, theirs = delta_rows(
                first, far_meta, tenant_slot, chunk, chunk_sibling, delta_values, delta_scales
            )
            both = mine + swap(theirs, 1)
            steps[s] = steps[s] + swap(both, mask).astype(jnp.float32)

    shard_rows = queries.shape[1]
    q = queries.reshape(2, shard_rows, KVH, GROUP, HD).transpose(1, 2, 0, 3, 4)
    q = q.reshape(shard_rows, 2 * HEADS, HD)
    cache_out, cache_lse = attend_cache(cache_length, q, kv_cache)

    if tensor <= 4:
        sums = [scatter_sum(part.astype(jnp.bfloat16), tensor) for part in steps]
    else:
        sums = [
            lax.psum_scatter(part, "tensor", scatter_dimension=1, tiled=True) for part in steps
        ]
    new_kv = jnp.concatenate([part.astype(jnp.bfloat16) for part in sums], axis=0)
    split = new_kv.reshape(2, shard_rows, 2, KVH, HD).transpose(2, 1, 0, 3, 4)
    split = split.reshape(2, shard_rows, 2 * KVH, HD)
    joined = attend_join(q, cache_out, cache_lse, split[0], split[1])
    attention = joined.reshape(shard_rows, KVH, 2, GROUP, HD).transpose(2, 0, 1, 3, 4)
    return (new_kv, attention.reshape(2, shard_rows, HEADS * HD))


def solution(mesh):
    placed = (
        P(None, ("groups", "replica"), "tensor"),
        P("tensor", None),
        P(("groups", "replica"), "tensor", None),
        P(("groups", "replica"), "tensor", None),
        P(),
        P(("groups", "replica"), None),
        P(("groups", "replica"), None),
        P(None, ("groups", "replica", "tensor"), None),
        P(("groups", "replica", "tensor"), None, None),
        P(("groups", "replica", "tensor")),
    )
    return jax.shard_map(
        functools.partial(local, mesh.shape["replica"], mesh.shape["tensor"]),
        mesh=mesh,
        in_specs=placed,
        out_specs=(
            P(None, ("groups", "replica", "tensor"), None),
            P(None, ("groups", "replica", "tensor"), None),
        ),
        check_vma=False,
    )
```

```python
import functools
import math

import jax
import jax.numpy as jnp
from jax import lax
from jax.experimental import pallas as pl
from jax.experimental.pallas import tpu as pltpu
from jax.sharding import PartitionSpec as P

HEADS = 64
KVH = 8
HD = 128
GROUP = HEADS // KVH
KEYS = KVH * HD
BLOCK = 128
SEG_MOST = 40
SLOTS = 2
NEG = -1e30
VMEM_LIMIT = 52 * 1024 * 1024
LIGHT = pl.CostEstimate(flops=1, bytes_accessed=1, transcendentals=0)
COVER = pl.CostEstimate(flops=1 << 34, bytes_accessed=1 << 26, transcendentals=0)


def row_positions(meta_ref, slot_ref, first, steps, rows, shape, axis):
    index = lax.broadcasted_iota(jnp.int32, shape, axis)
    source = index // (steps * rows)
    step = (index // rows) % steps
    row = index % rows
    per_slot = 2 * steps * SEG_MOST
    place = jnp.full(shape, -1, jnp.int32)
    for src in range(2):
        begin = jnp.int32(0)
        for seg in range(meta_ref.shape[1] // 2):
            slot = slot_ref[meta_ref[src, seg]] - first
            length = meta_ref[src, meta_ref.shape[1] // 2 + seg]
            end = begin + length
            held = jnp.logical_and(slot >= 0, slot < SLOTS)
            offset = jnp.where(held, slot * per_slot + src * steps * SEG_MOST - begin, -(1 << 20))
            inside = (source == src) & (row >= begin) & (row < end)
            place = jnp.where(inside, offset + step * SEG_MOST + row, place)
            begin = end
    return place


def delta_body(with_base, chunks, steps, rows, *refs):
    first_ref, meta_ref, slot_ref = refs[:3]
    xa_refs, xb_refs = refs[3:3 + chunks], refs[3 + chunks:3 + 2 * chunks]
    val_ref, sc_ref = refs[3 + 2 * chunks:5 + 2 * chunks]
    da_ref, db_ref, xc_ref, scatter_ref = refs[-4:]
    width = val_ref.shape[1]
    tile = val_ref.shape[2]
    half = steps * rows
    taken = SLOTS * 2 * steps * SEG_MOST
    per_slot = taken // SLOTS

    @pl.when(pl.program_id(0) == 0)
    def _():
        first = first_ref[0]
        along = row_positions(meta_ref, slot_ref, first, steps, rows, (1, 2 * half), 1)
        picks = (lax.broadcasted_iota(jnp.int32, (taken, 2 * half), 0) == along).astype(jnp.bfloat16)
        down = row_positions(meta_ref, slot_ref, first, steps, rows, (2 * half, 1), 0)
        scatter_ref[...] = (
            lax.broadcasted_iota(jnp.int32, (2 * half, taken), 1) == down
        ).astype(jnp.bfloat16)
        begin = 0
        got = jnp.zeros(xc_ref.shape, jnp.float32)
        for xa_ref, xb_ref in zip(xa_refs, xb_refs):
            end = begin + xa_ref.shape[0]
            got += jnp.dot(picks[:, begin:end], xa_ref[...], preferred_element_type=jnp.float32)
            got += jnp.dot(
                picks[:, half + begin:half + end], xb_ref[...], preferred_element_type=jnp.float32
            )
            begin = end
        xc_ref[...] = got.astype(jnp.bfloat16)

    parts = []
    for slot in range(SLOTS):
        scaled = [
            val_ref[slot, b * BLOCK:(b + 1) * BLOCK, :] * sc_ref[slot, b:b + 1, :]
            for b in range(width // BLOCK)
        ]
        weight = jnp.concatenate(scaled, axis=0)
        parts.append(
            jnp.dot(
                xc_ref[slot * per_slot:(slot + 1) * per_slot, :], weight,
                preferred_element_type=jnp.float32,
            ).astype(jnp.bfloat16)
        )
    spread = jnp.dot(
        scatter_ref[...], jnp.concatenate(parts, axis=0), preferred_element_type=jnp.float32
    )
    own = spread[:half]
    if with_base:
        own = own + jnp.dot(
            xa_refs[0][...], refs[-5][...], preferred_element_type=jnp.float32
        )
    da_ref[...] = own.reshape(steps, rows, tile).astype(da_ref.dtype)
    db_ref[...] = spread[half:].reshape(steps, rows, tile).astype(db_ref.dtype)


def delta_rows(first, meta, slots, xa, xb, values, scales, base=None, start=0, columns=None):
    steps = 2
    rows = sum(x.shape[0] for x in xa) // steps
    width = values.shape[1]
    columns = columns or values.shape[2]
    tile = min(512, columns)
    skip = start // tile
    smem = pl.BlockSpec(memory_space=pltpu.SMEM)
    in_specs = [smem, smem, smem]
    in_specs += [pl.BlockSpec(x.shape, lambda i: (0, 0)) for x in (*xa, *xb)]
    in_specs += [
        pl.BlockSpec((SLOTS, width, tile), lambda i: (0, 0, i + skip)),
        pl.BlockSpec((SLOTS, width // BLOCK, tile), lambda i: (0, 0, i + skip)),
    ]
    args = [first, meta, slots, *xa, *xb, values, scales]
    if base is not None:
        in_specs.append(pl.BlockSpec((width, tile), lambda i: (0, i + skip)))
        args.append(base)
    out = pl.BlockSpec((steps, rows, tile), lambda i: (0, 0, i))
    taken = SLOTS * 2 * steps * SEG_MOST
    return pl.pallas_call(
        functools.partial(delta_body, base is not None, len(xa), steps, rows),
        grid=(columns // tile,),
        in_specs=in_specs,
        out_specs=(out, out),
        out_shape=(
            jax.ShapeDtypeStruct(
                (steps, rows, columns), jnp.bfloat16
            ),
            jax.ShapeDtypeStruct((steps, rows, columns), jnp.bfloat16),
        ),
        scratch_shapes=[
            pltpu.VMEM((taken, width), jnp.bfloat16),
            pltpu.VMEM((2 * steps * rows, taken), jnp.bfloat16),
        ],
        cost_estimate=LIGHT,
        compiler_params=pltpu.CompilerParams(vmem_limit_bytes=VMEM_LIMIT),
        name="delta_rows",
    )(*args)


def head_rows(ref, r):
    some = 2 * GROUP
    return jnp.concatenate(
        [ref[s, r, p * some:(p + 1) * some, :] for p in range(KVH // 2) for s in range(2)], axis=0
    )


def cache_body(start, len_ref, q_ref, kv_ref, *refs):
    o_ref, lse_ref = refs[-2:]
    block = q_ref.shape[1]
    cached = kv_ref.shape[1]
    some = 4 * GROUP
    scale = 1.0 / math.sqrt(HD)
    position = lax.broadcasted_iota(jnp.int32, (2 * HEADS, cached), 1)
    wide = (some, 2 * HD)
    diagonal = (lax.broadcasted_iota(jnp.int32, wide, 0) // GROUP) % 2 == (
        lax.broadcasted_iota(jnp.int32, wide, 1) // HD
    )
    first = (lax.broadcasted_iota(jnp.int32, (some, HD), 0) // GROUP) % 2 == 0
    scores = []
    for r in range(block):
        rows = head_rows(q_ref, r)
        parts = []
        for p in range(KVH // 2):
            q = rows[p * some:(p + 1) * some]
            q = jnp.concatenate([q, q], axis=1)
            q = jnp.where(diagonal, q, jnp.zeros_like(q))
            parts.append(
                lax.dot_general(
                    q, kv_ref[r, :, p * 2 * HD:(p + 1) * 2 * HD], (((1,), (1,)), ((), ())),
                    preferred_element_type=jnp.float32,
                )
            )
        one = jnp.concatenate(parts, axis=0) * scale
        length = len_ref[start + pl.program_id(0) * block + r]
        scores.append(jnp.where(position < length, one, NEG))
    scores = jnp.concatenate(scores, axis=0)
    top = jnp.max(scores, axis=1, keepdims=True)
    expo = jnp.exp(scores - top)
    total = jnp.sum(expo, axis=1, keepdims=True)
    lse = top + jnp.log(total)
    inverse = 1.0 / total
    expo = expo.astype(jnp.bfloat16)
    for r in range(block):
        base = r * 2 * HEADS
        parts = []
        for p in range(KVH // 2):
            out = jnp.dot(
                expo[base + p * some:base + (p + 1) * some],
                kv_ref[r, :, KEYS + p * 2 * HD:KEYS + (p + 1) * 2 * HD],
                preferred_element_type=jnp.float32,
            )
            parts.append(jnp.where(first, out[:, :HD], out[:, HD:]))
        o_ref[r] = jnp.concatenate(parts, axis=0) * inverse[base:base + 2 * HEADS]
        lse_ref[r] = lse[base:base + 2 * HEADS]


def attend_cache(lengths, q, kv_cache, start, count, before):
    rows = q.shape[1]
    cached, width = kv_cache.shape[1:]
    block = max(1, count // 2)
    skip = start // block
    any_spec = pl.BlockSpec(memory_space=pl.ANY)
    return pl.pallas_call(
        functools.partial(cache_body, start),
        grid=(count // block,),
        in_specs=[
            pl.BlockSpec(memory_space=pltpu.SMEM),
            pl.BlockSpec((2, block, HEADS, HD), lambda i: (0, i + skip, 0, 0)),
            pl.BlockSpec((block, cached, width), lambda i: (i + skip, 0, 0)),
            *[any_spec for _ in before],
        ],
        out_specs=(
            pl.BlockSpec((block, 2 * HEADS, HD), lambda i: (i + skip, 0, 0)),
            pl.BlockSpec((block, 2 * HEADS, 1), lambda i: (i + skip, 0, 0)),
        ),
        out_shape=(
            jax.ShapeDtypeStruct((rows, 2 * HEADS, HD), jnp.float32),
            jax.ShapeDtypeStruct((rows, 2 * HEADS, 1), jnp.float32),
        ),
        input_output_aliases={3 + i: i for i in range(len(before))},
        cost_estimate=COVER,
        compiler_params=pltpu.CompilerParams(vmem_limit_bytes=VMEM_LIMIT),
        name="attend_cache",
    )(lengths, q, kv_cache, *before)


def join_body(q_ref, o_ref, lse_ref, new_ref, out_ref):
    block = q_ref.shape[1]
    pairs = 2 * KVH
    shape = (2 * HEADS, pairs)
    row = lax.broadcasted_iota(jnp.int32, shape, 0)
    col = lax.broadcasted_iota(jnp.int32, shape, 1)
    head = row // (4 * GROUP) * 2 + (row // GROUP) % 2
    step = (row // (2 * GROUP)) % 2
    live = (head == col % KVH) & (col // KVH <= step)
    scale = 1.0 / math.sqrt(HD)
    scores = []
    for r in range(block):
        keys = jnp.concatenate([new_ref[s, r, :KVH, :] for s in range(2)], axis=0)
        one = lax.dot_general(
            head_rows(q_ref, r), keys.astype(jnp.bfloat16), (((1,), (1,)), ((), ())),
            preferred_element_type=jnp.float32,
        ) * scale
        scores.append(jnp.where(live, one, NEG))
    scores = jnp.concatenate(scores, axis=0)
    lse = lse_ref[...].reshape(block * 2 * HEADS, 1)
    top = jnp.maximum(jnp.max(scores, axis=1, keepdims=True), lse)
    expo = jnp.exp(scores - top)
    before = jnp.exp(lse - top)
    inverse = 1.0 / (before + jnp.sum(expo, axis=1, keepdims=True))
    before = before * inverse
    expo = (expo * inverse).astype(jnp.bfloat16)
    some = 2 * GROUP
    for r in range(block):
        rows = slice(r * 2 * HEADS, (r + 1) * 2 * HEADS)
        vals = jnp.concatenate([new_ref[s, r, KVH:, :] for s in range(2)], axis=0)
        out = o_ref[r] * before[rows] + jnp.dot(
            expo[rows], vals.astype(jnp.bfloat16), preferred_element_type=jnp.float32
        )
        out = out.astype(jnp.bfloat16)
        for p in range(KVH // 2):
            for s in range(2):
                at = (2 * p + s) * some
                out_ref[s, r, p * some:(p + 1) * some, :] = out[at:at + some]


def attend_join(q, o, lse, new_kv):
    rows = q.shape[1]
    block = min(8, rows)
    heads = pl.BlockSpec((2, block, HEADS, HD), lambda i: (0, i, 0, 0))
    return pl.pallas_call(
        join_body,
        grid=(rows // block,),
        in_specs=[
            heads,
            pl.BlockSpec((block, 2 * HEADS, HD), lambda i: (i, 0, 0)),
            pl.BlockSpec((block, 2 * HEADS, 1), lambda i: (i, 0, 0)),
            pl.BlockSpec((2, block, 2 * KVH, HD), lambda i: (0, i, 0, 0)),
        ],
        out_specs=heads,
        out_shape=jax.ShapeDtypeStruct((2, rows, HEADS, HD), jnp.bfloat16),
        cost_estimate=LIGHT,
        compiler_params=pltpu.CompilerParams(vmem_limit_bytes=VMEM_LIMIT),
        name="attend_join",
    )(q, o, lse, new_kv)


def after(value, *others):
    return lax.optimization_barrier((value, *others))[0]


def tensor_start(terms, tensor, mask):
    steps, blocks, rows, columns = terms[0].shape
    bit = (lax.axis_index("tensor") // mask) % 2

    def half(at):
        pairs = [t.reshape(steps, blocks // 2, 2, rows, columns) for t in terms]
        return sum(lax.dynamic_index_in_dim(p, at, 2, False).astype(jnp.float32) for p in pairs)

    sent = half(1 - bit).astype(jnp.bfloat16)
    ring = [(i, i ^ mask) for i in range(tensor)]
    return half(bit), sent, lax.ppermute(sent, "tensor", ring)


def local(
    replicas,
    tensor,
    hidden,
    base_weight,
    delta_values,
    delta_scales,
    tenant_slot,
    seg_tenant,
    seg_length,
    queries,
    kv_cache,
    cache_length,
):
    def swap(value, mask):
        return lax.ppermute(value, "replica", [(i, i ^ mask) for i in range(replicas)])

    rows = hidden.shape[1]
    columns = base_weight.shape[1]
    shard_rows = rows // tensor
    half = columns // 2
    parts = [slice(0, half), slice(half, columns)]
    masks = [1 << i for i in range(tensor.bit_length() - 1)]

    def split(value):
        return value.reshape(2, tensor, shard_rows, value.shape[2])

    flat = hidden.reshape(2 * rows, hidden.shape[2])
    cuts = [0, 2 * rows * 11 // 16, 2 * rows]
    sends = [flat[begin:end] for begin, end in zip(cuts[:-1], cuts[1:])]
    piece = shard_rows // 4

    first = (lax.axis_index("replica") * SLOTS).reshape(1)
    meta = jnp.concatenate([seg_tenant, seg_length], axis=1)
    meta = jnp.concatenate([meta, swap(meta, 1)], axis=0)
    sibling = swap(flat, 1)
    masks_far = list(range(2, replicas, 2))
    far_meta = [swap(meta, mask) for mask in masks_far]
    q = queries.reshape(2, shard_rows, HEADS, HD)

    def cached(at, before, *gates):
        return attend_cache(
            cache_length, after(q, *gates), kv_cache, at * piece, piece, before
        )

    early = [swap(sends[0], mask) for mask in masks_far]
    own, other = delta_rows(
        first, meta, tenant_slot, [flat], [after(sibling, q, *sends)], delta_values, delta_scales,
        base_weight,
    )
    early = [after(chunk, own) for chunk in early]
    later = [swap(send, mask) for send in (after(sends[1], own),) for mask in masks_far]
    done = cached(0, (), own, *early)
    back = after(swap(other, 1), *done)
    kept, sent, came = tensor_start([split(own), split(back)], tensor, masks[0])
    done = cached(1, done, sent)
    later = [after(chunk, *done) for chunk in later]
    near = [kept, after(came, *done, *later)]
    for mask in masks[1:-1]:
        kept, sent, came = tensor_start(near, tensor, mask)
        near = [kept, came]
    kept, last, came = tensor_start(near, tensor, masks[-1])

    flying = [[0, None, kept, came]]
    order = [(at, part) for at in range(len(masks_far)) for part in parts]
    theirs_in = [[swap(chunk, 1) for chunk in (early[at], later[at])] for at in range(len(masks_far))]
    for count, (at, part) in enumerate(order):
        mine, theirs = delta_rows(
            first, after(far_meta[at], last), tenant_slot, [early[at], later[at]], theirs_in[at],
            delta_values, delta_scales, None, part.start, half,
        )
        back = swap(theirs, 1)
        flying[-1][3] = after(flying[-1][3], theirs)
        if count < 2:
            done = cached(2 + count, done, theirs, flying[-1][3])
            back = after(back, *done)
        kept, last, came = tensor_start([split(mine), split(back)], tensor, masks[0])
        flying.append([masks_far[at], part, kept, came])
    _, _, kept, came = flying.pop(0)
    near = kept + came.astype(jnp.float32)
    totals = [near[:, 0, :, part] for part in parts]

    for mask, part, kept, came in flying:
        value = [kept, came]
        for step in masks[1:]:
            kept, _, came = tensor_start(value, tensor, step)
            value = [kept, came]
        value = sum(term.astype(jnp.float32) for term in value)
        value = swap(value[:, 0].astype(jnp.bfloat16), mask)
        at = parts.index(part)
        totals[at] = totals[at] + value.astype(jnp.float32)

    new_kv = jnp.concatenate(totals, axis=2).astype(jnp.bfloat16)
    tokens = new_kv.astype(jnp.float32).reshape(2, shard_rows, 2 * KVH, HD)
    attention = attend_join(q, *done, tokens)
    return (new_kv, attention.reshape(2, shard_rows, HEADS * HD))


def solution(mesh):
    placed = (
        P(None, ("groups", "replica"), "tensor"),
        P("tensor", None),
        P(("groups", "replica"), "tensor", None),
        P(("groups", "replica"), "tensor", None),
        P(),
        P(("groups", "replica"), None),
        P(("groups", "replica"), None),
        P(None, ("groups", "replica", "tensor"), None),
        P(("groups", "replica", "tensor"), None, None),
        P(("groups", "replica", "tensor")),
    )
    return jax.shard_map(
        functools.partial(local, mesh.shape["replica"], mesh.shape["tensor"]),
        mesh=mesh,
        in_specs=placed,
        out_specs=(
            P(None, ("groups", "replica", "tensor"), None),
            P(None, ("groups", "replica", "tensor"), None),
        ),
        check_vma=False,
    )
```

```python
import functools
import math

import jax
import jax.numpy as jnp
from jax import lax
from jax.experimental import pallas as pl
from jax.experimental.pallas import tpu as pltpu
from jax.sharding import PartitionSpec as P

HEADS = 64
KVH = 8
HD = 128
GROUP = HEADS // KVH
KEYS = KVH * HD
BLOCK = 128
SEG_MOST = 40
SLOTS = 2
NEG = -1e30
DELTA_VMEM = 50 * 1024 * 1024
ATTEND_VMEM = 50 * 1024 * 1024
LIGHT = pl.CostEstimate(flops=1, bytes_accessed=1, transcendentals=0)
FLAG = pltpu.HBM((8, 128), jnp.float32)
COVER = pl.CostEstimate(flops=1 << 34, bytes_accessed=1 << 26, transcendentals=0)


def in_hbm(*values):
    return [pltpu.with_memory_space_constraint(value, pltpu.HBM) for value in values]


def in_vmem(*values):
    return [pltpu.with_memory_space_constraint(value, pltpu.VMEM) for value in values]


def scatter_order(me, tensor, steps, rows, shape, axis):
    out = lax.broadcasted_iota(jnp.int32, shape, axis) % (steps * rows)
    shard = rows // tensor
    turn = tensor - 1 - out // (steps * shard)
    bits = tensor.bit_length() - 1
    apart = jnp.zeros(shape, jnp.int32)
    for bit in range(bits):
        apart = apart | (((turn >> (bits - 1 - bit)) & 1) << bit)
    step = (out // shard) % steps
    return step * rows + (apart ^ me) * shard + out % shard


def row_positions(meta_ref, slot_ref, first, steps, rows, source, index):
    step = index // rows
    row = index % rows
    per_slot = 2 * steps * SEG_MOST
    place = jnp.full(index.shape, -1, jnp.int32)
    for src in range(2):
        begin = jnp.int32(0)
        for seg in range(meta_ref.shape[1] // 2):
            slot = slot_ref[meta_ref[src, seg]] - first
            length = meta_ref[src, meta_ref.shape[1] // 2 + seg]
            end = begin + length
            held = jnp.logical_and(slot >= 0, slot < SLOTS)
            offset = jnp.where(held, slot * per_slot + src * steps * SEG_MOST - begin, -(1 << 20))
            inside = (source == src) & (row >= begin) & (row < end)
            place = jnp.where(inside, offset + step * SEG_MOST + row, place)
            begin = end
    return place


def delta_body(with_base, tensor, steps, rows, *refs):
    place_ref, slot_ref, meta_ref, xa_ref, xb_ref, val_ref, sc_ref, base_ref = refs[:8]
    if with_base:
        da_ref, db_ref, _, xc_ref, scatter_ref, xo_ref = refs[-6:]
    else:
        da_ref, db_ref, _, xc_ref, scatter_ref = refs[-5:]
    width = val_ref.shape[1]
    half = steps * rows
    taken = SLOTS * 2 * steps * SEG_MOST
    per_slot = taken // SLOTS

    @pl.when(pl.program_id(0) == 0)
    def _():
        first, me = place_ref[0], place_ref[1]
        flat = lax.broadcasted_iota(jnp.int32, (1, 2 * half), 1)
        along = row_positions(meta_ref, slot_ref, first, steps, rows, flat // half, flat % half)
        picks = (lax.broadcasted_iota(jnp.int32, (taken, 2 * half), 0) == along).astype(jnp.bfloat16)
        got = jnp.dot(picks[:, :half], xa_ref[...], preferred_element_type=jnp.float32)
        got += jnp.dot(picks[:, half:], xb_ref[...], preferred_element_type=jnp.float32)
        xc_ref[...] = got.astype(jnp.bfloat16)
        order = scatter_order(me, tensor, steps, rows, (1, 2 * half), 1)
        along = row_positions(meta_ref, slot_ref, first, steps, rows, flat // half, order)
        picks = lax.broadcasted_iota(jnp.int32, (taken, 2 * half), 0) == along
        scatter_ref[...] = picks.astype(jnp.float32).T.astype(jnp.bfloat16)
        if with_base:
            picks = lax.broadcasted_iota(jnp.int32, (half, half), 0) == order[:, :half]
            xo_ref[...] = jnp.dot(
                picks.astype(jnp.float32).T.astype(jnp.bfloat16), xa_ref[...],
                preferred_element_type=jnp.float32,
            ).astype(jnp.bfloat16)

    parts = []
    for slot in range(SLOTS):
        scaled = [
            val_ref[slot, b * BLOCK:(b + 1) * BLOCK, :] * sc_ref[slot, b:b + 1, :]
            for b in range(width // BLOCK)
        ]
        weight = jnp.concatenate(scaled, axis=0)
        parts.append(
            jnp.dot(
                xc_ref[slot * per_slot:(slot + 1) * per_slot, :], weight,
                preferred_element_type=jnp.float32,
            ).astype(jnp.bfloat16)
        )
    spread = jnp.dot(
        scatter_ref[...], jnp.concatenate(parts, axis=0), preferred_element_type=jnp.float32
    )
    own = spread[:half]
    if with_base:
        own = own + jnp.dot(xo_ref[...], base_ref[...], preferred_element_type=jnp.float32)
    da_ref[...] = own.astype(da_ref.dtype)
    db_ref[...] = spread[half:].astype(db_ref.dtype)


def delta_rows(place, slots, meta, xa, xb, values, scales, tensor, base=None, start=0, columns=None, gates=()):
    steps = 2
    rows = xa.shape[0] // steps
    width = values.shape[1]
    columns = columns or values.shape[2]
    tile = min(512, columns)
    skip = start // tile
    smem = pl.BlockSpec(memory_space=pltpu.SMEM)
    whole = pl.BlockSpec(xa.shape, lambda i: (0, 0))
    in_specs = [
        smem, smem, smem, whole, whole,
        pl.BlockSpec((SLOTS, width, tile), lambda i: (0, 0, i + skip)),
        pl.BlockSpec((SLOTS, width // BLOCK, tile), lambda i: (0, 0, i + skip)),
    ]
    args = [place, *in_hbm(slots), meta, *in_vmem(xa, xb), *in_hbm(values, scales)]
    if base is not None:
        in_specs.append(pl.BlockSpec((width, tile), lambda i: (0, i + skip)))
        args += in_hbm(base)
    in_specs += [pl.BlockSpec(memory_space=pltpu.HBM) for _ in gates]
    args += in_hbm(*gates)
    taken = SLOTS * 2 * steps * SEG_MOST
    out = pl.BlockSpec((steps * rows, tile), lambda i: (0, i))
    shape = pltpu.HBM((steps * rows, columns), jnp.bfloat16)
    scratch = [
        pltpu.VMEM((taken, width), jnp.bfloat16),
        pltpu.VMEM((2 * steps * rows, taken), jnp.bfloat16),
    ]
    if base is not None:
        scratch.append(pltpu.VMEM((steps * rows, width), jnp.bfloat16))
    return pl.pallas_call(
        functools.partial(delta_body, base is not None, tensor, steps, rows),
        grid=(columns // tile,),
        in_specs=in_specs,
        out_specs=(out, out, pl.BlockSpec(memory_space=pltpu.HBM)),
        out_shape=(shape, shape, FLAG),
        scratch_shapes=scratch,
        cost_estimate=LIGHT,
        compiler_params=pltpu.CompilerParams(vmem_limit_bytes=DELTA_VMEM),
        name="delta_rows",
    )(*args)


def head_rows(ref, r):
    some = 2 * GROUP
    return jnp.concatenate(
        [ref[s, r, p * some:(p + 1) * some, :] for p in range(KVH // 2) for s in range(2)], axis=0
    )


def cache_body(start, len_ref, q_ref, kv_ref, *refs):
    o_ref, lse_ref, _ = refs[-3:]
    block = q_ref.shape[1]
    cached = kv_ref.shape[1]
    some = 4 * GROUP
    scale = 1.0 / math.sqrt(HD)
    position = lax.broadcasted_iota(jnp.int32, (2 * HEADS, cached), 1)
    wide = (some, 2 * HD)
    diagonal = (lax.broadcasted_iota(jnp.int32, wide, 0) // GROUP) % 2 == (
        lax.broadcasted_iota(jnp.int32, wide, 1) // HD
    )
    first = (lax.broadcasted_iota(jnp.int32, (some, HD), 0) // GROUP) % 2 == 0
    scores = []
    for r in range(block):
        rows = head_rows(q_ref, r)
        parts = []
        for p in range(KVH // 2):
            q = rows[p * some:(p + 1) * some]
            q = jnp.concatenate([q, q], axis=1)
            q = jnp.where(diagonal, q, jnp.zeros_like(q))
            parts.append(
                lax.dot_general(
                    q, kv_ref[r, :, p * 2 * HD:(p + 1) * 2 * HD], (((1,), (1,)), ((), ())),
                    preferred_element_type=jnp.float32,
                )
            )
        one = jnp.concatenate(parts, axis=0) * scale
        length = len_ref[start + pl.program_id(0) * block + r]
        scores.append(jnp.where(position < length, one, NEG))
    scores = jnp.concatenate(scores, axis=0)
    top = jnp.max(scores, axis=1, keepdims=True)
    expo = jnp.exp(scores - top)
    total = jnp.sum(expo, axis=1, keepdims=True)
    lse = top + jnp.log(total)
    inverse = 1.0 / total
    expo = expo.astype(jnp.bfloat16)
    for r in range(block):
        base = r * 2 * HEADS
        parts = []
        for p in range(KVH // 2):
            out = jnp.dot(
                expo[base + p * some:base + (p + 1) * some],
                kv_ref[r, :, KEYS + p * 2 * HD:KEYS + (p + 1) * 2 * HD],
                preferred_element_type=jnp.float32,
            )
            parts.append(jnp.where(first, out[:, :HD], out[:, HD:]))
        o_ref[r] = jnp.concatenate(parts, axis=0) * inverse[base:base + 2 * HEADS]
        lse_ref[r] = lse[base:base + 2 * HEADS]


def attend_cache(lengths, q, kv_cache, start, count, before, cost, gates):
    rows = q.shape[1]
    cached, width = kv_cache.shape[1:]
    block = min(8, count)
    skip = start // block
    any_spec = pl.BlockSpec(memory_space=pltpu.HBM)
    return pl.pallas_call(
        functools.partial(cache_body, start),
        grid=(count // block,),
        in_specs=[
            pl.BlockSpec(memory_space=pltpu.SMEM),
            pl.BlockSpec((2, block, HEADS, HD), lambda i: (0, i + skip, 0, 0)),
            pl.BlockSpec((block, cached, width), lambda i: (i + skip, 0, 0)),
            *[any_spec for _ in (*before, *gates)],
        ],
        out_specs=(
            pl.BlockSpec((block, 2 * HEADS, HD), lambda i: (i + skip, 0, 0)),
            pl.BlockSpec((block, 2 * HEADS, 1), lambda i: (i + skip, 0, 0)),
            any_spec,
        ),
        out_shape=(
            pltpu.HBM((rows, 2 * HEADS, HD), jnp.float32),
            pltpu.HBM((rows, 2 * HEADS, 1), jnp.float32),
            FLAG,
        ),
        input_output_aliases={3 + i: i for i in range(len(before))},
        cost_estimate=cost,
        compiler_params=pltpu.CompilerParams(vmem_limit_bytes=ATTEND_VMEM),
        name="attend_cache",
    )(lengths, *in_hbm(q, kv_cache, *before, *gates))


def weigh_body(q_ref, o_ref, lse_ref, keys_ref, prob_ref, out_ref):
    block = q_ref.shape[1]
    shape = (2 * HEADS, 2 * KVH)
    row = lax.broadcasted_iota(jnp.int32, shape, 0)
    col = lax.broadcasted_iota(jnp.int32, shape, 1)
    head = row // (4 * GROUP) * 2 + (row // GROUP) % 2
    step = (row // (2 * GROUP)) % 2
    live = (head == col % KVH) & (col // KVH <= step)
    scale = 1.0 / math.sqrt(HD)
    scores = []
    for r in range(block):
        keys = jnp.concatenate([keys_ref[s, r] for s in range(2)], axis=0).astype(jnp.bfloat16)
        one = lax.dot_general(
            head_rows(q_ref, r), keys, (((1,), (1,)), ((), ())), preferred_element_type=jnp.float32
        ) * scale
        scores.append(jnp.where(live, one, NEG))
    scores = jnp.concatenate(scores, axis=0)
    lse = lse_ref[...].reshape(block * 2 * HEADS, 1)
    top = jnp.maximum(jnp.max(scores, axis=1, keepdims=True), lse)
    expo = jnp.exp(scores - top)
    before = jnp.exp(lse - top)
    inverse = 1.0 / (before + jnp.sum(expo, axis=1, keepdims=True))
    before = before * inverse
    prob_ref[...] = (expo * inverse).astype(jnp.bfloat16).reshape(prob_ref.shape)
    for r in range(block):
        out_ref[r] = o_ref[r] * before[r * 2 * HEADS:(r + 1) * 2 * HEADS]


def weigh_new(q, o, lse, keys):
    rows = q.shape[1]
    block = min(8, rows)
    half = pl.BlockSpec((block, 2 * HEADS, HD), lambda i: (i, 0, 0))
    return pl.pallas_call(
        weigh_body,
        grid=(rows // block,),
        in_specs=[
            pl.BlockSpec((2, block, HEADS, HD), lambda i: (0, i, 0, 0)),
            half,
            pl.BlockSpec((block, 2 * HEADS, 1), lambda i: (i, 0, 0)),
            pl.BlockSpec((2, block, KVH, HD), lambda i: (0, i, 0, 0)),
        ],
        out_specs=(pl.BlockSpec((block, 2 * HEADS, 2 * KVH), lambda i: (i, 0, 0)), half),
        out_shape=(
            pltpu.VMEM((rows, 2 * HEADS, 2 * KVH), jnp.bfloat16),
            pltpu.VMEM(o.shape, jnp.float32),
        ),
        cost_estimate=LIGHT,
        compiler_params=pltpu.CompilerParams(vmem_limit_bytes=ATTEND_VMEM),
        name="weigh_new",
    )(*in_hbm(q, o, lse), keys)


def add_body(prob_ref, o_ref, vals_ref, out_ref, sum_ref):
    block = o_ref.shape[0]
    for r in range(block):
        vals = jnp.concatenate([vals_ref[s, r] for s in range(2)], axis=0).astype(jnp.bfloat16)
        sum_ref[r * 2 * HEADS:(r + 1) * 2 * HEADS, :] = o_ref[r] + jnp.dot(
            prob_ref[r], vals, preferred_element_type=jnp.float32
        )
    some = 2 * GROUP
    for at in range(2 * HEADS):
        pair, step, head = at // (2 * some), (at // some) % 2, at % some
        column = (pair * some + head) * HD
        out_ref[step, :, column:column + HD] = sum_ref[
            pl.ds(at, block, stride=2 * HEADS), :
        ].astype(jnp.bfloat16)


def add_new(probs, o, vals):
    rows = o.shape[0]
    block = min(16, rows)
    return pl.pallas_call(
        add_body,
        grid=(rows // block,),
        in_specs=[
            pl.BlockSpec((block, 2 * HEADS, 2 * KVH), lambda i: (i, 0, 0)),
            pl.BlockSpec((block, 2 * HEADS, HD), lambda i: (i, 0, 0)),
            pl.BlockSpec((2, block, KVH, HD), lambda i: (0, i, 0, 0)),
        ],
        out_specs=pl.BlockSpec((2, block, HEADS * HD), lambda i: (0, i, 0)),
        out_shape=jax.ShapeDtypeStruct((2, rows, HEADS * HD), jnp.bfloat16),
        scratch_shapes=[pltpu.VMEM((block * 2 * HEADS, HD), jnp.float32)],
        cost_estimate=LIGHT,
        compiler_params=pltpu.CompilerParams(vmem_limit_bytes=ATTEND_VMEM),
        name="add_new",
    )(*in_vmem(probs, o), vals)


def marker_body(*refs):
    del refs


def marker(flag):
    any_spec = pl.BlockSpec(memory_space=pltpu.HBM)
    return pl.pallas_call(
        marker_body,
        in_specs=[any_spec],
        out_specs=any_spec,
        out_shape=FLAG,
        cost_estimate=COVER,
        compiler_params=pltpu.CompilerParams(vmem_limit_bytes=1 << 20),
        name="marker",
    )(*in_hbm(flag))


def tie(*values):
    return lax.optimization_barrier(values)


def halves(terms):
    half = terms[0].shape[0] // 2
    return [
        sum(term[begin:begin + half].astype(jnp.float32) for term in terms).astype(jnp.bfloat16)
        for begin in (0, half)
    ]


def sum_of(terms):
    return sum(term.astype(jnp.float32) for term in terms).astype(jnp.bfloat16)


def cross(value, tensor, mask):
    return lax.ppermute(value, "tensor", [(i, i ^ mask) for i in range(tensor)])


def local(
    replicas,
    tensor,
    hidden,
    base_weight,
    delta_values,
    delta_scales,
    tenant_slot,
    seg_tenant,
    seg_length,
    queries,
    kv_cache,
    cache_length,
):
    def swap(value, mask):
        return lax.ppermute(value, "replica", [(i, i ^ mask) for i in range(replicas)])

    rows = hidden.shape[1]
    columns = base_weight.shape[1]
    shard_rows = rows // tensor
    half = columns // 2
    masks = [1 << i for i in range(tensor.bit_length() - 1)]
    flat = hidden.reshape(2 * rows, hidden.shape[2])
    piece = shard_rows // 2
    masks_far = list(range(2, replicas, 2))

    place = jnp.stack([lax.axis_index("replica") * SLOTS, lax.axis_index("tensor")]).astype(jnp.int32)
    far = [swap(flat, mask) for mask in masks_far]
    sibling = swap(flat, 1)
    meta = jnp.concatenate([seg_tenant, seg_length], axis=1)
    meta = jnp.concatenate([meta, swap(meta, 1)], axis=0)
    far_meta = [swap(meta, mask) for mask in masks_far]

    def cached(at, before, flag):
        return attend_cache(cache_length, q, kv_cache, at * piece, piece, before, LIGHT, [flag])

    own, other, flag = delta_rows(
        place, tenant_slot, meta, flat, sibling, delta_values, delta_scales, tensor, base_weight
    )
    back = swap(other, 1)
    queries, flag = tie(queries, flag)
    q, flag = tie(queries.reshape(2, shard_rows, HEADS, HD), flag)
    flag = marker(flag)
    back, flag = tie(back, flag)
    sent, kept = halves([own, back])
    sent, far, flag = tie(sent, far, flag)
    theirs_in = [swap(rows_in, 1) for rows_in in far]
    near = [kept, cross(sent, tensor, masks[0])]

    flying = []
    for mask, pair, far_rows, far_sibling in zip(masks_far, far_meta, far, theirs_in):
        for start in (0, half):
            mine, theirs, flag = delta_rows(
                place, tenant_slot, pair, far_rows, far_sibling, delta_values, delta_scales,
                tensor, None, start, half, [flag],
            )
            back = swap(theirs, 1)
            if flying:
                flying[-1], flag = tie(flying[-1], flag)
                flying[-1] = swap(sum_of(flying[-1]), flying_mask)
            else:
                near, flag = tie(near, flag)
                near = sum_of(near)
            flag = marker(flag)
            back, flag = tie(back, flag)
            sent, kept = halves([mine, back])
            sent, flag = tie(sent, flag)
            flying.append([kept, cross(sent, tensor, masks[0])])
            flying_mask = mask

    *done, flag = cached(0, (), flag)
    flying, flag = tie(flying, flag)
    last = sum_of(flying[-1])
    values = [[near[:, start:start + half], *flying[at::2]] for at, start in enumerate((0, half))]
    sent, kept = halves(values[0])
    last, sent, flag = tie(last, sent, flag)
    values[1][-1] = swap(last, flying_mask)
    values[0] = [kept, cross(sent, tensor, masks[1])]
    *done, flag = cached(1, done, flag)
    values, done = tie(values, done)
    finals = []
    for at, value in enumerate(values):
        for mask in masks[2 - at:]:
            sent, kept = halves(value)
            value = [kept, cross(sent, tensor, mask)]
        finals.append(value)

    def by_head(value):
        return value.astype(jnp.float32).reshape(2, shard_rows, KVH, HD)

    keys = sum_of(finals[0]).reshape(2, shard_rows, half)
    probs, weighed = weigh_new(q, *done, by_head(keys))
    last, probs = tie(finals[1], probs)
    vals = sum_of(last).reshape(2, shard_rows, half)
    attention = add_new(probs, weighed, by_head(vals))
    return (jnp.concatenate([keys, vals], axis=2), attention)


def solution(mesh):
    placed = (
        P(None, ("groups", "replica"), "tensor"),
        P("tensor", None),
        P(("groups", "replica"), "tensor", None),
        P(("groups", "replica"), "tensor", None),
        P(),
        P(("groups", "replica"), None),
        P(("groups", "replica"), None),
        P(None, ("groups", "replica", "tensor"), None),
        P(("groups", "replica", "tensor"), None, None),
        P(("groups", "replica", "tensor")),
    )
    return jax.shard_map(
        functools.partial(local, mesh.shape["replica"], mesh.shape["tensor"]),
        mesh=mesh,
        in_specs=placed,
        out_specs=(
            P(None, ("groups", "replica", "tensor"), None),
            P(None, ("groups", "replica", "tensor"), None),
        ),
        check_vma=False,
    )
```

```python
import functools
import math

import jax
import jax.numpy as jnp
from jax import lax
from jax.experimental import pallas as pl
from jax.experimental.pallas import tpu as pltpu
from jax.sharding import PartitionSpec as P

HEADS = 64
KVH = 8
HD = 128
GROUP = HEADS // KVH
KEYS = KVH * HD
BLOCK = 128
SEG_MOST = 40
SLOTS = 2
QUARTERS = 4
NEG = -1e30
DELTA_VMEM = 50 * 1024 * 1024
ATTEND_VMEM = 50 * 1024 * 1024
LIGHT = pl.CostEstimate(flops=1, bytes_accessed=1, transcendentals=0)
FLAG = pltpu.HBM((8, 128), jnp.float32)
COVER = pl.CostEstimate(flops=1 << 34, bytes_accessed=1 << 26, transcendentals=0)


def in_hbm(*values):
    return [pltpu.with_memory_space_constraint(value, pltpu.HBM) for value in values]


def in_vmem(*values):
    return [pltpu.with_memory_space_constraint(value, pltpu.VMEM) for value in values]


def scatter_order(me, tensor, steps, rows, shape, axis):
    out = lax.broadcasted_iota(jnp.int32, shape, axis) % (steps * rows)
    shard = rows // tensor
    turn = tensor - 1 - out // (steps * shard)
    bits = tensor.bit_length() - 1
    apart = jnp.zeros(shape, jnp.int32)
    for bit in range(bits):
        apart = apart | (((turn >> (bits - 1 - bit)) & 1) << bit)
    step = (out // shard) % steps
    return step * rows + (apart ^ me) * shard + out % shard


def row_positions(meta_ref, slot_ref, first, steps, rows, source, index):
    step = index // rows
    row = index % rows
    per_slot = 2 * steps * SEG_MOST
    place = jnp.full(index.shape, -1, jnp.int32)
    for src in range(2):
        begin = jnp.int32(0)
        for seg in range(meta_ref.shape[1] // 2):
            slot = slot_ref[meta_ref[src, seg]] - first
            length = meta_ref[src, meta_ref.shape[1] // 2 + seg]
            end = begin + length
            held = jnp.logical_and(slot >= 0, slot < SLOTS)
            offset = jnp.where(held, slot * per_slot + src * steps * SEG_MOST - begin, -(1 << 20))
            inside = (source == src) & (row >= begin) & (row < end)
            place = jnp.where(inside, offset + step * SEG_MOST + row, place)
            begin = end
    return place


def delta_body(with_base, tensor, steps, rows, chunks, *refs):
    place_ref, slot_ref, meta_ref, xa_ref = refs[:4]
    xb_refs = refs[4:4 + chunks]
    val_ref, sc_ref, base_ref = refs[4 + chunks:7 + chunks]
    if with_base:
        da_ref, *db_refs, _, xc_ref, scatter_ref, xo_ref = refs[-5 - QUARTERS:]
    else:
        da_ref, *db_refs, _, xc_ref, scatter_ref = refs[-4 - QUARTERS:]
    half = steps * rows
    taken = SLOTS * 2 * steps * SEG_MOST

    @pl.when(pl.program_id(0) == 0)
    def _():
        first, me = place_ref[0], place_ref[1]
        flat = lax.broadcasted_iota(jnp.int32, (1, 2 * half), 1)
        along = row_positions(meta_ref, slot_ref, first, steps, rows, flat // half, flat % half)
        picks = (lax.broadcasted_iota(jnp.int32, (taken, 2 * half), 0) == along).astype(jnp.bfloat16)
        got = jnp.dot(picks[:, :half], xa_ref[...], preferred_element_type=jnp.float32)
        xb = jnp.concatenate([ref[...] for ref in xb_refs], axis=0)
        got += jnp.dot(picks[:, half:], xb, preferred_element_type=jnp.float32)
        xc_ref[...] = got.astype(jnp.bfloat16)
        order = scatter_order(me, tensor, steps, rows, (1, 2 * half), 1)
        along = row_positions(meta_ref, slot_ref, first, steps, rows, flat // half, order)
        picks = lax.broadcasted_iota(jnp.int32, (taken, 2 * half), 0) == along
        scatter_ref[...] = picks.astype(jnp.float32).T.astype(jnp.bfloat16)
        if with_base:
            picks = lax.broadcasted_iota(jnp.int32, (half, half), 0) == order[:, :half]
            xo_ref[...] = jnp.dot(
                picks.astype(jnp.float32).T.astype(jnp.bfloat16), xa_ref[...],
                preferred_element_type=jnp.float32,
            ).astype(jnp.bfloat16)

    spread = spread_products(xc_ref, scatter_ref, val_ref, sc_ref)
    own = spread[:half]
    if with_base:
        own = own + jnp.dot(xo_ref[...], base_ref[...], preferred_element_type=jnp.float32)
    da_ref[...] = own.astype(da_ref.dtype)
    put_quarters(db_refs, spread[half:])


def put_quarters(refs, value):
    rows = value.shape[0] // QUARTERS
    for at, ref in enumerate(refs):
        ref[...] = value[at * rows:(at + 1) * rows].astype(ref.dtype)


def spread_products(xc_ref, scatter_ref, val_ref, sc_ref):
    width = val_ref.shape[1]
    per_slot = xc_ref.shape[0] // SLOTS
    parts = []
    for slot in range(SLOTS):
        scaled = [
            val_ref[slot, b * BLOCK:(b + 1) * BLOCK, :] * sc_ref[slot, b:b + 1, :]
            for b in range(width // BLOCK)
        ]
        weight = jnp.concatenate(scaled, axis=0)
        parts.append(
            jnp.dot(
                xc_ref[slot * per_slot:(slot + 1) * per_slot, :], weight,
                preferred_element_type=jnp.float32,
            ).astype(jnp.bfloat16)
        )
    return jnp.dot(
        scatter_ref[...], jnp.concatenate(parts, axis=0), preferred_element_type=jnp.float32
    )


def more_body(xc_ref, scatter_ref, val_ref, sc_ref, *refs):
    da_ref, *db_refs, _ = refs[-2 - QUARTERS:]
    half = da_ref.shape[0]
    spread = spread_products(xc_ref, scatter_ref, val_ref, sc_ref)
    da_ref[...] = spread[:half].astype(da_ref.dtype)
    put_quarters(db_refs, spread[half:])


def more_delta_rows(gathered, scatter, values, scales, start, columns, gates):
    width = values.shape[1]
    half = scatter.shape[0] // 2
    tile = min(512, columns)
    skip = start // tile
    out = pl.BlockSpec((half, tile), lambda i: (0, i))
    shape = pltpu.VMEM((half, columns), jnp.bfloat16)
    quarters = [pl.BlockSpec((half // QUARTERS, tile), lambda i: (0, i))] * QUARTERS
    quarter_shapes = [pltpu.VMEM((half // QUARTERS, columns), jnp.bfloat16)] * QUARTERS
    return pl.pallas_call(
        more_body,
        grid=(columns // tile,),
        in_specs=[
            pl.BlockSpec(gathered.shape, lambda i: (0, 0)),
            pl.BlockSpec(scatter.shape, lambda i: (0, 0)),
            pl.BlockSpec((SLOTS, width, tile), lambda i: (0, 0, i + skip)),
            pl.BlockSpec((SLOTS, width // BLOCK, tile), lambda i: (0, 0, i + skip)),
            *[pl.BlockSpec(memory_space=pltpu.HBM) for _ in gates],
        ],
        out_specs=(out, *quarters, pl.BlockSpec(memory_space=pltpu.HBM)),
        out_shape=(shape, *quarter_shapes, FLAG),
        cost_estimate=LIGHT,
        compiler_params=pltpu.CompilerParams(vmem_limit_bytes=DELTA_VMEM),
        name="more_delta_rows",
    )(*in_vmem(gathered, scatter), *in_hbm(values, scales, *gates))


def delta_rows(place, slots, meta, xa, xb, values, scales, tensor, base=None, start=0, columns=None, gates=()):
    steps = 2
    rows = xa.shape[0] // steps
    width = values.shape[1]
    columns = columns or values.shape[2]
    tile = min(512, columns)
    skip = start // tile
    smem = pl.BlockSpec(memory_space=pltpu.SMEM)
    whole = pl.BlockSpec(xa.shape, lambda i: (0, 0))
    in_specs = [
        smem, smem, smem, whole, *[pl.BlockSpec(x.shape, lambda i: (0, 0)) for x in xb],
        pl.BlockSpec((SLOTS, width, tile), lambda i: (0, 0, i + skip)),
        pl.BlockSpec((SLOTS, width // BLOCK, tile), lambda i: (0, 0, i + skip)),
    ]
    args = [place, *in_hbm(slots), meta, *in_vmem(xa, *xb), *in_hbm(values, scales)]
    if base is not None:
        in_specs.append(pl.BlockSpec((width, tile), lambda i: (0, i + skip)))
        args += in_hbm(base)
    in_specs += [pl.BlockSpec(memory_space=pltpu.HBM) for _ in gates]
    args += in_hbm(*gates)
    taken = SLOTS * 2 * steps * SEG_MOST
    out = pl.BlockSpec((steps * rows, tile), lambda i: (0, i))
    shape = pltpu.VMEM((steps * rows, columns), jnp.bfloat16)
    quarter = steps * rows // QUARTERS
    quarters = [pl.BlockSpec((quarter, tile), lambda i: (0, i))] * QUARTERS
    quarter_shapes = [pltpu.VMEM((quarter, columns), jnp.bfloat16)] * QUARTERS
    gathered = (taken, width), (2 * steps * rows, taken)
    if base is not None:
        scratch = [pltpu.VMEM(dims, jnp.bfloat16) for dims in (*gathered, xa.shape)]
        kept_specs, kept_shapes = (), ()
    else:
        scratch = []
        kept_specs = tuple(pl.BlockSpec(dims, lambda i: (0, 0)) for dims in gathered)
        kept_shapes = tuple(pltpu.VMEM(dims, jnp.bfloat16) for dims in gathered)
    return pl.pallas_call(
        functools.partial(delta_body, base is not None, tensor, steps, rows, len(xb)),
        grid=(columns // tile,),
        in_specs=in_specs,
        out_specs=(out, *quarters, pl.BlockSpec(memory_space=pltpu.HBM), *kept_specs),
        out_shape=(shape, *quarter_shapes, FLAG, *kept_shapes),
        scratch_shapes=scratch,
        cost_estimate=LIGHT,
        compiler_params=pltpu.CompilerParams(vmem_limit_bytes=DELTA_VMEM),
        name="delta_rows",
    )(*args)


def cache_body(start, count, len_ref, q_ref, kv_ref, *refs):
    o_ref, lse_ref, rows_ref, _, sorted_ref = refs[-5:]
    block = rows_ref.shape[0]
    cached = kv_ref.shape[1]
    some = 4 * GROUP
    scale = 1.0 / math.sqrt(HD)

    @pl.when(pl.program_id(0) == 0)
    def _():
        low = start // 16 * 16
        high = min(-(-(start + count) // 16) * 16, q_ref.shape[1])
        for at in range(2 * HEADS):
            pair, step, head = at // some, at // (some // 2) % 2, at % (some // 2)
            column = (pair * some // 2 + head) * HD
            value = q_ref[step, low:high, column:column + HD].astype(jnp.float32)
            value = value[start - low:start - low + count]
            if count > 1:
                sorted_ref[pl.ds(at, count, stride=2 * HEADS), :] = value
            else:
                sorted_ref[at:at + 1, :] = value

    position = lax.broadcasted_iota(jnp.int32, (2 * HEADS, cached), 1)
    wide = (some, 2 * HD)
    diagonal = (lax.broadcasted_iota(jnp.int32, wide, 0) // GROUP) % 2 == (
        lax.broadcasted_iota(jnp.int32, wide, 1) // HD
    )
    first = (lax.broadcasted_iota(jnp.int32, (some, HD), 0) // GROUP) % 2 == 0
    scores = []
    for r in range(block):
        at = pl.multiple_of((pl.program_id(0) * block + r) * 2 * HEADS, 2 * HEADS)
        rows = sorted_ref[pl.ds(at, 2 * HEADS), :].astype(jnp.bfloat16)
        rows_ref[r] = rows
        parts = []
        for p in range(KVH // 2):
            q = rows[p * some:(p + 1) * some]
            q = jnp.concatenate([q, q], axis=1)
            q = jnp.where(diagonal, q, jnp.zeros_like(q))
            parts.append(
                lax.dot_general(
                    q, kv_ref[r, :, p * 2 * HD:(p + 1) * 2 * HD], (((1,), (1,)), ((), ())),
                    preferred_element_type=jnp.float32,
                )
            )
        one = jnp.concatenate(parts, axis=0) * scale
        length = len_ref[start + pl.program_id(0) * block + r]
        scores.append(jnp.where(position < length, one, NEG))
    scores = jnp.concatenate(scores, axis=0)
    top = jnp.max(scores, axis=1, keepdims=True)
    expo = jnp.exp(scores - top)
    total = jnp.sum(expo, axis=1, keepdims=True)
    lse = top + jnp.log(total)
    inverse = 1.0 / total
    expo = expo.astype(jnp.bfloat16)
    for r in range(block):
        base = r * 2 * HEADS
        parts = []
        for p in range(KVH // 2):
            out = jnp.dot(
                expo[base + p * some:base + (p + 1) * some],
                kv_ref[r, :, KEYS + p * 2 * HD:KEYS + (p + 1) * 2 * HD],
                preferred_element_type=jnp.float32,
            )
            parts.append(jnp.where(first, out[:, :HD], out[:, HD:]))
        o_ref[r] = jnp.concatenate(parts, axis=0) * inverse[base:base + 2 * HEADS]
        lse_ref[r] = lse[base:base + 2 * HEADS]


def attend_cache(lengths, queries, kv_cache, start, count, before, cost, gates):
    rows = queries.shape[1]
    cached, width = kv_cache.shape[1:]
    block = max(1, min(8, count // 2))
    skip = start // block
    in_place = pl.BlockSpec(memory_space=pltpu.HBM)
    return pl.pallas_call(
        functools.partial(cache_body, start, count),
        grid=(count // block,),
        in_specs=[
            pl.BlockSpec(memory_space=pltpu.SMEM),
            pl.BlockSpec(queries.shape, lambda i: (0, 0, 0)),
            pl.BlockSpec((block, cached, width), lambda i: (i + skip, 0, 0)),
            *[in_place for _ in (*before, *gates)],
        ],
        out_specs=(
            pl.BlockSpec((block, 2 * HEADS, HD), lambda i: (i + skip, 0, 0)),
            pl.BlockSpec((block, 2 * HEADS, 1), lambda i: (i + skip, 0, 0)),
            pl.BlockSpec((block, 2 * HEADS, HD), lambda i: (i + skip, 0, 0)),
            in_place,
        ),
        out_shape=(
            pltpu.HBM((rows, 2 * HEADS, HD), jnp.float32),
            pltpu.HBM((rows, 2 * HEADS, 1), jnp.float32),
            pltpu.HBM((rows, 2 * HEADS, HD), jnp.bfloat16),
            FLAG,
        ),
        scratch_shapes=[pltpu.VMEM((count * 2 * HEADS, HD), jnp.float32)],
        input_output_aliases={3 + i: i for i in range(len(before))},
        cost_estimate=cost,
        compiler_params=pltpu.CompilerParams(vmem_limit_bytes=ATTEND_VMEM),
        name="attend_cache",
    )(lengths, *in_hbm(queries, kv_cache, *before, *gates))


def weigh_body(o_ref, lse_ref, rows_ref, keys_ref, prob_ref, out_ref):
    block = o_ref.shape[0]
    shape = (2 * HEADS, 2 * KVH)
    row = lax.broadcasted_iota(jnp.int32, shape, 0)
    col = lax.broadcasted_iota(jnp.int32, shape, 1)
    head = row // (4 * GROUP) * 2 + (row // GROUP) % 2
    step = (row // (2 * GROUP)) % 2
    live = (head == col % KVH) & (col // KVH <= step)
    scale = 1.0 / math.sqrt(HD)
    scores = []
    for r in range(block):
        keys = jnp.concatenate([keys_ref[s, r] for s in range(2)], axis=0).astype(jnp.bfloat16)
        one = lax.dot_general(
            rows_ref[r], keys, (((1,), (1,)), ((), ())), preferred_element_type=jnp.float32
        ) * scale
        scores.append(jnp.where(live, one, NEG))
    scores = jnp.concatenate(scores, axis=0)
    lse = lse_ref[...].reshape(block * 2 * HEADS, 1)
    top = jnp.maximum(jnp.max(scores, axis=1, keepdims=True), lse)
    expo = jnp.exp(scores - top)
    before = jnp.exp(lse - top)
    inverse = 1.0 / (before + jnp.sum(expo, axis=1, keepdims=True))
    before = before * inverse
    prob_ref[...] = (expo * inverse).astype(jnp.bfloat16).reshape(prob_ref.shape)
    for r in range(block):
        out_ref[r] = o_ref[r] * before[r * 2 * HEADS:(r + 1) * 2 * HEADS]


def weigh_new(o, lse, queries, keys):
    rows = o.shape[0]
    block = min(8, rows)
    half = pl.BlockSpec((block, 2 * HEADS, HD), lambda i: (i, 0, 0))
    return pl.pallas_call(
        weigh_body,
        grid=(rows // block,),
        in_specs=[
            half,
            pl.BlockSpec((block, 2 * HEADS, 1), lambda i: (i, 0, 0)),
            half,
            pl.BlockSpec((2, block, KVH, HD), lambda i: (0, i, 0, 0)),
        ],
        out_specs=(pl.BlockSpec((block, 2 * HEADS, 2 * KVH), lambda i: (i, 0, 0)), half),
        out_shape=(
            pltpu.VMEM((rows, 2 * HEADS, 2 * KVH), jnp.bfloat16),
            pltpu.VMEM(o.shape, jnp.float32),
        ),
        cost_estimate=LIGHT,
        compiler_params=pltpu.CompilerParams(vmem_limit_bytes=ATTEND_VMEM),
        name="weigh_new",
    )(*in_hbm(o, lse, queries), keys)


def add_body(prob_ref, o_ref, keys_ref, flat_ref, vals_ref, out_ref, new_ref, sum_ref):
    half = keys_ref.shape[2]
    new_ref[:, :, :half] = keys_ref[...]
    new_ref[:, :, half:] = flat_ref[...]
    block = o_ref.shape[0]
    for r in range(block):
        vals = jnp.concatenate([vals_ref[s, r] for s in range(2)], axis=0).astype(jnp.bfloat16)
        sum_ref[r * 2 * HEADS:(r + 1) * 2 * HEADS, :] = o_ref[r] + jnp.dot(
            prob_ref[r], vals, preferred_element_type=jnp.float32
        )
    some = 2 * GROUP
    for at in range(2 * HEADS):
        pair, step, head = at // (2 * some), (at // some) % 2, at % some
        column = (pair * some + head) * HD
        out_ref[step, :, column:column + HD] = sum_ref[
            pl.ds(at, block, stride=2 * HEADS), :
        ].astype(jnp.bfloat16)


def add_new(probs, o, keys, flat, vals):
    rows = o.shape[0]
    block = min(16, rows)
    return pl.pallas_call(
        add_body,
        grid=(rows // block,),
        in_specs=[
            pl.BlockSpec((block, 2 * HEADS, 2 * KVH), lambda i: (i, 0, 0)),
            pl.BlockSpec((block, 2 * HEADS, HD), lambda i: (i, 0, 0)),
            pl.BlockSpec((2, block, KEYS), lambda i: (0, i, 0)),
            pl.BlockSpec((2, block, KEYS), lambda i: (0, i, 0)),
            pl.BlockSpec((2, block, KVH, HD), lambda i: (0, i, 0, 0)),
        ],
        out_specs=(
            pl.BlockSpec((2, block, HEADS * HD), lambda i: (0, i, 0)),
            pl.BlockSpec((2, block, 2 * KEYS), lambda i: (0, i, 0)),
        ),
        out_shape=(
            jax.ShapeDtypeStruct((2, rows, HEADS * HD), jnp.bfloat16),
            jax.ShapeDtypeStruct((2, rows, 2 * KEYS), jnp.bfloat16),
        ),
        scratch_shapes=[pltpu.VMEM((block * 2 * HEADS, HD), jnp.float32)],
        cost_estimate=LIGHT,
        compiler_params=pltpu.CompilerParams(vmem_limit_bytes=ATTEND_VMEM),
        name="add_new",
    )(*in_vmem(probs, o), keys, flat, vals)


def marker_body(*refs):
    del refs


def marker(flag, cost):
    any_spec = pl.BlockSpec(memory_space=pltpu.HBM)
    return pl.pallas_call(
        marker_body,
        in_specs=[any_spec],
        out_specs=any_spec,
        out_shape=FLAG,
        cost_estimate=cost,
        compiler_params=pltpu.CompilerParams(vmem_limit_bytes=1 << 20),
        name="marker",
    )(*in_hbm(flag))


def tie(*values):
    return lax.optimization_barrier(values)


def halves(terms):
    half = terms[0].shape[0] // 2
    return [
        sum(term[begin:begin + half].astype(jnp.float32) for term in terms).astype(jnp.bfloat16)
        for begin in (0, half)
    ]


def sum_of(terms):
    return sum(term.astype(jnp.float32) for term in terms).astype(jnp.bfloat16)


def cross(value, tensor, mask):
    return lax.ppermute(value, "tensor", [(i, i ^ mask) for i in range(tensor)])


def local(
    replicas,
    tensor,
    hidden,
    base_weight,
    delta_values,
    delta_scales,
    tenant_slot,
    seg_tenant,
    seg_length,
    queries,
    kv_cache,
    cache_length,
):
    def swap(value, mask):
        return lax.ppermute(value, "replica", [(i, i ^ mask) for i in range(replicas)])

    rows = hidden.shape[1]
    columns = base_weight.shape[1]
    shard_rows = rows // tensor
    half = columns // 2
    masks = [1 << i for i in range(tensor.bit_length() - 1)]
    flat = hidden.reshape(2 * rows, hidden.shape[2])
    piece = shard_rows // 4
    masks_far = list(range(2, replicas, 2))

    place = jnp.stack([lax.axis_index("replica") * SLOTS, lax.axis_index("tensor")]).astype(jnp.int32)
    far = [swap(flat, mask) for mask in masks_far]
    sibling = swap(flat, 1)
    meta = jnp.concatenate([seg_tenant, seg_length], axis=1)
    meta = jnp.concatenate([meta, swap(meta, 1)], axis=0)
    far_meta = [swap(meta, mask) for mask in masks_far]

    def cached(at, count, before, cost, flag):
        return attend_cache(
            cache_length, queries, kv_cache, at * piece, count * piece, before, cost, [flag]
        )

    own, *other, flag = delta_rows(
        place, tenant_slot, meta, flat, [sibling], delta_values, delta_scales, tensor, base_weight
    )
    back = [swap(part, 1) for part in other]
    flag = marker(flag, COVER)
    back, flag = tie(back, flag)
    sent, kept = halves([own, jnp.concatenate(back, axis=0)])
    sent, flag = tie(sent, flag)
    near = [kept, cross(sent, tensor, masks[0])]
    *done, flag = cached(0, 1, (), LIGHT, flag)
    far, far_meta, flag = tie(far, far_meta, flag)
    quarter = rows // 2
    theirs_in = [
        [swap(rows_in[at:at + quarter], 1) for at in range(0, 2 * rows, quarter)] for rows_in in far
    ]

    flying = []
    for mask, pair, far_rows, far_sibling in zip(masks_far, far_meta, far, theirs_in):
        for start in (0, half):
            if start == 0:
                mine, *theirs, flag, gathered, spread = delta_rows(
                    place, tenant_slot, pair, far_rows, far_sibling, delta_values, delta_scales,
                    tensor, None, start, half, [flag],
                )
            else:
                mine, *theirs, flag = more_delta_rows(
                    gathered, spread, delta_values, delta_scales, start, half, [flag]
                )
            back = [swap(part, 1) for part in theirs]
            if flying:
                flying[-1], flag = tie(flying[-1], flag)
                flying[-1] = swap(sum_of(flying[-1]), flying_mask)
                flag = marker(flag, COVER)
            else:
                near, flag = tie(near, flag)
                near = sum_of(near)
                flag = marker(flag, LIGHT)
            back, flag = tie(back, flag)
            sent, kept = halves([mine, jnp.concatenate(back, axis=0)])
            sent, flag = tie(sent, flag)
            flying.append([kept, cross(sent, tensor, masks[0])])
            flying_mask = mask

    *done, flag = cached(1, 2, done, LIGHT, flag)
    flying, flag = tie(flying, flag)
    last = sum_of(flying[-1])
    values = [[near[:, start:start + half], *flying[at::2]] for at, start in enumerate((0, half))]
    sent, kept = halves(values[0])
    last, sent, flag = tie(last, sent, flag)
    values[1][-1] = swap(last, flying_mask)
    values[0] = [kept, cross(sent, tensor, masks[1])]
    *done, flag = cached(3, 1, done, LIGHT, flag)
    values[1], done = tie(values[1], done)
    for mask in masks[1:]:
        sent, kept = halves(values[1])
        values[1] = [kept, cross(sent, tensor, mask)]
    values[0], sent = tie(values[0], sent)
    for mask in masks[2:]:
        sent, kept = halves(values[0])
        values[0] = [kept, cross(sent, tensor, mask)]

    def by_head(value):
        return value.astype(jnp.float32).reshape(2, shard_rows, KVH, HD)

    keys = sum_of(values[0]).reshape(2, shard_rows, half)
    probs, weighed = weigh_new(*done, by_head(keys))
    last, probs = tie(values[1], probs)
    vals = sum_of(last).reshape(2, shard_rows, half)
    attention, new_kv = add_new(probs, weighed, keys, vals, by_head(vals))
    return (new_kv, attention)


def solution(mesh):
    placed = (
        P(None, ("groups", "replica"), "tensor"),
        P("tensor", None),
        P(("groups", "replica"), "tensor", None),
        P(("groups", "replica"), "tensor", None),
        P(),
        P(("groups", "replica"), None),
        P(("groups", "replica"), None),
        P(None, ("groups", "replica", "tensor"), None),
        P(("groups", "replica", "tensor"), None, None),
        P(("groups", "replica", "tensor")),
    )
    return jax.shard_map(
        functools.partial(local, mesh.shape["replica"], mesh.shape["tensor"]),
        mesh=mesh,
        in_specs=placed,
        out_specs=(
            P(None, ("groups", "replica", "tensor"), None),
            P(None, ("groups", "replica", "tensor"), None),
        ),
        check_vma=False,
    )
```

```python
import functools
import math

import jax
import jax.numpy as jnp
from jax import lax
from jax.experimental import pallas as pl
from jax.experimental.pallas import tpu as pltpu
from jax.sharding import PartitionSpec as P

HEADS = 64
KVH = 8
HD = 128
GROUP = HEADS // KVH
KEYS = KVH * HD
BLOCK = 128
SEG_MOST = 40
SLOTS = 2
QUARTERS = 4
NEG = -1e30
LIGHT = pl.CostEstimate(flops=1, bytes_accessed=1, transcendentals=0)
FLAG = pltpu.HBM((8, 128), jnp.float32)
SMEM = pl.BlockSpec(memory_space=pltpu.SMEM)
VMEM = pl.BlockSpec(memory_space=pltpu.VMEM)
HBM = pl.BlockSpec(memory_space=pltpu.HBM)
KERNEL_VMEM = 28 * 1024 * 1024
COVER = pl.CostEstimate(flops=1 << 34, bytes_accessed=1 << 26, transcendentals=0)


def in_hbm(*values):
    return [pltpu.with_memory_space_constraint(value, pltpu.HBM) for value in values]


def in_vmem(*values):
    return [pltpu.with_memory_space_constraint(value, pltpu.VMEM) for value in values]


def scatter_order(me, tensor, steps, rows, shape, axis):
    out = lax.broadcasted_iota(jnp.int32, shape, axis) % (steps * rows)
    shard = rows // tensor
    turn = tensor - 1 - out // (steps * shard)
    bits = tensor.bit_length() - 1
    apart = jnp.zeros(shape, jnp.int32)
    for bit in range(bits):
        apart = apart | (((turn >> (bits - 1 - bit)) & 1) << bit)
    step = (out // shard) % steps
    return step * rows + (apart ^ me) * shard + out % shard


def row_positions(meta_refs, slot_ref, first, steps, rows, source, index):
    step = index // rows
    row = index % rows
    per_slot = 2 * steps * SEG_MOST
    place = jnp.full(index.shape, -1, jnp.int32)
    for src, meta_ref in enumerate(meta_refs):
        begin = jnp.int32(0)
        for seg in range(meta_ref.shape[1] // 2):
            slot = slot_ref[meta_ref[0, seg]] - first
            length = meta_ref[0, meta_ref.shape[1] // 2 + seg]
            end = begin + length
            held = jnp.logical_and(slot >= 0, slot < SLOTS)
            offset = jnp.where(held, slot * per_slot + src * steps * SEG_MOST - begin, -(1 << 20))
            inside = (source == src) & (row >= begin) & (row < end)
            place = jnp.where(inside, offset + step * SEG_MOST + row, place)
            begin = end
    return place


def place_rows(tensor, steps, rows, slot_ref, meta_refs):
    half = steps * rows
    taken = SLOTS * 2 * steps * SEG_MOST
    first, me = lax.axis_index("replica") * SLOTS, lax.axis_index("tensor")
    flat = lax.broadcasted_iota(jnp.int32, (1, 2 * half), 1)
    order = scatter_order(me, tensor, steps, rows, (1, 2 * half), 1)
    chosen = []
    for index in (flat % half, order):
        along = row_positions(meta_refs, slot_ref, first, steps, rows, flat // half, index)
        chosen.append(lax.broadcasted_iota(jnp.int32, (taken, 2 * half), 0) == along)
    picks = chosen[0].astype(jnp.bfloat16)
    scatter = chosen[1].astype(jnp.float32).T.astype(jnp.bfloat16)
    return picks, scatter, order[:, :half]


def gather_rows(picks, xa, xb):
    half = xa.shape[0]
    got = jnp.dot(picks[:, :half], xa, preferred_element_type=jnp.float32)
    got += jnp.dot(picks[:, half:], xb, preferred_element_type=jnp.float32)
    return got.astype(jnp.bfloat16)


def spread_products(xc_ref, scatter_ref, weight_ref, cols):
    per_slot = xc_ref.shape[0] // SLOTS
    parts = [
        jnp.dot(
            xc_ref[slot * per_slot:(slot + 1) * per_slot, :], weight_ref[slot, :, cols],
            preferred_element_type=jnp.float32,
        ).astype(jnp.bfloat16)
        for slot in range(SLOTS)
    ]
    return jnp.dot(
        scatter_ref[...], jnp.concatenate(parts, axis=0), preferred_element_type=jnp.float32
    )


def first_body(tensor, steps, rows, *refs):
    slot_ref, meta_a, meta_b, xa_hbm, xb_ref, val_hbm, sc_hbm, base_hbm = refs[:8]
    da_ref, *db_refs = refs[8:9 + QUARTERS]
    weight_ref, _, xa_ref, sc_ref, base_ref, xc_ref, scatter_ref, xo_ref, sems = refs[9 + QUARTERS:]
    half = steps * rows
    width, columns = base_ref.shape
    tile = min(512, columns)
    tiles = [slice(at, at + tile) for at in range(0, columns, tile)]

    def copy(source, target, at):
        started = pltpu.make_async_copy(source, target, sems.at[at])
        started.start()
        return started

    rows_here = copy(xa_hbm, xa_ref, 0)
    scales = copy(sc_hbm, sc_ref, 1)
    coming = [
        (
            copy(val_hbm.at[:, :, cols], weight_ref.at[:, :, cols], 2 + 2 * at),
            copy(base_hbm.at[:, cols], base_ref.at[:, cols], 3 + 2 * at),
        )
        for at, cols in enumerate(tiles)
    ]
    picks, scatter, order = place_rows(tensor, steps, rows, slot_ref, (meta_a, meta_b))
    scatter_ref[...] = scatter
    turned = lax.broadcasted_iota(jnp.int32, (half, half), 0) == order
    turned = turned.astype(jnp.float32).T.astype(jnp.bfloat16)
    rows_here.wait()
    xc_ref[...] = gather_rows(picks, xa_ref[...], xb_ref[...])
    xo_ref[...] = jnp.dot(
        turned, xa_ref[...], preferred_element_type=jnp.float32
    ).astype(jnp.bfloat16)
    scales.wait()
    for cols, (values, base) in zip(tiles, coming):
        values.wait()
        for slot in range(SLOTS):
            for b in range(width // BLOCK):
                held = slice(b * BLOCK, (b + 1) * BLOCK)
                weight_ref[slot, held, cols] = (
                    weight_ref[slot, held, cols] * sc_ref[slot, b:b + 1, cols]
                )
        spread = spread_products(xc_ref, scatter_ref, weight_ref, cols)
        base.wait()
        own = spread[:half] + jnp.dot(
            xo_ref[...], base_ref[:, cols], preferred_element_type=jnp.float32
        )
        da_ref[:, cols] = own.astype(da_ref.dtype)
        put_quarters(db_refs, spread[half:], cols)


def far_body(tensor, steps, rows, start, chunks, *refs):
    slot_ref, meta_a, meta_b, xa_ref = refs[:4]
    xb_refs = refs[4:4 + chunks]
    weight_ref = refs[4 + chunks]
    da_ref, *db_refs, _, xc_ref, scatter_ref = refs[-4 - QUARTERS:]
    picks, scatter, _ = place_rows(tensor, steps, rows, slot_ref, (meta_a, meta_b))
    scatter_ref[...] = scatter
    xb = jnp.concatenate([ref[...] for ref in xb_refs], axis=0)
    xc_ref[...] = gather_rows(picks, xa_ref[...], xb)
    far_columns(start, xc_ref, scatter_ref, weight_ref, da_ref, db_refs)


def more_body(start, xc_ref, scatter_ref, weight_ref, *refs):
    da_ref, *db_refs, _ = refs[-2 - QUARTERS:]
    far_columns(start, xc_ref, scatter_ref, weight_ref, da_ref, db_refs)


def far_columns(start, xc_ref, scatter_ref, weight_ref, da_ref, db_refs):
    half, columns = da_ref.shape
    tile = min(512, columns)
    for at in range(0, columns, tile):
        spread = spread_products(
            xc_ref, scatter_ref, weight_ref, slice(start + at, start + at + tile)
        )
        cols = slice(at, at + tile)
        da_ref[:, cols] = spread[:half].astype(da_ref.dtype)
        put_quarters(db_refs, spread[half:], cols)


def put_quarters(refs, value, cols):
    rows = value.shape[0] // QUARTERS
    for at, ref in enumerate(refs):
        ref[:, cols] = value[at * rows:(at + 1) * rows].astype(ref.dtype)


def sums_shapes(half, columns):
    quarter = pltpu.VMEM((half // QUARTERS, columns), jnp.bfloat16)
    return [pltpu.VMEM((half, columns), jnp.bfloat16)] + [quarter] * QUARTERS


def first_delta(slots, metas, xa, xb, values, scales, base, tensor):
    steps = 2
    half, width = xa.shape
    rows = half // steps
    columns = base.shape[1]
    taken = SLOTS * 2 * steps * SEG_MOST
    outs = [*sums_shapes(half, columns), pltpu.VMEM(values.shape, jnp.bfloat16), FLAG]
    return pl.pallas_call(
        functools.partial(first_body, tensor, steps, rows),
        in_specs=[SMEM, SMEM, SMEM, HBM, VMEM, HBM, HBM, HBM],
        out_specs=[VMEM] * (len(outs) - 1) + [HBM],
        out_shape=outs,
        scratch_shapes=[
            pltpu.VMEM(xa.shape, jnp.bfloat16),
            pltpu.VMEM(scales.shape, jnp.bfloat16),
            pltpu.VMEM(base.shape, jnp.bfloat16),
            pltpu.VMEM((taken, width), jnp.bfloat16),
            pltpu.VMEM((2 * half, taken), jnp.bfloat16),
            pltpu.VMEM(xa.shape, jnp.bfloat16),
            pltpu.SemaphoreType.DMA((2 + 2 * max(1, columns // 512),)),
        ],
        cost_estimate=LIGHT,
        compiler_params=pltpu.CompilerParams(vmem_limit_bytes=22 << 20),
        name="first_delta",
    )(*in_hbm(slots), *metas, *in_hbm(xa), *in_vmem(xb), *in_hbm(values, scales, base))


def far_delta(slots, metas, xa, xb, weights, tensor, start, columns, gates):
    steps = 2
    half, width = xa.shape
    taken = SLOTS * 2 * steps * SEG_MOST
    kept = [pltpu.VMEM((taken, width), jnp.bfloat16), pltpu.VMEM((2 * half, taken), jnp.bfloat16)]
    outs = [*sums_shapes(half, columns), FLAG, *kept]
    return pl.pallas_call(
        functools.partial(far_body, tensor, steps, half // steps, start, len(xb)),
        in_specs=[SMEM, SMEM, SMEM] + [VMEM] * (2 + len(xb)) + [HBM] * len(gates),
        out_specs=[VMEM] * (1 + QUARTERS) + [HBM, VMEM, VMEM],
        out_shape=outs,
        cost_estimate=LIGHT,
        compiler_params=pltpu.CompilerParams(vmem_limit_bytes=12 << 20),
        name="far_delta",
    )(*in_hbm(slots), *metas, *in_vmem(xa, *xb, weights), *in_hbm(*gates))


def more_delta(gathered, scatter, weights, start, columns, gates):
    outs = [*sums_shapes(scatter.shape[0] // 2, columns), FLAG]
    return pl.pallas_call(
        functools.partial(more_body, start),
        in_specs=[VMEM] * 3 + [HBM] * len(gates),
        out_specs=[VMEM] * (1 + QUARTERS) + [HBM],
        out_shape=outs,
        cost_estimate=LIGHT,
        compiler_params=pltpu.CompilerParams(vmem_limit_bytes=8 << 20),
        name="more_delta",
    )(*in_vmem(gathered, scatter, weights), *in_hbm(*gates))


def add_quarters_body(value_ref, *refs):
    quarters, halves_out = refs[:QUARTERS], refs[QUARTERS:]
    rows = value_ref.shape[0] // QUARTERS
    for at, quarter in enumerate(quarters):
        target = halves_out[2 * at // QUARTERS]
        begin = at * rows % target.shape[0]
        target[begin:begin + rows, :] = (
            value_ref[at * rows:(at + 1) * rows, :].astype(jnp.float32)
            + quarter[...].astype(jnp.float32)
        ).astype(jnp.bfloat16)


def add_quarters(value, quarters):
    half = pltpu.VMEM((value.shape[0] // 2, value.shape[1]), jnp.bfloat16)
    return pl.pallas_call(
        add_quarters_body,
        in_specs=[VMEM] * (1 + QUARTERS),
        out_specs=[VMEM] * 2,
        out_shape=[half] * 2,
        cost_estimate=LIGHT,
        compiler_params=pltpu.CompilerParams(vmem_limit_bytes=4 << 20),
        name="add_quarters",
    )(*in_vmem(value, *quarters))


def cut_body(value_ref, *refs):
    rows = refs[0].shape[0]
    for at, ref in enumerate(refs):
        ref[...] = value_ref[at * rows:(at + 1) * rows, :]


def cut(value):
    quarter = pltpu.VMEM((value.shape[0] // QUARTERS, value.shape[1]), value.dtype)
    return pl.pallas_call(
        cut_body,
        in_specs=[VMEM],
        out_specs=[VMEM] * QUARTERS,
        out_shape=[quarter] * QUARTERS,
        cost_estimate=LIGHT,
        compiler_params=pltpu.CompilerParams(vmem_limit_bytes=4 << 20),
        name="cut",
    )(*in_vmem(value))


def cache_body(start, count, len_ref, q_ref, kv_ref, *refs):
    o_ref, lse_ref, turned_ref, _, sorted_ref = refs[-5:]
    block = o_ref.shape[0]
    cached = kv_ref.shape[1]
    some = 4 * GROUP
    scale = 1.0 / math.sqrt(HD)

    @pl.when(pl.program_id(0) == 0)
    def _():
        low = start // q_ref.shape[1] * q_ref.shape[1]
        for at in range(2 * HEADS):
            pair, step, head = at // some, at // (some // 2) % 2, at % (some // 2)
            column = (pair * some // 2 + head) * HD
            value = q_ref[step, :, column:column + HD].astype(jnp.float32)
            value = value[start - low:start - low + count]
            if count > 1:
                sorted_ref[pl.ds(at, count, stride=2 * HEADS), :] = value
            else:
                sorted_ref[at:at + 1, :] = value

    position = lax.broadcasted_iota(jnp.int32, (cached, 2 * HEADS), 0)
    column = lax.broadcasted_iota(jnp.int32, (HD, 2 * HEADS), 1)
    heads = column // some * 2 + column // GROUP % 2
    first = (lax.broadcasted_iota(jnp.int32, (some, HD), 0) // GROUP) % 2 == 0
    probs = []
    for r in range(block):
        at = pl.multiple_of((pl.program_id(0) * block + r) * 2 * HEADS, 2 * HEADS)
        turned = sorted_ref[pl.ds(at, 2 * HEADS), :].astype(jnp.bfloat16).T
        turned_ref[r] = turned
        wide = jnp.concatenate(
            [jnp.where(heads == k, turned, jnp.zeros_like(turned)) for k in range(KVH)], axis=0
        )
        scores = scale * jnp.dot(kv_ref[r, :, :KEYS], wide, preferred_element_type=jnp.float32)
        length = len_ref[start + pl.program_id(0) * block + r]
        scores = jnp.where(position < length, scores, NEG)
        top = jnp.max(scores, axis=0, keepdims=True)
        expo = jnp.exp(scores - top)
        total = jnp.sum(expo, axis=0, keepdims=True)
        lse_ref[r] = top + jnp.log(total)
        probs.append((expo * (1.0 / total)).astype(jnp.bfloat16).T)
    for r in range(block):
        parts = []
        for p in range(KVH // 2):
            out = jnp.dot(
                probs[r][p * some:(p + 1) * some],
                kv_ref[r, :, KEYS + p * 2 * HD:KEYS + (p + 1) * 2 * HD],
                preferred_element_type=jnp.float32,
            )
            parts.append(jnp.where(first, out[:, :HD], out[:, HD:]))
        o_ref[r] = jnp.concatenate(parts, axis=0)


def attend_cache(lengths, queries, kv_cache, start, count, before, cost, gates):
    rows = queries.shape[1]
    cached, width = kv_cache.shape[1:]
    block = max(1, min(8, count // 2))
    skip = start // block
    together = 16 if rows % 16 == 0 else rows
    in_place = pl.BlockSpec(memory_space=pltpu.HBM)
    return pl.pallas_call(
        functools.partial(cache_body, start, count),
        grid=(count // block,),
        in_specs=[
            pl.BlockSpec(memory_space=pltpu.SMEM),
            pl.BlockSpec((2, together, queries.shape[2]), lambda i: (0, start // together, 0)),
            pl.BlockSpec((block, cached, width), lambda i: (i + skip, 0, 0)),
            *[in_place for _ in (*before, *gates)],
        ],
        out_specs=(
            pl.BlockSpec((block, 2 * HEADS, HD), lambda i: (i + skip, 0, 0)),
            pl.BlockSpec((block, 1, 2 * HEADS), lambda i: (i + skip, 0, 0)),
            pl.BlockSpec((block, HD, 2 * HEADS), lambda i: (i + skip, 0, 0)),
            in_place,
        ),
        out_shape=(
            pltpu.VMEM((rows, 2 * HEADS, HD), jnp.float32),
            pltpu.VMEM((rows, 1, 2 * HEADS), jnp.float32),
            pltpu.VMEM((rows, HD, 2 * HEADS), jnp.bfloat16),
            FLAG,
        ),
        scratch_shapes=[pltpu.VMEM((count * 2 * HEADS, HD), jnp.float32)],
        input_output_aliases={3 + i: i for i in range(len(before))},
        cost_estimate=cost,
        compiler_params=pltpu.CompilerParams(vmem_limit_bytes=22 << 20),
        name="attend_cache",
    )(lengths, *in_hbm(queries, kv_cache), *in_vmem(*before), *in_hbm(*gates))


def weigh_body(o_ref, lse_ref, turned_ref, keys_ref, prob_ref, out_ref):
    rows = o_ref.shape[0]
    block = min(8, rows)
    pairs = 2 * KVH
    shape = (pairs, 2 * HEADS)
    row = lax.broadcasted_iota(jnp.int32, shape, 0)
    col = lax.broadcasted_iota(jnp.int32, shape, 1)
    head = col // (4 * GROUP) * 2 + (col // GROUP) % 2
    step = (col // (2 * GROUP)) % 2
    live = (head == row % KVH) & (row // KVH <= step)
    scale = 1.0 / math.sqrt(HD)

    def some_rows(at, carry):
        for inner in range(block):
            r = at * block + inner
            keys = jnp.concatenate([keys_ref[s, r] for s in range(2)], axis=0).astype(jnp.bfloat16)
            scores = scale * jnp.dot(keys, turned_ref[r], preferred_element_type=jnp.float32)
            scores = jnp.where(live, scores, NEG)
            lse = lse_ref[r]
            top = jnp.maximum(jnp.max(scores, axis=0, keepdims=True), lse)
            expo = jnp.exp(scores - top)
            before = jnp.exp(lse - top)
            inverse = 1.0 / (before + jnp.sum(expo, axis=0, keepdims=True))
            shares = jnp.broadcast_to(before * inverse, shape)
            both = jnp.concatenate([expo * inverse, shares], axis=0).T
            prob_ref[r] = both[:, :pairs].astype(jnp.bfloat16)
            out_ref[r] = o_ref[r] * both[:, pairs:pairs + 1]
        return carry

    lax.fori_loop(0, rows // block, some_rows, 0)


def weigh_new(o, lse, turned, keys):
    rows = o.shape[0]
    return pl.pallas_call(
        weigh_body,
        in_specs=[VMEM] * 4,
        out_specs=[VMEM] * 2,
        out_shape=(
            pltpu.VMEM((rows, 2 * HEADS, 2 * KVH), jnp.bfloat16),
            pltpu.VMEM(o.shape, jnp.float32),
        ),
        cost_estimate=LIGHT,
        compiler_params=pltpu.CompilerParams(vmem_limit_bytes=8 << 20),
        name="weigh_new",
    )(*in_vmem(o, lse, turned, keys))


def add_body(prob_ref, o_ref, keys_ref, flat_ref, vals_ref, out_hbm, new_hbm, out_ref, sum_ref, sems):
    half = keys_ref.shape[2]
    rows = o_ref.shape[0]
    block = min(16, rows)
    some = 2 * GROUP
    copies = [
        pltpu.make_async_copy(keys_ref, new_hbm.at[:, :, :half], sems.at[0]),
        pltpu.make_async_copy(flat_ref, new_hbm.at[:, :, half:], sems.at[1]),
    ]
    for copy in copies:
        copy.start()
    for begin in range(0, rows, block):
        for r in range(block):
            vals = jnp.concatenate([vals_ref[s, begin + r] for s in range(2)], axis=0)
            sum_ref[r * 2 * HEADS:(r + 1) * 2 * HEADS, :] = o_ref[begin + r] + jnp.dot(
                prob_ref[begin + r], vals.astype(jnp.bfloat16), preferred_element_type=jnp.float32
            )
        for at in range(2 * HEADS):
            pair, step, head = at // (2 * some), (at // some) % 2, at % some
            column = (pair * some + head) * HD
            out_ref[step, begin:begin + block, column:column + HD] = sum_ref[
                pl.ds(at, block, stride=2 * HEADS), :
            ].astype(jnp.bfloat16)
        copies.append(
            pltpu.make_async_copy(
                out_ref.at[:, begin:begin + block, :], out_hbm.at[:, begin:begin + block, :],
                sems.at[2 + begin // block],
            )
        )
        copies[-1].start()
    for copy in copies:
        copy.wait()


def add_new(probs, o, keys, flat, vals):
    rows = o.shape[0]
    block = min(16, rows)
    return pl.pallas_call(
        add_body,
        in_specs=[VMEM] * 5,
        out_specs=[HBM, HBM],
        out_shape=(
            jax.ShapeDtypeStruct((2, rows, HEADS * HD), jnp.bfloat16),
            jax.ShapeDtypeStruct((2, rows, 2 * KEYS), jnp.bfloat16),
        ),
        scratch_shapes=[
            pltpu.VMEM((2, rows, HEADS * HD), jnp.bfloat16),
            pltpu.VMEM((block * 2 * HEADS, HD), jnp.float32),
            pltpu.SemaphoreType.DMA((2 + rows // block,)),
        ],
        cost_estimate=LIGHT,
        compiler_params=pltpu.CompilerParams(vmem_limit_bytes=12 << 20),
        name="add_new",
    )(*in_vmem(probs, o, keys, flat, vals))


def marker_body(*refs):
    del refs


def marker(flag, cost):
    any_spec = pl.BlockSpec(memory_space=pltpu.HBM)
    return pl.pallas_call(
        marker_body,
        in_specs=[any_spec],
        out_specs=any_spec,
        out_shape=FLAG,
        cost_estimate=cost,
        compiler_params=pltpu.CompilerParams(vmem_limit_bytes=1 << 20),
        name="marker",
    )(*in_hbm(flag))


def tie(*values):
    return lax.optimization_barrier(values)


def halves(terms):
    half = terms[0].shape[0] // 2
    return [
        sum(term[begin:begin + half].astype(jnp.float32) for term in terms).astype(jnp.bfloat16)
        for begin in (0, half)
    ]


def sum_of(terms):
    return sum(term.astype(jnp.float32) for term in terms).astype(jnp.bfloat16)


def cross(value, tensor, mask):
    return lax.ppermute(value, "tensor", [(i, i ^ mask) for i in range(tensor)])


def local(
    replicas,
    tensor,
    hidden,
    base_weight,
    delta_values,
    delta_scales,
    tenant_slot,
    seg_tenant,
    seg_length,
    queries,
    kv_cache,
    cache_length,
):
    def swap(value, mask):
        return lax.ppermute(value, "replica", [(i, i ^ mask) for i in range(replicas)])

    rows = hidden.shape[1]
    columns = base_weight.shape[1]
    shard_rows = rows // tensor
    half = columns // 2
    masks = [1 << i for i in range(tensor.bit_length() - 1)]
    flat = hidden.reshape(2 * rows, hidden.shape[2])
    piece = shard_rows // 4
    masks_far = list(range(2, replicas, 2))

    far = [swap(flat, mask) for mask in masks_far]
    sibling = swap(flat, 1)
    meta = jnp.concatenate([seg_tenant, seg_length], axis=1)
    metas = [meta, *[swap(meta, mask) for mask in range(1, replicas)]]

    def cached(at, count, before, cost, flag):
        return attend_cache(
            cache_length, queries, kv_cache, at * piece, count * piece, before, cost, [flag]
        )

    own, *other, weights, flag = first_delta(
        tenant_slot, metas[:2], flat, sibling, delta_values, delta_scales, base_weight, tensor
    )
    back = [swap(part, 1) for part in other]
    flag = marker(flag, COVER)
    back, flag = tie(back, flag)
    sent, kept = add_quarters(own, back)
    sent, flag = tie(sent, flag)
    near = [kept, cross(sent, tensor, masks[0])]
    *done, flag = cached(0, 1, (), LIGHT, flag)
    far, far_metas, flag = tie(far, metas[2:], flag)
    theirs_in = [[swap(part, 1) for part in cut(rows_in)] for rows_in in far]

    flying = []
    for mask, far_rows, far_sibling in zip(masks_far, far, theirs_in):
        pair = far_metas[mask - 2:mask]
        for start in (0, half):
            if start == 0:
                mine, *theirs, flag, gathered, spread = far_delta(
                    tenant_slot, pair, far_rows, far_sibling, weights, tensor, start, half, [flag]
                )
            else:
                mine, *theirs, flag = more_delta(gathered, spread, weights, start, half, [flag])
            back = [swap(part, 1) for part in theirs]
            if flying:
                flying[-1], flag = tie(flying[-1], flag)
                flying[-1] = swap(sum_of(flying[-1]), flying_mask)
                flag = marker(flag, COVER)
            else:
                near, flag = tie(near, flag)
                near = sum_of(near)
                flag = marker(flag, LIGHT)
            back, flag = tie(back, flag)
            sent, kept = add_quarters(mine, back)
            sent, flag = tie(sent, flag)
            flying.append([kept, cross(sent, tensor, masks[0])])
            flying_mask = mask

    *done, flag = cached(2, 2, done, LIGHT, flag)
    flying, flag = tie(flying, flag)
    last = sum_of(flying[-1])
    values = [[near[:, start:start + half], *flying[at::2]] for at, start in enumerate((0, half))]
    sent, kept = halves(values[0])
    last, sent, flag = tie(last, sent, flag)
    values[1][-1] = swap(last, flying_mask)
    values[0] = [kept, cross(sent, tensor, masks[1])]
    *done, flag = cached(1, 1, done, LIGHT, flag)
    values[1], done = tie(values[1], done)
    for mask in masks[1:]:
        sent, kept = halves(values[1])
        values[1] = [kept, cross(sent, tensor, mask)]
    values[0], sent = tie(values[0], sent)
    for mask in masks[2:]:
        sent, kept = halves(values[0])
        values[0] = [kept, cross(sent, tensor, mask)]

    def by_head(value):
        return value.astype(jnp.float32).reshape(2, shard_rows, KVH, HD)

    keys = sum_of(values[0]).reshape(2, shard_rows, half)
    probs, weighed = weigh_new(*done, by_head(keys))
    last, probs = tie(values[1], probs)
    vals = sum_of(last).reshape(2, shard_rows, half)
    attention, new_kv = add_new(probs, weighed, keys, vals, by_head(vals))
    return (new_kv, attention)


def solution(mesh):
    placed = (
        P(None, ("groups", "replica"), "tensor"),
        P("tensor", None),
        P(("groups", "replica"), "tensor", None),
        P(("groups", "replica"), "tensor", None),
        P(),
        P(("groups", "replica"), None),
        P(("groups", "replica"), None),
        P(None, ("groups", "replica", "tensor"), None),
        P(("groups", "replica", "tensor"), None, None),
        P(("groups", "replica", "tensor")),
    )
    return jax.shard_map(
        functools.partial(local, mesh.shape["replica"], mesh.shape["tensor"]),
        mesh=mesh,
        in_specs=placed,
        out_specs=(
            P(None, ("groups", "replica", "tensor"), None),
            P(None, ("groups", "replica", "tensor"), None),
        ),
        check_vma=False,
    )
```

```python
import functools
import math

import jax
import jax.numpy as jnp
from jax import lax
from jax.experimental import pallas as pl
from jax.experimental.pallas import tpu as pltpu
from jax.sharding import PartitionSpec as P

HEADS = 64
KVH = 8
HD = 128
GROUP = HEADS // KVH
KEYS = KVH * HD
BLOCK = 128
SEG_MOST = 40
SLOTS = 2
QUARTERS = 4
NEG = -1e30
LIGHT = pl.CostEstimate(flops=1, bytes_accessed=1, transcendentals=0)
FLAG = pltpu.HBM((8, 128), jnp.float32)
SMEM = pl.BlockSpec(memory_space=pltpu.SMEM)
VMEM = pl.BlockSpec(memory_space=pltpu.VMEM)
HBM = pl.BlockSpec(memory_space=pltpu.HBM)
KERNEL_VMEM = 28 * 1024 * 1024
COVER = pl.CostEstimate(flops=1 << 34, bytes_accessed=1 << 26, transcendentals=0)


def in_hbm(*values):
    return [pltpu.with_memory_space_constraint(value, pltpu.HBM) for value in values]


def in_vmem(*values):
    return [pltpu.with_memory_space_constraint(value, pltpu.VMEM) for value in values]


def scatter_order(me, tensor, steps, rows, shape, axis):
    out = lax.broadcasted_iota(jnp.int32, shape, axis) % (steps * rows)
    shard = rows // tensor
    turn = tensor - 1 - out // (steps * shard)
    bits = tensor.bit_length() - 1
    apart = jnp.zeros(shape, jnp.int32)
    for bit in range(bits):
        apart = apart | (((turn >> (bits - 1 - bit)) & 1) << bit)
    step = (out // shard) % steps
    return step * rows + (apart ^ me) * shard + out % shard


def row_positions(meta_refs, slot_ref, first, steps, rows, source, index):
    step = index // rows
    row = index % rows
    per_slot = 2 * steps * SEG_MOST
    place = jnp.full(index.shape, -1, jnp.int32)
    for src, meta_ref in enumerate(meta_refs):
        begin = jnp.int32(0)
        for seg in range(meta_ref.shape[1] // 2):
            slot = slot_ref[meta_ref[0, seg]] - first
            length = meta_ref[0, meta_ref.shape[1] // 2 + seg]
            end = begin + length
            held = jnp.logical_and(slot >= 0, slot < SLOTS)
            offset = jnp.where(held, slot * per_slot + src * steps * SEG_MOST - begin, -(1 << 20))
            inside = (source == src) & (row >= begin) & (row < end)
            place = jnp.where(inside, offset + step * SEG_MOST + row, place)
            begin = end
    return place


def place_rows(tensor, steps, rows, slot_ref, meta_refs):
    half = steps * rows
    taken = SLOTS * 2 * steps * SEG_MOST
    first, me = lax.axis_index("replica") * SLOTS, lax.axis_index("tensor")
    flat = lax.broadcasted_iota(jnp.int32, (1, 2 * half), 1)
    order = scatter_order(me, tensor, steps, rows, (1, 2 * half), 1)
    chosen = []
    for index in (flat % half, order):
        along = row_positions(meta_refs, slot_ref, first, steps, rows, flat // half, index)
        chosen.append(lax.broadcasted_iota(jnp.int32, (taken, 2 * half), 0) == along)
    picks = chosen[0].astype(jnp.bfloat16)
    scatter = chosen[1].astype(jnp.float32).T.astype(jnp.bfloat16)
    return picks, scatter, order[:, :half]


def gather_rows(picks, xa, xb):
    half = xa.shape[0]
    got = jnp.dot(picks[:, :half], xa, preferred_element_type=jnp.float32)
    got += jnp.dot(picks[:, half:], xb, preferred_element_type=jnp.float32)
    return got.astype(jnp.bfloat16)


def spread_products(xc_ref, scatter_ref, weight_ref, cols):
    per_slot = xc_ref.shape[0] // SLOTS
    parts = [
        jnp.dot(
            xc_ref[slot * per_slot:(slot + 1) * per_slot, :], weight_ref[slot, :, cols],
            preferred_element_type=jnp.float32,
        ).astype(jnp.bfloat16)
        for slot in range(SLOTS)
    ]
    return jnp.dot(
        scatter_ref[...], jnp.concatenate(parts, axis=0), preferred_element_type=jnp.float32
    )


def first_body(tensor, steps, rows, *refs):
    slot_ref, meta_a, meta_b, xa_hbm, xb_ref, val_hbm, sc_hbm, base_hbm = refs[:8]
    da_ref, *db_refs = refs[8:9 + QUARTERS]
    weight_ref, _, xa_ref, sc_ref, base_ref, xc_ref, scatter_ref, xo_ref, sems = refs[9 + QUARTERS:]
    half = steps * rows
    width, columns = base_ref.shape
    tile = min(512, columns)
    tiles = [slice(at, at + tile) for at in range(0, columns, tile)]

    def copy(source, target, at):
        started = pltpu.make_async_copy(source, target, sems.at[at])
        started.start()
        return started

    rows_here = copy(xa_hbm, xa_ref, 0)
    scales = copy(sc_hbm, sc_ref, 1)
    coming = [
        (
            copy(val_hbm.at[:, :, cols], weight_ref.at[:, :, cols], 2 + 2 * at),
            copy(base_hbm.at[:, cols], base_ref.at[:, cols], 3 + 2 * at),
        )
        for at, cols in enumerate(tiles)
    ]
    picks, scatter, order = place_rows(tensor, steps, rows, slot_ref, (meta_a, meta_b))
    scatter_ref[...] = scatter
    turned = lax.broadcasted_iota(jnp.int32, (half, half), 0) == order
    turned = turned.astype(jnp.float32).T.astype(jnp.bfloat16)
    rows_here.wait()
    xc_ref[...] = gather_rows(picks, xa_ref[...], xb_ref[...])
    xo_ref[...] = jnp.dot(
        turned, xa_ref[...], preferred_element_type=jnp.float32
    ).astype(jnp.bfloat16)
    scales.wait()
    for cols, (values, base) in zip(tiles, coming):
        values.wait()
        for slot in range(SLOTS):
            for b in range(width // BLOCK):
                held = slice(b * BLOCK, (b + 1) * BLOCK)
                weight_ref[slot, held, cols] = (
                    weight_ref[slot, held, cols] * sc_ref[slot, b:b + 1, cols]
                )
        spread = spread_products(xc_ref, scatter_ref, weight_ref, cols)
        base.wait()
        own = spread[:half] + jnp.dot(
            xo_ref[...], base_ref[:, cols], preferred_element_type=jnp.float32
        )
        da_ref[:, cols] = own.astype(da_ref.dtype)
        put_quarters(db_refs, spread[half:], cols)


def far_body(tensor, steps, rows, start, chunks, *refs):
    slot_ref, meta_a, meta_b, xa_ref = refs[:4]
    xb_refs = refs[4:4 + chunks]
    weight_ref = refs[4 + chunks]
    da_ref, *db_refs, _, xc_ref, scatter_ref = refs[-4 - QUARTERS:]
    picks, scatter, _ = place_rows(tensor, steps, rows, slot_ref, (meta_a, meta_b))
    scatter_ref[...] = scatter
    xb = jnp.concatenate([ref[...] for ref in xb_refs], axis=0)
    xc_ref[...] = gather_rows(picks, xa_ref[...], xb)
    far_columns(start, xc_ref, scatter_ref, weight_ref, da_ref, db_refs)


def more_body(start, xc_ref, scatter_ref, weight_ref, *refs):
    da_ref, *db_refs, _ = refs[-2 - QUARTERS:]
    far_columns(start, xc_ref, scatter_ref, weight_ref, da_ref, db_refs)


def far_columns(start, xc_ref, scatter_ref, weight_ref, da_ref, db_refs):
    half, columns = da_ref.shape
    tile = min(512, columns)
    for at in range(0, columns, tile):
        spread = spread_products(
            xc_ref, scatter_ref, weight_ref, slice(start + at, start + at + tile)
        )
        cols = slice(at, at + tile)
        da_ref[:, cols] = spread[:half].astype(da_ref.dtype)
        put_quarters(db_refs, spread[half:], cols)


def put_quarters(refs, value, cols):
    rows = value.shape[0] // QUARTERS
    for at, ref in enumerate(refs):
        ref[:, cols] = value[at * rows:(at + 1) * rows].astype(ref.dtype)


def sums_shapes(half, columns):
    quarter = pltpu.VMEM((half // QUARTERS, columns), jnp.bfloat16)
    return [pltpu.VMEM((half, columns), jnp.bfloat16)] + [quarter] * QUARTERS


def first_delta(slots, metas, xa, xb, values, scales, base, tensor):
    steps = 2
    half, width = xa.shape
    rows = half // steps
    columns = base.shape[1]
    taken = SLOTS * 2 * steps * SEG_MOST
    outs = [*sums_shapes(half, columns), pltpu.VMEM(values.shape, jnp.bfloat16), FLAG]
    return pl.pallas_call(
        functools.partial(first_body, tensor, steps, rows),
        in_specs=[SMEM, SMEM, SMEM, HBM, VMEM, HBM, HBM, HBM],
        out_specs=[VMEM] * (len(outs) - 1) + [HBM],
        out_shape=outs,
        scratch_shapes=[
            pltpu.VMEM(xa.shape, jnp.bfloat16),
            pltpu.VMEM(scales.shape, jnp.bfloat16),
            pltpu.VMEM(base.shape, jnp.bfloat16),
            pltpu.VMEM((taken, width), jnp.bfloat16),
            pltpu.VMEM((2 * half, taken), jnp.bfloat16),
            pltpu.VMEM(xa.shape, jnp.bfloat16),
            pltpu.SemaphoreType.DMA((2 + 2 * max(1, columns // 512),)),
        ],
        cost_estimate=LIGHT,
        compiler_params=pltpu.CompilerParams(vmem_limit_bytes=22 << 20),
        name="first_delta",
    )(*in_hbm(slots), *metas, *in_hbm(xa), *in_vmem(xb), *in_hbm(values, scales, base))


def far_delta(slots, metas, xa, xb, weights, tensor, start, columns, gates):
    steps = 2
    half, width = xa.shape
    taken = SLOTS * 2 * steps * SEG_MOST
    kept = [pltpu.VMEM((taken, width), jnp.bfloat16), pltpu.VMEM((2 * half, taken), jnp.bfloat16)]
    outs = [*sums_shapes(half, columns), FLAG, *kept]
    return pl.pallas_call(
        functools.partial(far_body, tensor, steps, half // steps, start, len(xb)),
        in_specs=[SMEM, SMEM, SMEM] + [VMEM] * (2 + len(xb)) + [HBM] * len(gates),
        out_specs=[VMEM] * (1 + QUARTERS) + [HBM, VMEM, VMEM],
        out_shape=outs,
        cost_estimate=LIGHT,
        compiler_params=pltpu.CompilerParams(vmem_limit_bytes=12 << 20),
        name="far_delta",
    )(*in_hbm(slots), *metas, *in_vmem(xa, *xb, weights), *in_hbm(*gates))


def more_delta(gathered, scatter, weights, start, columns, gates):
    outs = [*sums_shapes(scatter.shape[0] // 2, columns), FLAG]
    return pl.pallas_call(
        functools.partial(more_body, start),
        in_specs=[VMEM] * 3 + [HBM] * len(gates),
        out_specs=[VMEM] * (1 + QUARTERS) + [HBM],
        out_shape=outs,
        cost_estimate=LIGHT,
        compiler_params=pltpu.CompilerParams(vmem_limit_bytes=8 << 20),
        name="more_delta",
    )(*in_vmem(gathered, scatter, weights), *in_hbm(*gates))


def add_quarters_body(value_ref, *refs):
    quarters, halves_out = refs[:QUARTERS], refs[QUARTERS:]
    rows = value_ref.shape[0] // QUARTERS
    for at, quarter in enumerate(quarters):
        target = halves_out[2 * at // QUARTERS]
        begin = at * rows % target.shape[0]
        target[begin:begin + rows, :] = (
            value_ref[at * rows:(at + 1) * rows, :].astype(jnp.float32)
            + quarter[...].astype(jnp.float32)
        ).astype(jnp.bfloat16)


def add_quarters(value, quarters):
    half = pltpu.VMEM((value.shape[0] // 2, value.shape[1]), jnp.bfloat16)
    return pl.pallas_call(
        add_quarters_body,
        in_specs=[VMEM] * (1 + QUARTERS),
        out_specs=[VMEM] * 2,
        out_shape=[half] * 2,
        cost_estimate=LIGHT,
        compiler_params=pltpu.CompilerParams(vmem_limit_bytes=4 << 20),
        name="add_quarters",
    )(*in_vmem(value, *quarters))


def cut_body(value_ref, *refs):
    rows = refs[0].shape[0]
    for at, ref in enumerate(refs):
        ref[...] = value_ref[at * rows:(at + 1) * rows, :]


def cut(value):
    quarter = pltpu.VMEM((value.shape[0] // QUARTERS, value.shape[1]), value.dtype)
    return pl.pallas_call(
        cut_body,
        in_specs=[VMEM],
        out_specs=[VMEM] * QUARTERS,
        out_shape=[quarter] * QUARTERS,
        cost_estimate=LIGHT,
        compiler_params=pltpu.CompilerParams(vmem_limit_bytes=4 << 20),
        name="cut",
    )(*in_vmem(value))


def cache_body(start, count, len_ref, q_ref, kv_ref, *refs):
    o_ref, lse_ref, turned_ref, _, sorted_ref = refs[-5:]
    block = o_ref.shape[0]
    cached = kv_ref.shape[1]
    some = 4 * GROUP
    scale = 1.0 / math.sqrt(HD)

    @pl.when(pl.program_id(0) == 0)
    def _():
        low = start // q_ref.shape[1] * q_ref.shape[1]
        for at in range(2 * HEADS):
            pair, step, head = at // some, at // (some // 2) % 2, at % (some // 2)
            column = (pair * some // 2 + head) * HD
            value = q_ref[step, :, column:column + HD].astype(jnp.float32)
            value = value[start - low:start - low + count]
            if count > 1:
                sorted_ref[pl.ds(at, count, stride=2 * HEADS), :] = value
            else:
                sorted_ref[at:at + 1, :] = value

    position = lax.broadcasted_iota(jnp.int32, (cached, 2 * HEADS), 0)
    column = lax.broadcasted_iota(jnp.int32, (HD, 2 * HEADS), 1)
    heads = column // some * 2 + column // GROUP % 2
    first = (lax.broadcasted_iota(jnp.int32, (some, HD), 0) // GROUP) % 2 == 0
    probs = []
    for r in range(block):
        at = pl.multiple_of((pl.program_id(0) * block + r) * 2 * HEADS, 2 * HEADS)
        turned = sorted_ref[pl.ds(at, 2 * HEADS), :].astype(jnp.bfloat16).T
        turned_ref[r] = turned
        wide = jnp.concatenate(
            [jnp.where(heads == k, turned, jnp.zeros_like(turned)) for k in range(KVH)], axis=0
        )
        scores = scale * jnp.dot(kv_ref[r, :, :KEYS], wide, preferred_element_type=jnp.float32)
        length = len_ref[start + pl.program_id(0) * block + r]
        scores = jnp.where(position < length, scores, NEG)
        top = jnp.max(scores, axis=0, keepdims=True)
        expo = jnp.exp(scores - top)
        total = jnp.sum(expo, axis=0, keepdims=True)
        lse_ref[r] = top + jnp.log(total)
        probs.append((expo * (1.0 / total)).astype(jnp.bfloat16).T)
    for r in range(block):
        parts = []
        for p in range(KVH // 2):
            out = jnp.dot(
                probs[r][p * some:(p + 1) * some],
                kv_ref[r, :, KEYS + p * 2 * HD:KEYS + (p + 1) * 2 * HD],
                preferred_element_type=jnp.float32,
            )
            parts.append(jnp.where(first, out[:, :HD], out[:, HD:]))
        o_ref[r] = jnp.concatenate(parts, axis=0)


def attend_cache(lengths, queries, kv_cache, start, count, before, cost, gates):
    rows = queries.shape[1]
    cached, width = kv_cache.shape[1:]
    block = max(1, min(8, count // 2))
    skip = start // block
    together = 16 if rows % 16 == 0 else rows
    in_place = pl.BlockSpec(memory_space=pltpu.HBM)
    return pl.pallas_call(
        functools.partial(cache_body, start, count),
        grid=(count // block,),
        in_specs=[
            pl.BlockSpec(memory_space=pltpu.SMEM),
            pl.BlockSpec((2, together, queries.shape[2]), lambda i: (0, start // together, 0)),
            pl.BlockSpec((block, cached, width), lambda i: (i + skip, 0, 0)),
            *[in_place for _ in (*before, *gates)],
        ],
        out_specs=(
            pl.BlockSpec((block, 2 * HEADS, HD), lambda i: (i + skip, 0, 0)),
            pl.BlockSpec((block, 1, 2 * HEADS), lambda i: (i + skip, 0, 0)),
            pl.BlockSpec((block, HD, 2 * HEADS), lambda i: (i + skip, 0, 0)),
            in_place,
        ),
        out_shape=(
            pltpu.VMEM((rows, 2 * HEADS, HD), jnp.float32),
            pltpu.VMEM((rows, 1, 2 * HEADS), jnp.float32),
            pltpu.VMEM((rows, HD, 2 * HEADS), jnp.bfloat16),
            FLAG,
        ),
        scratch_shapes=[pltpu.VMEM((count * 2 * HEADS, HD), jnp.float32)],
        input_output_aliases={3 + i: i for i in range(len(before))},
        cost_estimate=cost,
        compiler_params=pltpu.CompilerParams(vmem_limit_bytes=22 << 20),
        name="attend_cache",
    )(lengths, *in_hbm(queries, kv_cache), *in_vmem(*before), *in_hbm(*gates))


def weigh_body(lse_ref, turned_ref, keys_ref, o_ref, share_ref, early_ref):
    rows = lse_ref.shape[0]
    block = min(8, rows)
    shape = (2 * KVH, 2 * HEADS)
    row = lax.broadcasted_iota(jnp.int32, shape, 0)
    col = lax.broadcasted_iota(jnp.int32, shape, 1)
    head = col // (4 * GROUP) * 2 + (col // GROUP) % 2
    step = (col // (2 * GROUP)) % 2
    live = (head == row % KVH) & (row // KVH <= step)
    scale = 1.0 / math.sqrt(HD)

    def some_rows(at, carry):
        for inner in range(block):
            r = at * block + inner
            keys = jnp.concatenate([keys_ref[s, r] for s in range(2)], axis=0).astype(jnp.bfloat16)
            scores = scale * jnp.dot(keys, turned_ref[r], preferred_element_type=jnp.float32)
            scores = jnp.where(live, scores, NEG)
            lse = lse_ref[r]
            top = jnp.maximum(jnp.max(scores, axis=0, keepdims=True), lse)
            expo = jnp.exp(scores - top)
            before = jnp.exp(lse - top)
            parts = [jnp.sum(expo[s * KVH:(s + 1) * KVH], axis=0, keepdims=True) for s in range(2)]
            inverse = 1.0 / (before + parts[0] + parts[1])
            for place, part in enumerate((before, *parts)):
                share_ref[place, pl.ds(r, 1), :] = part * inverse
        return carry

    lax.fori_loop(0, rows // block, some_rows, 0)
    some = 4 * GROUP

    def one_pair(pair, carry):
        back = (2 * HEADS - some * pair) % (2 * HEADS)
        share = pltpu.roll(share_ref[0], back, 1)
        for inner in range(some):
            value = o_ref[pl.ds(pair * some + inner, rows, stride=2 * HEADS), :]
            column = pl.multiple_of((pair * (some // 2) + inner % (some // 2)) * HD, HD)
            early_ref[inner // (some // 2), :, pl.ds(column, HD)] = value * share[:, inner:inner + 1]
        return carry

    lax.fori_loop(0, KVH // 2, one_pair, 0)


def weigh_new(lse, turned, keys, o):
    rows = o.shape[0]
    return pl.pallas_call(
        weigh_body,
        in_specs=[VMEM] * 4,
        out_specs=[VMEM] * 2,
        out_shape=(
            pltpu.VMEM((3, rows, 2 * HEADS), jnp.float32),
            pltpu.VMEM((2, rows, HEADS * HD), jnp.float32),
        ),
        cost_estimate=LIGHT,
        compiler_params=pltpu.CompilerParams(vmem_limit_bytes=8 << 20),
        name="weigh_new",
    )(*in_vmem(lse, turned, keys, o.reshape(rows * 2 * HEADS, HD)))


def add_body(share_ref, early_ref, keys_ref, vals_ref, out_hbm, new_hbm, out_ref, sems):
    half = keys_ref.shape[2]
    rows = keys_ref.shape[1]
    some = 4 * GROUP
    wide = some // 2 * HD

    def piece(pair):
        cols = pl.ds(pl.multiple_of(pair * wide, wide), wide)
        return pltpu.make_async_copy(
            out_ref.at[:, :, cols], out_hbm.at[:, :, cols], sems.at[2 + pair]
        )

    first = pltpu.make_async_copy(keys_ref, new_hbm.at[:, :, :half], sems.at[0])
    second = pltpu.make_async_copy(vals_ref, new_hbm.at[:, :, half:], sems.at[1])
    first.start()
    second.start()

    def one_pair(pair, carry):
        back = (2 * HEADS - some * pair) % (2 * HEADS)
        shares = [pltpu.roll(share_ref[1 + s], back, 1) for s in range(2)]
        for head in range(2):
            at = pl.multiple_of((2 * pair + head) * HD, HD)
            vals = [vals_ref[s, :, pl.ds(at, HD)].astype(jnp.float32) for s in range(2)]
            for step in range(2):
                for member in range(GROUP):
                    inner = step * some // 2 + head * GROUP + member
                    column = pl.multiple_of(pair * wide + (head * GROUP + member) * HD, HD)
                    value = early_ref[step, :, pl.ds(column, HD)]
                    for s in range(step + 1):
                        value = value + vals[s] * shares[s][:, inner:inner + 1]
                    out_ref[step, :, pl.ds(column, HD)] = value.astype(jnp.bfloat16)
        piece(pair).start()
        return carry

    lax.fori_loop(0, KVH // 2, one_pair, 0)
    for pair in range(KVH // 2):
        piece(pair).wait()
    first.wait()
    second.wait()


def add_new(shares, early, keys, vals):
    rows = keys.shape[1]
    return pl.pallas_call(
        add_body,
        in_specs=[VMEM] * 4,
        out_specs=[HBM, HBM],
        out_shape=(
            jax.ShapeDtypeStruct((2, rows, HEADS * HD), jnp.bfloat16),
            jax.ShapeDtypeStruct((2, rows, 2 * KEYS), jnp.bfloat16),
        ),
        scratch_shapes=[
            pltpu.VMEM((2, rows, HEADS * HD), jnp.bfloat16),
            pltpu.SemaphoreType.DMA((2 + KVH // 2,)),
        ],
        cost_estimate=LIGHT,
        compiler_params=pltpu.CompilerParams(vmem_limit_bytes=12 << 20),
        name="add_new",
    )(*in_vmem(shares, early, keys, vals))


def marker_body(*refs):
    del refs


def marker(flag, cost):
    any_spec = pl.BlockSpec(memory_space=pltpu.HBM)
    return pl.pallas_call(
        marker_body,
        in_specs=[any_spec],
        out_specs=any_spec,
        out_shape=FLAG,
        cost_estimate=cost,
        compiler_params=pltpu.CompilerParams(vmem_limit_bytes=1 << 20),
        name="marker",
    )(*in_hbm(flag))


def tie(*values):
    return lax.optimization_barrier(values)


def halves(terms):
    half = terms[0].shape[0] // 2
    return [
        sum(term[begin:begin + half].astype(jnp.float32) for term in terms).astype(jnp.bfloat16)
        for begin in (0, half)
    ]


def sum_of(terms):
    return sum(term.astype(jnp.float32) for term in terms).astype(jnp.bfloat16)


def cross(value, tensor, mask):
    return lax.ppermute(value, "tensor", [(i, i ^ mask) for i in range(tensor)])


def local(
    replicas,
    tensor,
    hidden,
    base_weight,
    delta_values,
    delta_scales,
    tenant_slot,
    seg_tenant,
    seg_length,
    queries,
    kv_cache,
    cache_length,
):
    def swap(value, mask):
        return lax.ppermute(value, "replica", [(i, i ^ mask) for i in range(replicas)])

    rows = hidden.shape[1]
    columns = base_weight.shape[1]
    shard_rows = rows // tensor
    half = columns // 2
    masks = [1 << i for i in range(tensor.bit_length() - 1)]
    flat = hidden.reshape(2 * rows, hidden.shape[2])
    piece = shard_rows // 4
    masks_far = list(range(2, replicas, 2))

    far = [swap(flat, mask) for mask in masks_far]
    sibling = swap(flat, 1)
    meta = jnp.concatenate([seg_tenant, seg_length], axis=1)
    metas = [meta, *[swap(meta, mask) for mask in range(1, replicas)]]

    def cached(at, count, before, cost, flag):
        return attend_cache(
            cache_length, queries, kv_cache, at * piece, count * piece, before, cost, [flag]
        )

    own, *other, weights, flag = first_delta(
        tenant_slot, metas[:2], flat, sibling, delta_values, delta_scales, base_weight, tensor
    )
    back = [swap(part, 1) for part in other]
    flag = marker(flag, COVER)
    back, flag = tie(back, flag)
    sent, kept = add_quarters(own, back)
    sent, flag = tie(sent, flag)
    near = [kept, cross(sent, tensor, masks[0])]
    *done, flag = cached(0, 1, (), LIGHT, flag)
    far, far_metas, flag = tie(far, metas[2:], flag)
    theirs_in = [[swap(part, 1) for part in cut(rows_in)] for rows_in in far]

    flying = []
    for mask, far_rows, far_sibling in zip(masks_far, far, theirs_in):
        pair = far_metas[mask - 2:mask]
        for start in (0, half):
            if start == 0:
                mine, *theirs, flag, gathered, spread = far_delta(
                    tenant_slot, pair, far_rows, far_sibling, weights, tensor, start, half, [flag]
                )
            else:
                mine, *theirs, flag = more_delta(gathered, spread, weights, start, half, [flag])
            back = [swap(part, 1) for part in theirs]
            if not flying:
                near, flag = tie(near, flag)
                near = sum_of(near)
            flag = marker(flag, LIGHT)
            back, flag = tie(back, flag)
            sent, kept = add_quarters(mine, back)
            sent, flag = tie(sent, flag)
            flying.append([kept, cross(sent, tensor, masks[0])])
            if len(flying) > 1:
                flying[-2], flag = tie(flying[-2], flag)
                early, flag = tie(sum_of(flying[-2]), flag)
                flying[-2] = swap(early, flying_mask)
            flying_mask = mask

    *done, flag = cached(2, 2, done, LIGHT, flag)
    flying[-1], flag = tie(flying[-1], flag)
    last, flag = tie(sum_of(flying[-1]), flag)
    flying[-1] = swap(last, flying_mask)
    flying[:-1], flag = tie(flying[:-1], flag)
    values = [[near[:, start:start + half], *flying[at::2]] for at, start in enumerate((0, half))]
    sent, kept = halves(values[0])
    sent, flag = tie(sent, flag)
    values[0] = [kept, cross(sent, tensor, masks[1])]
    *done, flag = cached(1, 1, done, LIGHT, flag)
    values[1], done = tie(values[1], done)
    for mask in masks[1:]:
        sent, kept = halves(values[1])
        values[1] = [kept, cross(sent, tensor, mask)]
    values[0], sent = tie(values[0], sent)
    for mask in masks[2:]:
        sent, kept = halves(values[0])
        values[0] = [kept, cross(sent, tensor, mask)]

    def by_head(value):
        return value.astype(jnp.float32).reshape(2, shard_rows, KVH, HD)

    keys = sum_of(values[0]).reshape(2, shard_rows, half)
    o, lse, turned = done
    shares, early = weigh_new(lse, turned, by_head(keys), o)
    last, shares = tie(values[1], shares)
    vals = sum_of(last).reshape(2, shard_rows, half)
    attention, new_kv = add_new(shares, early, keys, vals)
    return (new_kv, attention)


def solution(mesh):
    placed = (
        P(None, ("groups", "replica"), "tensor"),
        P("tensor", None),
        P(("groups", "replica"), "tensor", None),
        P(("groups", "replica"), "tensor", None),
        P(),
        P(("groups", "replica"), None),
        P(("groups", "replica"), None),
        P(None, ("groups", "replica", "tensor"), None),
        P(("groups", "replica", "tensor"), None, None),
        P(("groups", "replica", "tensor")),
    )
    return jax.shard_map(
        functools.partial(local, mesh.shape["replica"], mesh.shape["tensor"]),
        mesh=mesh,
        in_specs=placed,
        out_specs=(
            P(None, ("groups", "replica", "tensor"), None),
            P(None, ("groups", "replica", "tensor"), None),
        ),
        check_vma=False,
    )
```

```python
import functools
import math

import jax
import jax.numpy as jnp
from jax import lax
from jax.experimental import pallas as pl
from jax.experimental.pallas import tpu as pltpu
from jax.sharding import PartitionSpec as P

HEADS = 64
KVH = 8
HD = 128
GROUP = HEADS // KVH
KEYS = KVH * HD
BLOCK = 128
SEG_MOST = 40
SLOTS = 2
QUARTERS = 4
NEG = -1e30
LIGHT = pl.CostEstimate(flops=1, bytes_accessed=1, transcendentals=0)
FLAG = pltpu.HBM((8, 128), jnp.float32)
SMEM = pl.BlockSpec(memory_space=pltpu.SMEM)
VMEM = pl.BlockSpec(memory_space=pltpu.VMEM)
HBM = pl.BlockSpec(memory_space=pltpu.HBM)
KERNEL_VMEM = 28 * 1024 * 1024
COVER = pl.CostEstimate(flops=1 << 34, bytes_accessed=1 << 26, transcendentals=0)


def in_hbm(*values):
    return [pltpu.with_memory_space_constraint(value, pltpu.HBM) for value in values]


def in_vmem(*values):
    return [pltpu.with_memory_space_constraint(value, pltpu.VMEM) for value in values]


def scatter_order(me, tensor, steps, rows, shape, axis):
    out = lax.broadcasted_iota(jnp.int32, shape, axis) % (steps * rows)
    shard = rows // tensor
    turn = tensor - 1 - out // (steps * shard)
    bits = tensor.bit_length() - 1
    apart = jnp.zeros(shape, jnp.int32)
    for bit in range(bits):
        apart = apart | (((turn >> (bits - 1 - bit)) & 1) << bit)
    step = (out // shard) % steps
    return step * rows + (apart ^ me) * shard + out % shard


def row_positions(meta_refs, slot_ref, first, steps, rows, source, index):
    step = index // rows
    row = index % rows
    per_slot = 2 * steps * SEG_MOST
    place = jnp.full(index.shape, -1, jnp.int32)
    for src, meta_ref in enumerate(meta_refs):
        begin = jnp.int32(0)
        for seg in range(meta_ref.shape[1] // 2):
            slot = slot_ref[meta_ref[0, seg]] - first
            length = meta_ref[0, meta_ref.shape[1] // 2 + seg]
            end = begin + length
            held = jnp.logical_and(slot >= 0, slot < SLOTS)
            offset = jnp.where(held, slot * per_slot + src * steps * SEG_MOST - begin, -(1 << 20))
            inside = (source == src) & (row >= begin) & (row < end)
            place = jnp.where(inside, offset + step * SEG_MOST + row, place)
            begin = end
    return place


def place_rows(tensor, steps, rows, slot_ref, meta_refs):
    half = steps * rows
    taken = SLOTS * 2 * steps * SEG_MOST
    first, me = lax.axis_index("replica") * SLOTS, lax.axis_index("tensor")
    flat = lax.broadcasted_iota(jnp.int32, (1, 2 * half), 1)
    order = scatter_order(me, tensor, steps, rows, (1, 2 * half), 1)
    chosen = []
    for index in (flat % half, order):
        along = row_positions(meta_refs, slot_ref, first, steps, rows, flat // half, index)
        chosen.append(lax.broadcasted_iota(jnp.int32, (taken, 2 * half), 0) == along)
    picks = chosen[0].astype(jnp.bfloat16)
    scatter = chosen[1].astype(jnp.float32).T.astype(jnp.bfloat16)
    return picks, scatter, order[:, :half]


def gather_rows(picks, xa, xb):
    half = xa.shape[0]
    got = jnp.dot(picks[:, :half], xa, preferred_element_type=jnp.float32)
    got += jnp.dot(picks[:, half:], xb, preferred_element_type=jnp.float32)
    return got.astype(jnp.bfloat16)


def spread_products(xc_ref, scatter_ref, weight_ref, cols):
    per_slot = xc_ref.shape[0] // SLOTS
    parts = [
        jnp.dot(
            xc_ref[slot * per_slot:(slot + 1) * per_slot, :], weight_ref[slot, :, cols],
            preferred_element_type=jnp.float32,
        ).astype(jnp.bfloat16)
        for slot in range(SLOTS)
    ]
    return jnp.dot(
        scatter_ref[...], jnp.concatenate(parts, axis=0), preferred_element_type=jnp.float32
    )


def first_body(tensor, steps, rows, *refs):
    slot_ref, meta_a, meta_b, xa_hbm, xb_ref, val_hbm, sc_hbm, base_hbm = refs[:8]
    da_ref, *db_refs = refs[8:9 + QUARTERS]
    weight_ref, _, xa_ref, sc_ref, base_ref, xc_ref, scatter_ref, xo_ref, sems = refs[9 + QUARTERS:]
    half = steps * rows
    width, columns = base_ref.shape
    tile = min(512, columns)
    tiles = [slice(at, at + tile) for at in range(0, columns, tile)]

    def copy(source, target, at):
        started = pltpu.make_async_copy(source, target, sems.at[at])
        started.start()
        return started

    rows_here = copy(xa_hbm, xa_ref, 0)
    scales = copy(sc_hbm, sc_ref, 1)
    coming = [
        (
            copy(val_hbm.at[:, :, cols], weight_ref.at[:, :, cols], 2 + 2 * at),
            copy(base_hbm.at[:, cols], base_ref.at[:, cols], 3 + 2 * at),
        )
        for at, cols in enumerate(tiles)
    ]
    picks, scatter, order = place_rows(tensor, steps, rows, slot_ref, (meta_a, meta_b))
    scatter_ref[...] = scatter
    turned = lax.broadcasted_iota(jnp.int32, (half, half), 0) == order
    turned = turned.astype(jnp.float32).T.astype(jnp.bfloat16)
    rows_here.wait()
    xc_ref[...] = gather_rows(picks, xa_ref[...], xb_ref[...])
    xo_ref[...] = jnp.dot(
        turned, xa_ref[...], preferred_element_type=jnp.float32
    ).astype(jnp.bfloat16)
    scales.wait()
    for cols, (values, base) in zip(tiles, coming):
        values.wait()
        for slot in range(SLOTS):
            for b in range(width // BLOCK):
                held = slice(b * BLOCK, (b + 1) * BLOCK)
                weight_ref[slot, held, cols] = (
                    weight_ref[slot, held, cols] * sc_ref[slot, b:b + 1, cols]
                )
        spread = spread_products(xc_ref, scatter_ref, weight_ref, cols)
        base.wait()
        own = spread[:half] + jnp.dot(
            xo_ref[...], base_ref[:, cols], preferred_element_type=jnp.float32
        )
        da_ref[:, cols] = own.astype(da_ref.dtype)
        put_quarters(db_refs, spread[half:], cols)


def ready_body(tensor, steps, rows, slot_ref, meta_a, meta_b, xa_ref, *refs):
    got_ref, picks_ref, scatter_ref = refs[-3:]
    picks, scatter, _ = place_rows(tensor, steps, rows, slot_ref, (meta_a, meta_b))
    half = steps * rows
    scatter_ref[...] = scatter
    picks_ref[...] = picks[:, half:]
    got_ref[...] = jnp.dot(
        picks[:, :half], xa_ref[...], preferred_element_type=jnp.float32
    ).astype(jnp.bfloat16)


def far_body(start, chunks, *refs):
    got_ref, picks_ref, scatter_ref = refs[:3]
    xb_refs = refs[3:3 + chunks]
    weight_ref = refs[3 + chunks]
    da_ref, *db_refs, _, xc_ref = refs[-3 - QUARTERS:]
    xb = jnp.concatenate([ref[...] for ref in xb_refs], axis=0)
    more = jnp.dot(picks_ref[...], xb, preferred_element_type=jnp.float32)
    xc_ref[...] = (got_ref[...].astype(jnp.float32) + more).astype(jnp.bfloat16)
    far_columns(start, xc_ref, scatter_ref, weight_ref, da_ref, db_refs)


def more_body(start, xc_ref, scatter_ref, weight_ref, *refs):
    da_ref, *db_refs, _ = refs[-2 - QUARTERS:]
    far_columns(start, xc_ref, scatter_ref, weight_ref, da_ref, db_refs)


def far_columns(start, xc_ref, scatter_ref, weight_ref, da_ref, db_refs):
    half, columns = da_ref.shape
    tile = min(512, columns)
    for at in range(0, columns, tile):
        spread = spread_products(
            xc_ref, scatter_ref, weight_ref, slice(start + at, start + at + tile)
        )
        cols = slice(at, at + tile)
        da_ref[:, cols] = spread[:half].astype(da_ref.dtype)
        put_quarters(db_refs, spread[half:], cols)


def put_quarters(refs, value, cols):
    rows = value.shape[0] // QUARTERS
    for at, ref in enumerate(refs):
        ref[:, cols] = value[at * rows:(at + 1) * rows].astype(ref.dtype)


def sums_shapes(half, columns):
    quarter = pltpu.VMEM((half // QUARTERS, columns), jnp.bfloat16)
    return [pltpu.VMEM((half, columns), jnp.bfloat16)] + [quarter] * QUARTERS


def first_delta(slots, metas, xa, xb, values, scales, base, tensor):
    steps = 2
    half, width = xa.shape
    rows = half // steps
    columns = base.shape[1]
    taken = SLOTS * 2 * steps * SEG_MOST
    outs = [*sums_shapes(half, columns), pltpu.VMEM(values.shape, jnp.bfloat16), FLAG]
    return pl.pallas_call(
        functools.partial(first_body, tensor, steps, rows),
        in_specs=[SMEM, SMEM, SMEM, HBM, VMEM, HBM, HBM, HBM],
        out_specs=[VMEM] * (len(outs) - 1) + [HBM],
        out_shape=outs,
        scratch_shapes=[
            pltpu.VMEM(xa.shape, jnp.bfloat16),
            pltpu.VMEM(scales.shape, jnp.bfloat16),
            pltpu.VMEM(base.shape, jnp.bfloat16),
            pltpu.VMEM((taken, width), jnp.bfloat16),
            pltpu.VMEM((2 * half, taken), jnp.bfloat16),
            pltpu.VMEM(xa.shape, jnp.bfloat16),
            pltpu.SemaphoreType.DMA((2 + 2 * max(1, columns // 512),)),
        ],
        cost_estimate=LIGHT,
        compiler_params=pltpu.CompilerParams(vmem_limit_bytes=22 << 20),
        name="first_delta",
    )(*in_hbm(slots), *metas, *in_hbm(xa), *in_vmem(xb), *in_hbm(values, scales, base))


def far_ready(slots, metas, xa, tensor, gates):
    steps = 2
    half, width = xa.shape
    taken = SLOTS * 2 * steps * SEG_MOST
    return pl.pallas_call(
        functools.partial(ready_body, tensor, steps, half // steps),
        in_specs=[SMEM, SMEM, SMEM, VMEM] + [HBM] * len(gates),
        out_specs=[VMEM] * 3,
        out_shape=[
            pltpu.VMEM((taken, width), jnp.bfloat16),
            pltpu.VMEM((taken, half), jnp.bfloat16),
            pltpu.VMEM((2 * half, taken), jnp.bfloat16),
        ],
        cost_estimate=LIGHT,
        compiler_params=pltpu.CompilerParams(vmem_limit_bytes=12 << 20),
        name="far_ready",
    )(*in_hbm(slots), *metas, *in_vmem(xa), *in_hbm(*gates))


def far_delta(ready, xb, weights, start, columns, gates):
    got, picks, scatter = ready
    outs = [*sums_shapes(picks.shape[1], columns), FLAG, pltpu.VMEM(got.shape, jnp.bfloat16)]
    return pl.pallas_call(
        functools.partial(far_body, start, len(xb)),
        in_specs=[VMEM] * (4 + len(xb)) + [HBM] * len(gates),
        out_specs=[VMEM] * (1 + QUARTERS) + [HBM, VMEM],
        out_shape=outs,
        cost_estimate=LIGHT,
        compiler_params=pltpu.CompilerParams(vmem_limit_bytes=12 << 20),
        name="far_delta",
    )(*in_vmem(got, picks, scatter, *xb, weights), *in_hbm(*gates))


def more_delta(gathered, scatter, weights, start, columns, gates):
    outs = [*sums_shapes(scatter.shape[0] // 2, columns), FLAG]
    return pl.pallas_call(
        functools.partial(more_body, start),
        in_specs=[VMEM] * 3 + [HBM] * len(gates),
        out_specs=[VMEM] * (1 + QUARTERS) + [HBM],
        out_shape=outs,
        cost_estimate=LIGHT,
        compiler_params=pltpu.CompilerParams(vmem_limit_bytes=8 << 20),
        name="more_delta",
    )(*in_vmem(gathered, scatter, weights), *in_hbm(*gates))


def add_quarters_body(value_ref, *refs):
    quarters, halves_out = refs[:QUARTERS], refs[QUARTERS:]
    rows = value_ref.shape[0] // QUARTERS
    for at, quarter in enumerate(quarters):
        target = halves_out[2 * at // QUARTERS]
        begin = at * rows % target.shape[0]
        target[begin:begin + rows, :] = (
            value_ref[at * rows:(at + 1) * rows, :].astype(jnp.float32)
            + quarter[...].astype(jnp.float32)
        ).astype(jnp.bfloat16)


def add_quarters(value, quarters):
    half = pltpu.VMEM((value.shape[0] // 2, value.shape[1]), jnp.bfloat16)
    return pl.pallas_call(
        add_quarters_body,
        in_specs=[VMEM] * (1 + QUARTERS),
        out_specs=[VMEM] * 2,
        out_shape=[half] * 2,
        cost_estimate=LIGHT,
        compiler_params=pltpu.CompilerParams(vmem_limit_bytes=4 << 20),
        name="add_quarters",
    )(*in_vmem(value, *quarters))


def cut_body(value_ref, *refs):
    rows = refs[0].shape[0]
    for at, ref in enumerate(refs):
        ref[...] = value_ref[at * rows:(at + 1) * rows, :]


def cut(value):
    quarter = pltpu.VMEM((value.shape[0] // QUARTERS, value.shape[1]), value.dtype)
    return pl.pallas_call(
        cut_body,
        in_specs=[VMEM],
        out_specs=[VMEM] * QUARTERS,
        out_shape=[quarter] * QUARTERS,
        cost_estimate=LIGHT,
        compiler_params=pltpu.CompilerParams(vmem_limit_bytes=4 << 20),
        name="cut",
    )(*in_vmem(value))


def cache_body(start, count, len_ref, q_ref, kv_ref, *refs):
    o_ref, lse_ref, turned_ref, _, sorted_ref = refs[-5:]
    block = o_ref.shape[0]
    cached = kv_ref.shape[1]
    some = 4 * GROUP
    scale = 1.0 / math.sqrt(HD)

    @pl.when(pl.program_id(0) == 0)
    def _():
        low = start // q_ref.shape[1] * q_ref.shape[1]
        for at in range(2 * HEADS):
            pair, step, head = at // some, at // (some // 2) % 2, at % (some // 2)
            column = (pair * some // 2 + head) * HD
            value = q_ref[step, :, column:column + HD].astype(jnp.float32)
            value = value[start - low:start - low + count]
            if count > 1:
                sorted_ref[pl.ds(at, count, stride=2 * HEADS), :] = value
            else:
                sorted_ref[at:at + 1, :] = value

    position = lax.broadcasted_iota(jnp.int32, (cached, 2 * HEADS), 0)
    column = lax.broadcasted_iota(jnp.int32, (HD, 2 * HEADS), 1)
    heads = column // some * 2 + column // GROUP % 2
    first = (lax.broadcasted_iota(jnp.int32, (some, HD), 0) // GROUP) % 2 == 0
    probs = []
    for r in range(block):
        at = pl.multiple_of((pl.program_id(0) * block + r) * 2 * HEADS, 2 * HEADS)
        turned = sorted_ref[pl.ds(at, 2 * HEADS), :].astype(jnp.bfloat16).T
        turned_ref[r] = turned
        wide = jnp.concatenate(
            [jnp.where(heads == k, turned, jnp.zeros_like(turned)) for k in range(KVH)], axis=0
        )
        scores = scale * jnp.dot(kv_ref[r, :, :KEYS], wide, preferred_element_type=jnp.float32)
        length = len_ref[start + pl.program_id(0) * block + r]
        scores = jnp.where(position < length, scores, NEG)
        top = jnp.max(scores, axis=0, keepdims=True)
        expo = jnp.exp(scores - top)
        total = jnp.sum(expo, axis=0, keepdims=True)
        lse_ref[r] = top + jnp.log(total)
        probs.append((expo * (1.0 / total)).astype(jnp.bfloat16).T)
    for r in range(block):
        parts = []
        for p in range(KVH // 2):
            out = jnp.dot(
                probs[r][p * some:(p + 1) * some],
                kv_ref[r, :, KEYS + p * 2 * HD:KEYS + (p + 1) * 2 * HD],
                preferred_element_type=jnp.float32,
            )
            parts.append(jnp.where(first, out[:, :HD], out[:, HD:]))
        o_ref[r] = jnp.concatenate(parts, axis=0)


def attend_cache(lengths, queries, kv_cache, start, count, before, cost, gates):
    rows = queries.shape[1]
    cached, width = kv_cache.shape[1:]
    block = max(1, min(8, count // 2))
    skip = start // block
    together = 16 if rows % 16 == 0 else rows
    in_place = pl.BlockSpec(memory_space=pltpu.HBM)
    return pl.pallas_call(
        functools.partial(cache_body, start, count),
        grid=(count // block,),
        in_specs=[
            pl.BlockSpec(memory_space=pltpu.SMEM),
            pl.BlockSpec((2, together, queries.shape[2]), lambda i: (0, start // together, 0)),
            pl.BlockSpec((block, cached, width), lambda i: (i + skip, 0, 0)),
            *[in_place for _ in (*before, *gates)],
        ],
        out_specs=(
            pl.BlockSpec((block, 2 * HEADS, HD), lambda i: (i + skip, 0, 0)),
            pl.BlockSpec((block, 1, 2 * HEADS), lambda i: (i + skip, 0, 0)),
            pl.BlockSpec((block, HD, 2 * HEADS), lambda i: (i + skip, 0, 0)),
            in_place,
        ),
        out_shape=(
            pltpu.VMEM((rows, 2 * HEADS, HD), jnp.float32),
            pltpu.VMEM((rows, 1, 2 * HEADS), jnp.float32),
            pltpu.VMEM((rows, HD, 2 * HEADS), jnp.bfloat16),
            FLAG,
        ),
        scratch_shapes=[pltpu.VMEM((count * 2 * HEADS, HD), jnp.float32)],
        input_output_aliases={3 + i: i for i in range(len(before))},
        cost_estimate=cost,
        compiler_params=pltpu.CompilerParams(vmem_limit_bytes=22 << 20),
        name="attend_cache",
    )(lengths, *in_hbm(queries, kv_cache), *in_vmem(*before), *in_hbm(*gates))


def weigh_body(lse_ref, turned_ref, keys_ref, o_ref, share_ref, early_ref):
    rows = lse_ref.shape[0]
    block = min(8, rows)
    shape = (2 * KVH, 2 * HEADS)
    row = lax.broadcasted_iota(jnp.int32, shape, 0)
    col = lax.broadcasted_iota(jnp.int32, shape, 1)
    head = col // (4 * GROUP) * 2 + (col // GROUP) % 2
    step = (col // (2 * GROUP)) % 2
    live = (head == row % KVH) & (row // KVH <= step)
    scale = 1.0 / math.sqrt(HD)

    def some_rows(at, carry):
        for inner in range(block):
            r = at * block + inner
            keys = jnp.concatenate([keys_ref[s, r] for s in range(2)], axis=0).astype(jnp.bfloat16)
            scores = scale * jnp.dot(keys, turned_ref[r], preferred_element_type=jnp.float32)
            scores = jnp.where(live, scores, NEG)
            lse = lse_ref[r]
            top = jnp.maximum(jnp.max(scores, axis=0, keepdims=True), lse)
            expo = jnp.exp(scores - top)
            before = jnp.exp(lse - top)
            parts = [jnp.sum(expo[s * KVH:(s + 1) * KVH], axis=0, keepdims=True) for s in range(2)]
            inverse = 1.0 / (before + parts[0] + parts[1])
            for place, part in enumerate((before, *parts)):
                share_ref[place, pl.ds(r, 1), :] = part * inverse
        return carry

    lax.fori_loop(0, rows // block, some_rows, 0)
    some = 4 * GROUP

    def one_pair(pair, carry):
        back = (2 * HEADS - some * pair) % (2 * HEADS)
        share = pltpu.roll(share_ref[0], back, 1)
        for inner in range(some):
            value = o_ref[pl.ds(pair * some + inner, rows, stride=2 * HEADS), :]
            column = pl.multiple_of((pair * (some // 2) + inner % (some // 2)) * HD, HD)
            early_ref[inner // (some // 2), :, pl.ds(column, HD)] = value * share[:, inner:inner + 1]
        return carry

    lax.fori_loop(0, KVH // 2, one_pair, 0)


def weigh_new(lse, turned, keys, o):
    rows = o.shape[0]
    return pl.pallas_call(
        weigh_body,
        in_specs=[VMEM] * 4,
        out_specs=[VMEM] * 2,
        out_shape=(
            pltpu.VMEM((3, rows, 2 * HEADS), jnp.float32),
            pltpu.VMEM((2, rows, HEADS * HD), jnp.float32),
        ),
        cost_estimate=LIGHT,
        compiler_params=pltpu.CompilerParams(vmem_limit_bytes=8 << 20),
        name="weigh_new",
    )(*in_vmem(lse, turned, keys, o.reshape(rows * 2 * HEADS, HD)))


def add_body(share_ref, early_ref, keys_ref, vals_ref, out_hbm, new_hbm, out_ref, sems):
    half = keys_ref.shape[2]
    rows = keys_ref.shape[1]
    some = 4 * GROUP
    wide = some // 2 * HD

    def piece(pair):
        cols = pl.ds(pl.multiple_of(pair * wide, wide), wide)
        return pltpu.make_async_copy(
            out_ref.at[:, :, cols], out_hbm.at[:, :, cols], sems.at[2 + pair]
        )

    first = pltpu.make_async_copy(keys_ref, new_hbm.at[:, :, :half], sems.at[0])
    second = pltpu.make_async_copy(vals_ref, new_hbm.at[:, :, half:], sems.at[1])
    first.start()
    second.start()

    def one_pair(pair, carry):
        back = (2 * HEADS - some * pair) % (2 * HEADS)
        shares = [pltpu.roll(share_ref[1 + s], back, 1) for s in range(2)]
        for head in range(2):
            at = pl.multiple_of((2 * pair + head) * HD, HD)
            vals = [vals_ref[s, :, pl.ds(at, HD)].astype(jnp.float32) for s in range(2)]
            for step in range(2):
                for member in range(GROUP):
                    inner = step * some // 2 + head * GROUP + member
                    column = pl.multiple_of(pair * wide + (head * GROUP + member) * HD, HD)
                    value = early_ref[step, :, pl.ds(column, HD)]
                    for s in range(step + 1):
                        value = value + vals[s] * shares[s][:, inner:inner + 1]
                    out_ref[step, :, pl.ds(column, HD)] = value.astype(jnp.bfloat16)
        piece(pair).start()
        return carry

    lax.fori_loop(0, KVH // 2, one_pair, 0)
    for pair in range(KVH // 2):
        piece(pair).wait()
    first.wait()
    second.wait()


def add_new(shares, early, keys, vals):
    rows = keys.shape[1]
    return pl.pallas_call(
        add_body,
        in_specs=[VMEM] * 4,
        out_specs=[HBM, HBM],
        out_shape=(
            jax.ShapeDtypeStruct((2, rows, HEADS * HD), jnp.bfloat16),
            jax.ShapeDtypeStruct((2, rows, 2 * KEYS), jnp.bfloat16),
        ),
        scratch_shapes=[
            pltpu.VMEM((2, rows, HEADS * HD), jnp.bfloat16),
            pltpu.SemaphoreType.DMA((2 + KVH // 2,)),
        ],
        cost_estimate=LIGHT,
        compiler_params=pltpu.CompilerParams(vmem_limit_bytes=12 << 20),
        name="add_new",
    )(*in_vmem(shares, early, keys, vals))


def marker_body(*refs):
    del refs


def marker(flag, cost):
    any_spec = pl.BlockSpec(memory_space=pltpu.HBM)
    return pl.pallas_call(
        marker_body,
        in_specs=[any_spec],
        out_specs=any_spec,
        out_shape=FLAG,
        cost_estimate=cost,
        compiler_params=pltpu.CompilerParams(vmem_limit_bytes=1 << 20),
        name="marker",
    )(*in_hbm(flag))


def tie(*values):
    return lax.optimization_barrier(values)


def halves(terms):
    half = terms[0].shape[0] // 2
    return [
        sum(term[begin:begin + half].astype(jnp.float32) for term in terms).astype(jnp.bfloat16)
        for begin in (0, half)
    ]


def sum_of(terms):
    return sum(term.astype(jnp.float32) for term in terms).astype(jnp.bfloat16)


def cross(value, tensor, mask):
    return lax.ppermute(value, "tensor", [(i, i ^ mask) for i in range(tensor)])


def local(
    replicas,
    tensor,
    hidden,
    base_weight,
    delta_values,
    delta_scales,
    tenant_slot,
    seg_tenant,
    seg_length,
    queries,
    kv_cache,
    cache_length,
):
    def swap(value, mask):
        return lax.ppermute(value, "replica", [(i, i ^ mask) for i in range(replicas)])

    rows = hidden.shape[1]
    columns = base_weight.shape[1]
    shard_rows = rows // tensor
    half = columns // 2
    masks = [1 << i for i in range(tensor.bit_length() - 1)]
    flat = hidden.reshape(2 * rows, hidden.shape[2])
    piece = shard_rows // 4
    masks_far = list(range(2, replicas, 2))

    far = [swap(flat, mask) for mask in masks_far]
    sibling = swap(flat, 1)
    meta = jnp.concatenate([seg_tenant, seg_length], axis=1)
    metas = [meta, *[swap(meta, mask) for mask in range(1, replicas)]]

    def cached(at, count, before, cost, flag):
        return attend_cache(
            cache_length, queries, kv_cache, at * piece, count * piece, before, cost, [flag]
        )

    own, *other, weights, flag = first_delta(
        tenant_slot, metas[:2], flat, sibling, delta_values, delta_scales, base_weight, tensor
    )
    back = [swap(part, 1) for part in other]
    flag = marker(flag, COVER)
    back, flag = tie(back, flag)
    sent, kept = add_quarters(own, back)
    sent, flag = tie(sent, flag)
    near = [kept, cross(sent, tensor, masks[0])]
    *done, flag = cached(0, 1, (), LIGHT, flag)
    far, far_metas, flag = tie(far, metas[2:], flag)
    theirs_in = [[swap(part, 1) for part in cut(rows_in)] for rows_in in far]

    flying = []
    for mask, far_rows, far_sibling in zip(masks_far, far, theirs_in):
        pair = far_metas[mask - 2:mask]
        for start in (0, half):
            if start == 0:
                ready = far_ready(tenant_slot, pair, far_rows, tensor, [flag])
                spread = ready[2]
                mine, *theirs, flag, gathered = far_delta(
                    ready, far_sibling, weights, start, half, [flag]
                )
            else:
                mine, *theirs, flag = more_delta(gathered, spread, weights, start, half, [flag])
            back = [swap(part, 1) for part in theirs]
            if not flying:
                near, flag = tie(near, flag)
                near = sum_of(near)
            flag = marker(flag, LIGHT)
            back, flag = tie(back, flag)
            sent, kept = add_quarters(mine, back)
            sent, flag = tie(sent, flag)
            flying.append([kept, cross(sent, tensor, masks[0])])
            if len(flying) > 1:
                flying[-2], flag = tie(flying[-2], flag)
                early, flag = tie(sum_of(flying[-2]), flag)
                flying[-2] = swap(early, flying_mask)
            flying_mask = mask

    *done, flag = cached(2, 2, done, LIGHT, flag)
    flying[-1], flag = tie(flying[-1], flag)
    last, flag = tie(sum_of(flying[-1]), flag)
    flying[-1] = swap(last, flying_mask)
    flying[:-1], flag = tie(flying[:-1], flag)
    values = [[near[:, start:start + half], *flying[at::2]] for at, start in enumerate((0, half))]
    sent, kept = halves(values[0])
    sent, flag = tie(sent, flag)
    values[0] = [kept, cross(sent, tensor, masks[1])]
    *done, flag = cached(1, 1, done, LIGHT, flag)
    values[1], done = tie(values[1], done)
    for mask in masks[1:]:
        sent, kept = halves(values[1])
        values[1] = [kept, cross(sent, tensor, mask)]
    values[0], sent = tie(values[0], sent)
    for mask in masks[2:]:
        sent, kept = halves(values[0])
        values[0] = [kept, cross(sent, tensor, mask)]

    def by_head(value):
        return value.astype(jnp.float32).reshape(2, shard_rows, KVH, HD)

    keys = sum_of(values[0]).reshape(2, shard_rows, half)
    o, lse, turned = done
    shares, early = weigh_new(lse, turned, by_head(keys), o)
    last, shares = tie(values[1], shares)
    vals = sum_of(last).reshape(2, shard_rows, half)
    attention, new_kv = add_new(shares, early, keys, vals)
    return (new_kv, attention)


def solution(mesh):
    placed = (
        P(None, ("groups", "replica"), "tensor"),
        P("tensor", None),
        P(("groups", "replica"), "tensor", None),
        P(("groups", "replica"), "tensor", None),
        P(),
        P(("groups", "replica"), None),
        P(("groups", "replica"), None),
        P(None, ("groups", "replica", "tensor"), None),
        P(("groups", "replica", "tensor"), None, None),
        P(("groups", "replica", "tensor")),
    )
    return jax.shard_map(
        functools.partial(local, mesh.shape["replica"], mesh.shape["tensor"]),
        mesh=mesh,
        in_specs=placed,
        out_specs=(
            P(None, ("groups", "replica", "tensor"), None),
            P(None, ("groups", "replica", "tensor"), None),
        ),
        check_vma=False,
    )
```

```python
import functools
import math

import jax
import jax.numpy as jnp
from jax import lax
from jax.experimental import pallas as pl
from jax.experimental.pallas import tpu as pltpu
from jax.sharding import PartitionSpec as P

HEADS = 64
KVH = 8
HD = 128
GROUP = HEADS // KVH
KEYS = KVH * HD
BLOCK = 128
SEG_MOST = 40
SLOTS = 2
QUARTERS = 4
NEG = -1e30
LIGHT = pl.CostEstimate(flops=1, bytes_accessed=1, transcendentals=0)
FLAG = pltpu.HBM((8, 128), jnp.float32)
SMEM = pl.BlockSpec(memory_space=pltpu.SMEM)
VMEM = pl.BlockSpec(memory_space=pltpu.VMEM)
HBM = pl.BlockSpec(memory_space=pltpu.HBM)
KERNEL_VMEM = 28 * 1024 * 1024
COVER = pl.CostEstimate(flops=1 << 34, bytes_accessed=1 << 26, transcendentals=0)


def in_hbm(*values):
    return [pltpu.with_memory_space_constraint(value, pltpu.HBM) for value in values]


def in_vmem(*values):
    return [pltpu.with_memory_space_constraint(value, pltpu.VMEM) for value in values]


def scatter_order(me, tensor, steps, rows, shape, axis):
    out = lax.broadcasted_iota(jnp.int32, shape, axis) % (steps * rows)
    shard = rows // tensor
    turn = tensor - 1 - out // (steps * shard)
    bits = tensor.bit_length() - 1
    apart = jnp.zeros(shape, jnp.int32)
    for bit in range(bits):
        apart = apart | (((turn >> (bits - 1 - bit)) & 1) << bit)
    step = (out // shard) % steps
    return step * rows + (apart ^ me) * shard + out % shard


def row_positions(meta_refs, slot_ref, first, steps, rows, source, index):
    step = index // rows
    row = index % rows
    per_slot = 2 * steps * SEG_MOST
    place = jnp.full(index.shape, -1, jnp.int32)
    for src, meta_ref in enumerate(meta_refs):
        begin = jnp.int32(0)
        for seg in range(meta_ref.shape[1] // 2):
            slot = slot_ref[meta_ref[0, seg]] - first
            length = meta_ref[0, meta_ref.shape[1] // 2 + seg]
            end = begin + length
            held = jnp.logical_and(slot >= 0, slot < SLOTS)
            offset = jnp.where(held, slot * per_slot + src * steps * SEG_MOST - begin, -(1 << 20))
            inside = (source == src) & (row >= begin) & (row < end)
            place = jnp.where(inside, offset + step * SEG_MOST + row, place)
            begin = end
    return place


def place_rows(tensor, steps, rows, slot_ref, meta_refs):
    half = steps * rows
    taken = SLOTS * 2 * steps * SEG_MOST
    first, me = lax.axis_index("replica") * SLOTS, lax.axis_index("tensor")
    flat = lax.broadcasted_iota(jnp.int32, (1, 2 * half), 1)
    order = scatter_order(me, tensor, steps, rows, (1, 2 * half), 1)
    chosen = []
    for index in (flat % half, order):
        along = row_positions(meta_refs, slot_ref, first, steps, rows, flat // half, index)
        chosen.append(lax.broadcasted_iota(jnp.int32, (taken, 2 * half), 0) == along)
    picks = chosen[0].astype(jnp.bfloat16)
    scatter = chosen[1].astype(jnp.float32).T.astype(jnp.bfloat16)
    return picks, scatter, order[:, :half]


def gather_rows(picks, xa, xb):
    half = xa.shape[0]
    got = jnp.dot(picks[:, :half], xa, preferred_element_type=jnp.float32)
    got += jnp.dot(picks[:, half:], xb, preferred_element_type=jnp.float32)
    return got.astype(jnp.bfloat16)


def spread_products(xc_ref, scatter_ref, weight_ref, cols):
    per_slot = xc_ref.shape[0] // SLOTS
    parts = [
        jnp.dot(
            xc_ref[slot * per_slot:(slot + 1) * per_slot, :], weight_ref[slot, :, cols],
            preferred_element_type=jnp.float32,
        ).astype(jnp.bfloat16)
        for slot in range(SLOTS)
    ]
    return jnp.dot(
        scatter_ref[...], jnp.concatenate(parts, axis=0), preferred_element_type=jnp.float32
    )


def first_body(tensor, steps, rows, *refs):
    slot_ref, meta_a, meta_b, xa_hbm, xb_ref, val_hbm, sc_hbm, base_hbm = refs[:8]
    da_ref, *db_refs = refs[8:9 + QUARTERS]
    weight_ref, _, xa_ref, sc_ref, base_ref, xc_ref, scatter_ref, xo_ref, sems = refs[9 + QUARTERS:]
    half = steps * rows
    width, columns = base_ref.shape
    tile = min(512, columns)
    tiles = [slice(at, at + tile) for at in range(0, columns, tile)]

    def copy(source, target, at):
        started = pltpu.make_async_copy(source, target, sems.at[at])
        started.start()
        return started

    rows_here = copy(xa_hbm, xa_ref, 0)
    scales = copy(sc_hbm, sc_ref, 1)
    coming = [
        (
            copy(val_hbm.at[:, :, cols], weight_ref.at[:, :, cols], 2 + 2 * at),
            copy(base_hbm.at[:, cols], base_ref.at[:, cols], 3 + 2 * at),
        )
        for at, cols in enumerate(tiles)
    ]
    picks, scatter, order = place_rows(tensor, steps, rows, slot_ref, (meta_a, meta_b))
    scatter_ref[...] = scatter
    turned = lax.broadcasted_iota(jnp.int32, (half, half), 0) == order
    turned = turned.astype(jnp.float32).T.astype(jnp.bfloat16)
    rows_here.wait()
    xc_ref[...] = gather_rows(picks, xa_ref[...], xb_ref[...])
    xo_ref[...] = jnp.dot(
        turned, xa_ref[...], preferred_element_type=jnp.float32
    ).astype(jnp.bfloat16)
    scales.wait()
    for cols, (values, base) in zip(tiles, coming):
        values.wait()
        for slot in range(SLOTS):
            for b in range(width // BLOCK):
                held = slice(b * BLOCK, (b + 1) * BLOCK)
                weight_ref[slot, held, cols] = (
                    weight_ref[slot, held, cols] * sc_ref[slot, b:b + 1, cols]
                )
        spread = spread_products(xc_ref, scatter_ref, weight_ref, cols)
        base.wait()
        own = spread[:half] + jnp.dot(
            xo_ref[...], base_ref[:, cols], preferred_element_type=jnp.float32
        )
        da_ref[:, cols] = own.astype(da_ref.dtype)
        put_quarters(db_refs, spread[half:], cols)


def ready_body(tensor, steps, rows, slot_ref, meta_a, meta_b, xa_ref, *refs):
    got_ref, picks_ref, scatter_ref = refs[-3:]
    picks, scatter, _ = place_rows(tensor, steps, rows, slot_ref, (meta_a, meta_b))
    half = steps * rows
    scatter_ref[...] = scatter
    picks_ref[...] = picks[:, half:]
    got_ref[...] = jnp.dot(
        picks[:, :half], xa_ref[...], preferred_element_type=jnp.float32
    ).astype(jnp.bfloat16)


def far_body(start, chunks, *refs):
    got_ref, picks_ref, scatter_ref = refs[:3]
    xb_refs = refs[3:3 + chunks]
    weight_ref = refs[3 + chunks]
    da_ref, *db_refs, _, xc_ref = refs[-3 - QUARTERS:]
    xb = jnp.concatenate([ref[...] for ref in xb_refs], axis=0)
    more = jnp.dot(picks_ref[...], xb, preferred_element_type=jnp.float32)
    xc_ref[...] = (got_ref[...].astype(jnp.float32) + more).astype(jnp.bfloat16)
    far_columns(start, xc_ref, scatter_ref, weight_ref, da_ref, db_refs)


def more_body(start, xc_ref, scatter_ref, weight_ref, *refs):
    da_ref, *db_refs, _ = refs[-2 - QUARTERS:]
    far_columns(start, xc_ref, scatter_ref, weight_ref, da_ref, db_refs)


def far_columns(start, xc_ref, scatter_ref, weight_ref, da_ref, db_refs):
    half, columns = da_ref.shape
    tile = min(512, columns)
    for at in range(0, columns, tile):
        spread = spread_products(
            xc_ref, scatter_ref, weight_ref, slice(start + at, start + at + tile)
        )
        cols = slice(at, at + tile)
        da_ref[:, cols] = spread[:half].astype(da_ref.dtype)
        put_quarters(db_refs, spread[half:], cols)


def put_quarters(refs, value, cols):
    rows = value.shape[0] // QUARTERS
    for at, ref in enumerate(refs):
        ref[:, cols] = value[at * rows:(at + 1) * rows].astype(ref.dtype)


def sums_shapes(half, columns):
    quarter = pltpu.VMEM((half // QUARTERS, columns), jnp.bfloat16)
    return [pltpu.VMEM((half, columns), jnp.bfloat16)] + [quarter] * QUARTERS


def first_delta(slots, metas, xa, xb, values, scales, base, tensor):
    steps = 2
    half, width = xa.shape
    rows = half // steps
    columns = base.shape[1]
    taken = SLOTS * 2 * steps * SEG_MOST
    outs = [*sums_shapes(half, columns), pltpu.VMEM(values.shape, jnp.bfloat16), FLAG]
    return pl.pallas_call(
        functools.partial(first_body, tensor, steps, rows),
        in_specs=[SMEM, SMEM, SMEM, HBM, VMEM, HBM, HBM, HBM],
        out_specs=[VMEM] * (len(outs) - 1) + [HBM],
        out_shape=outs,
        scratch_shapes=[
            pltpu.VMEM(xa.shape, jnp.bfloat16),
            pltpu.VMEM(scales.shape, jnp.bfloat16),
            pltpu.VMEM(base.shape, jnp.bfloat16),
            pltpu.VMEM((taken, width), jnp.bfloat16),
            pltpu.VMEM((2 * half, taken), jnp.bfloat16),
            pltpu.VMEM(xa.shape, jnp.bfloat16),
            pltpu.SemaphoreType.DMA((2 + 2 * max(1, columns // 512),)),
        ],
        cost_estimate=LIGHT,
        compiler_params=pltpu.CompilerParams(vmem_limit_bytes=22 << 20),
        name="first_delta",
    )(*in_hbm(slots), *metas, *in_hbm(xa), *in_vmem(xb), *in_hbm(values, scales, base))


def far_ready(slots, metas, xa, tensor, gates):
    steps = 2
    half, width = xa.shape
    taken = SLOTS * 2 * steps * SEG_MOST
    return pl.pallas_call(
        functools.partial(ready_body, tensor, steps, half // steps),
        in_specs=[SMEM, SMEM, SMEM, VMEM] + [HBM] * len(gates),
        out_specs=[VMEM] * 3,
        out_shape=[
            pltpu.VMEM((taken, width), jnp.bfloat16),
            pltpu.VMEM((taken, half), jnp.bfloat16),
            pltpu.VMEM((2 * half, taken), jnp.bfloat16),
        ],
        cost_estimate=LIGHT,
        compiler_params=pltpu.CompilerParams(vmem_limit_bytes=12 << 20),
        name="far_ready",
    )(*in_hbm(slots), *metas, *in_vmem(xa), *in_hbm(*gates))


def far_delta(ready, xb, weights, start, columns, gates):
    got, picks, scatter = ready
    outs = [*sums_shapes(picks.shape[1], columns), FLAG, pltpu.VMEM(got.shape, jnp.bfloat16)]
    return pl.pallas_call(
        functools.partial(far_body, start, len(xb)),
        in_specs=[VMEM] * (4 + len(xb)) + [HBM] * len(gates),
        out_specs=[VMEM] * (1 + QUARTERS) + [HBM, VMEM],
        out_shape=outs,
        cost_estimate=LIGHT,
        compiler_params=pltpu.CompilerParams(vmem_limit_bytes=12 << 20),
        name="far_delta",
    )(*in_vmem(got, picks, scatter, *xb, weights), *in_hbm(*gates))


def more_delta(gathered, scatter, weights, start, columns, gates):
    outs = [*sums_shapes(scatter.shape[0] // 2, columns), FLAG]
    return pl.pallas_call(
        functools.partial(more_body, start),
        in_specs=[VMEM] * 3 + [HBM] * len(gates),
        out_specs=[VMEM] * (1 + QUARTERS) + [HBM],
        out_shape=outs,
        cost_estimate=LIGHT,
        compiler_params=pltpu.CompilerParams(vmem_limit_bytes=8 << 20),
        name="more_delta",
    )(*in_vmem(gathered, scatter, weights), *in_hbm(*gates))


def add_quarters_body(value_ref, *refs):
    quarters, halves_out = refs[:QUARTERS], refs[QUARTERS:]
    rows = value_ref.shape[0] // QUARTERS
    for at, quarter in enumerate(quarters):
        target = halves_out[2 * at // QUARTERS]
        begin = at * rows % target.shape[0]
        target[begin:begin + rows, :] = (
            value_ref[at * rows:(at + 1) * rows, :].astype(jnp.float32)
            + quarter[...].astype(jnp.float32)
        ).astype(jnp.bfloat16)


def add_quarters(value, quarters):
    half = pltpu.VMEM((value.shape[0] // 2, value.shape[1]), jnp.bfloat16)
    return pl.pallas_call(
        add_quarters_body,
        in_specs=[VMEM] * (1 + QUARTERS),
        out_specs=[VMEM] * 2,
        out_shape=[half] * 2,
        cost_estimate=LIGHT,
        compiler_params=pltpu.CompilerParams(vmem_limit_bytes=4 << 20),
        name="add_quarters",
    )(*in_vmem(value, *quarters))


def cut_body(value_ref, *refs):
    rows = refs[0].shape[0]
    for at, ref in enumerate(refs):
        ref[...] = value_ref[at * rows:(at + 1) * rows, :]


def cut(value):
    quarter = pltpu.VMEM((value.shape[0] // QUARTERS, value.shape[1]), value.dtype)
    return pl.pallas_call(
        cut_body,
        in_specs=[VMEM],
        out_specs=[VMEM] * QUARTERS,
        out_shape=[quarter] * QUARTERS,
        cost_estimate=LIGHT,
        compiler_params=pltpu.CompilerParams(vmem_limit_bytes=4 << 20),
        name="cut",
    )(*in_vmem(value))


def cache_body(start, count, len_ref, q_ref, key_ref, val_ref, *refs):
    o_ref, lse_ref, turned_ref, _, sorted_ref = refs[-5:]
    block = o_ref.shape[0]
    cached = key_ref.shape[1]
    some = 4 * GROUP
    scale = 1.0 / math.sqrt(HD)

    @pl.when(pl.program_id(0) == 0)
    def _():
        low = start // q_ref.shape[1] * q_ref.shape[1]
        for at in range(2 * HEADS):
            pair, step, head = at // some, at // (some // 2) % 2, at % (some // 2)
            column = (pair * some // 2 + head) * HD
            value = q_ref[step, :, column:column + HD].astype(jnp.float32)
            value = value[start - low:start - low + count]
            if count > 1:
                sorted_ref[pl.ds(at, count, stride=2 * HEADS), :] = value
            else:
                sorted_ref[at:at + 1, :] = value

    position = lax.broadcasted_iota(jnp.int32, (cached, 2 * HEADS), 0)
    column = lax.broadcasted_iota(jnp.int32, (HD, 2 * HEADS), 1)
    heads = column // some * 2 + column // GROUP % 2
    first = (lax.broadcasted_iota(jnp.int32, (some, HD), 0) // GROUP) % 2 == 0
    probs = []
    for r in range(block):
        at = pl.multiple_of((pl.program_id(0) * block + r) * 2 * HEADS, 2 * HEADS)
        turned = sorted_ref[pl.ds(at, 2 * HEADS), :].astype(jnp.bfloat16).T
        turned_ref[r] = turned
        wide = jnp.concatenate(
            [jnp.where(heads == k, turned, jnp.zeros_like(turned)) for k in range(KVH)], axis=0
        )
        scores = scale * jnp.dot(key_ref[r], wide, preferred_element_type=jnp.float32)
        length = len_ref[start + pl.program_id(0) * block + r]
        scores = jnp.where(position < length, scores, NEG)
        top = jnp.max(scores, axis=0, keepdims=True)
        expo = jnp.exp(scores - top)
        total = jnp.sum(expo, axis=0, keepdims=True)
        lse_ref[r] = top + jnp.log(total)
        probs.append((expo * (1.0 / total)).astype(jnp.bfloat16).T)
    for r in range(block):
        parts = []
        for p in range(KVH // 2):
            out = jnp.dot(
                probs[r][p * some:(p + 1) * some],
                val_ref[r, :, p * 2 * HD:(p + 1) * 2 * HD],
                preferred_element_type=jnp.float32,
            )
            parts.append(jnp.where(first, out[:, :HD], out[:, HD:]))
        o_ref[r] = jnp.concatenate(parts, axis=0)


def attend_cache(lengths, queries, kv_cache, start, count, before, cost, gates):
    rows = queries.shape[1]
    cached, width = kv_cache.shape[1:]
    block = max(1, min(8, count // 2))
    skip = start // block
    together = 16 if rows % 16 == 0 else rows
    in_place = pl.BlockSpec(memory_space=pltpu.HBM)
    return pl.pallas_call(
        functools.partial(cache_body, start, count),
        grid=(count // block,),
        in_specs=[
            pl.BlockSpec(memory_space=pltpu.SMEM),
            pl.BlockSpec((2, together, queries.shape[2]), lambda i: (0, start // together, 0)),
            pl.BlockSpec((block, cached, width // 2), lambda i: (i + skip, 0, 0)),
            pl.BlockSpec((block, cached, width // 2), lambda i: (i + skip, 0, 1)),
            *[in_place for _ in (*before, *gates)],
        ],
        out_specs=(
            pl.BlockSpec((block, 2 * HEADS, HD), lambda i: (i + skip, 0, 0)),
            pl.BlockSpec((block, 1, 2 * HEADS), lambda i: (i + skip, 0, 0)),
            pl.BlockSpec((block, HD, 2 * HEADS), lambda i: (i + skip, 0, 0)),
            in_place,
        ),
        out_shape=(
            pltpu.VMEM((rows, 2 * HEADS, HD), jnp.float32),
            pltpu.VMEM((rows, 1, 2 * HEADS), jnp.float32),
            pltpu.VMEM((rows, HD, 2 * HEADS), jnp.bfloat16),
            FLAG,
        ),
        scratch_shapes=[pltpu.VMEM((count * 2 * HEADS, HD), jnp.float32)],
        input_output_aliases={4 + i: i for i in range(len(before))},
        cost_estimate=cost,
        compiler_params=pltpu.CompilerParams(vmem_limit_bytes=22 << 20),
        name="attend_cache",
    )(lengths, *in_hbm(queries, kv_cache, kv_cache), *in_vmem(*before), *in_hbm(*gates))


def weigh_body(lse_ref, turned_ref, keys_ref, o_ref, share_ref, early_ref):
    rows = lse_ref.shape[0]
    block = min(8, rows)
    shape = (2 * KVH, 2 * HEADS)
    row = lax.broadcasted_iota(jnp.int32, shape, 0)
    col = lax.broadcasted_iota(jnp.int32, shape, 1)
    head = col // (4 * GROUP) * 2 + (col // GROUP) % 2
    step = (col // (2 * GROUP)) % 2
    live = (head == row % KVH) & (row // KVH <= step)
    scale = 1.0 / math.sqrt(HD)

    def some_rows(at, carry):
        for inner in range(block):
            r = at * block + inner
            keys = jnp.concatenate([keys_ref[s, r] for s in range(2)], axis=0).astype(jnp.bfloat16)
            scores = scale * jnp.dot(keys, turned_ref[r], preferred_element_type=jnp.float32)
            scores = jnp.where(live, scores, NEG)
            lse = lse_ref[r]
            top = jnp.maximum(jnp.max(scores, axis=0, keepdims=True), lse)
            expo = jnp.exp(scores - top)
            before = jnp.exp(lse - top)
            parts = [jnp.sum(expo[s * KVH:(s + 1) * KVH], axis=0, keepdims=True) for s in range(2)]
            inverse = 1.0 / (before + parts[0] + parts[1])
            for place, part in enumerate((before, *parts)):
                share_ref[place, pl.ds(r, 1), :] = part * inverse
        return carry

    lax.fori_loop(0, rows // block, some_rows, 0)
    some = 4 * GROUP

    def one_pair(pair, carry):
        back = (2 * HEADS - some * pair) % (2 * HEADS)
        share = pltpu.roll(share_ref[0], back, 1)
        for inner in range(some):
            value = o_ref[pl.ds(pair * some + inner, rows, stride=2 * HEADS), :]
            column = pl.multiple_of((pair * (some // 2) + inner % (some // 2)) * HD, HD)
            early_ref[inner // (some // 2), :, pl.ds(column, HD)] = value * share[:, inner:inner + 1]
        return carry

    lax.fori_loop(0, KVH // 2, one_pair, 0)


def weigh_new(lse, turned, keys, o):
    rows = o.shape[0]
    return pl.pallas_call(
        weigh_body,
        in_specs=[VMEM] * 4,
        out_specs=[VMEM] * 2,
        out_shape=(
            pltpu.VMEM((3, rows, 2 * HEADS), jnp.float32),
            pltpu.VMEM((2, rows, HEADS * HD), jnp.float32),
        ),
        cost_estimate=LIGHT,
        compiler_params=pltpu.CompilerParams(vmem_limit_bytes=8 << 20),
        name="weigh_new",
    )(*in_vmem(lse, turned, keys, o.reshape(rows * 2 * HEADS, HD)))


def add_body(share_ref, early_ref, keys_ref, vals_ref, out_hbm, new_hbm, out_ref, sems):
    half = keys_ref.shape[2]
    rows = keys_ref.shape[1]
    some = 4 * GROUP
    wide = some // 2 * HD

    def piece(pair):
        cols = pl.ds(pl.multiple_of(pair * wide, wide), wide)
        return pltpu.make_async_copy(
            out_ref.at[:, :, cols], out_hbm.at[:, :, cols], sems.at[2 + pair]
        )

    first = pltpu.make_async_copy(keys_ref, new_hbm.at[:, :, :half], sems.at[0])
    second = pltpu.make_async_copy(vals_ref, new_hbm.at[:, :, half:], sems.at[1])
    first.start()
    second.start()

    def one_pair(pair, carry):
        back = (2 * HEADS - some * pair) % (2 * HEADS)
        shares = [pltpu.roll(share_ref[1 + s], back, 1) for s in range(2)]
        for head in range(2):
            at = pl.multiple_of((2 * pair + head) * HD, HD)
            vals = [vals_ref[s, :, pl.ds(at, HD)].astype(jnp.float32) for s in range(2)]
            for step in range(2):
                for member in range(GROUP):
                    inner = step * some // 2 + head * GROUP + member
                    column = pl.multiple_of(pair * wide + (head * GROUP + member) * HD, HD)
                    value = early_ref[step, :, pl.ds(column, HD)]
                    for s in range(step + 1):
                        value = value + vals[s] * shares[s][:, inner:inner + 1]
                    out_ref[step, :, pl.ds(column, HD)] = value.astype(jnp.bfloat16)
        piece(pair).start()
        return carry

    lax.fori_loop(0, KVH // 2, one_pair, 0)
    for pair in range(KVH // 2):
        piece(pair).wait()
    first.wait()
    second.wait()


def add_new(shares, early, keys, vals):
    rows = keys.shape[1]
    return pl.pallas_call(
        add_body,
        in_specs=[VMEM] * 4,
        out_specs=[HBM, HBM],
        out_shape=(
            jax.ShapeDtypeStruct((2, rows, HEADS * HD), jnp.bfloat16),
            jax.ShapeDtypeStruct((2, rows, 2 * KEYS), jnp.bfloat16),
        ),
        scratch_shapes=[
            pltpu.VMEM((2, rows, HEADS * HD), jnp.bfloat16),
            pltpu.SemaphoreType.DMA((2 + KVH // 2,)),
        ],
        cost_estimate=LIGHT,
        compiler_params=pltpu.CompilerParams(vmem_limit_bytes=12 << 20),
        name="add_new",
    )(*in_vmem(shares, early, keys, vals))


def marker_body(*refs):
    del refs


def marker(flag, cost):
    any_spec = pl.BlockSpec(memory_space=pltpu.HBM)
    return pl.pallas_call(
        marker_body,
        in_specs=[any_spec],
        out_specs=any_spec,
        out_shape=FLAG,
        cost_estimate=cost,
        compiler_params=pltpu.CompilerParams(vmem_limit_bytes=1 << 20),
        name="marker",
    )(*in_hbm(flag))


def tie(*values):
    return lax.optimization_barrier(values)


def halves(terms):
    half = terms[0].shape[0] // 2
    return [
        sum(term[begin:begin + half].astype(jnp.float32) for term in terms).astype(jnp.bfloat16)
        for begin in (0, half)
    ]


def sum_of(terms):
    return sum(term.astype(jnp.float32) for term in terms).astype(jnp.bfloat16)


def cross(value, tensor, mask):
    return lax.ppermute(value, "tensor", [(i, i ^ mask) for i in range(tensor)])


def local(
    replicas,
    tensor,
    hidden,
    base_weight,
    delta_values,
    delta_scales,
    tenant_slot,
    seg_tenant,
    seg_length,
    queries,
    kv_cache,
    cache_length,
):
    def swap(value, mask):
        return lax.ppermute(value, "replica", [(i, i ^ mask) for i in range(replicas)])

    rows = hidden.shape[1]
    columns = base_weight.shape[1]
    shard_rows = rows // tensor
    half = columns // 2
    masks = [1 << i for i in range(tensor.bit_length() - 1)]
    flat = hidden.reshape(2 * rows, hidden.shape[2])
    piece = shard_rows // 4
    masks_far = list(range(2, replicas, 2))

    far = [swap(flat, mask) for mask in masks_far]
    sibling = swap(flat, 1)
    meta = jnp.concatenate([seg_tenant, seg_length], axis=1)
    metas = [meta, *[swap(meta, mask) for mask in range(1, replicas)]]

    def cached(at, count, before, cost, flag):
        return attend_cache(
            cache_length, queries, kv_cache, at * piece, count * piece, before, cost, [flag]
        )

    own, *other, weights, flag = first_delta(
        tenant_slot, metas[:2], flat, sibling, delta_values, delta_scales, base_weight, tensor
    )
    back = [swap(part, 1) for part in other]
    flag = marker(flag, COVER)
    back, flag = tie(back, flag)
    sent, kept = add_quarters(own, back)
    sent, flag = tie(sent, flag)
    near = [kept, cross(sent, tensor, masks[0])]
    *done, flag = cached(0, 1, (), LIGHT, flag)
    far, far_metas, flag = tie(far, metas[2:], flag)
    theirs_in = [[swap(part, 1) for part in cut(rows_in)] for rows_in in far]

    flying = []
    for mask, far_rows, far_sibling in zip(masks_far, far, theirs_in):
        pair = far_metas[mask - 2:mask]
        for start in (0, half):
            if start == 0:
                ready = far_ready(tenant_slot, pair, far_rows, tensor, [flag])
                spread = ready[2]
                mine, *theirs, flag, gathered = far_delta(
                    ready, far_sibling, weights, start, half, [flag]
                )
            else:
                mine, *theirs, flag = more_delta(gathered, spread, weights, start, half, [flag])
            back = [swap(part, 1) for part in theirs]
            if not flying:
                near, flag = tie(near, flag)
                near = sum_of(near)
            flag = marker(flag, LIGHT)
            back, flag = tie(back, flag)
            sent, kept = add_quarters(mine, back)
            sent, flag = tie(sent, flag)
            flying.append([kept, cross(sent, tensor, masks[0])])
            if len(flying) > 1:
                flying[-2], flag = tie(flying[-2], flag)
                early, flag = tie(sum_of(flying[-2]), flag)
                flying[-2] = swap(early, flying_mask)
            flying_mask = mask

    *done, flag = cached(2, 2, done, LIGHT, flag)
    flying[-1], flag = tie(flying[-1], flag)
    last, flag = tie(sum_of(flying[-1]), flag)
    flying[-1] = swap(last, flying_mask)
    flying[:-1], flag = tie(flying[:-1], flag)
    values = [[near[:, start:start + half], *flying[at::2]] for at, start in enumerate((0, half))]
    sent, kept = halves(values[0])
    sent, flag = tie(sent, flag)
    values[0] = [kept, cross(sent, tensor, masks[1])]
    *done, flag = cached(1, 1, done, LIGHT, flag)
    values[1], done = tie(values[1], done)
    for mask in masks[1:]:
        sent, kept = halves(values[1])
        values[1] = [kept, cross(sent, tensor, mask)]
    values[0], sent = tie(values[0], sent)
    for mask in masks[2:]:
        sent, kept = halves(values[0])
        values[0] = [kept, cross(sent, tensor, mask)]

    def by_head(value):
        return value.astype(jnp.float32).reshape(2, shard_rows, KVH, HD)

    keys = sum_of(values[0]).reshape(2, shard_rows, half)
    o, lse, turned = done
    shares, early = weigh_new(lse, turned, by_head(keys), o)
    last, shares = tie(values[1], shares)
    vals = sum_of(last).reshape(2, shard_rows, half)
    attention, new_kv = add_new(shares, early, keys, vals)
    return (new_kv, attention)


def solution(mesh):
    placed = (
        P(None, ("groups", "replica"), "tensor"),
        P("tensor", None),
        P(("groups", "replica"), "tensor", None),
        P(("groups", "replica"), "tensor", None),
        P(),
        P(("groups", "replica"), None),
        P(("groups", "replica"), None),
        P(None, ("groups", "replica", "tensor"), None),
        P(("groups", "replica", "tensor"), None, None),
        P(("groups", "replica", "tensor")),
    )
    return jax.shard_map(
        functools.partial(local, mesh.shape["replica"], mesh.shape["tensor"]),
        mesh=mesh,
        in_specs=placed,
        out_specs=(
            P(None, ("groups", "replica", "tensor"), None),
            P(None, ("groups", "replica", "tensor"), None),
        ),
        check_vma=False,
    )
```
